128 devices in a mesh: dp: 64 (over x, y, z), mp: 2 (over core).
Axes of the slice: x: 4, y: 4, z: 4, core: 2. Of those that a mesh axis runs over, the one named last changes fastest.
Arguments:
- block_input: bfloat16 [8192, 2048], P('dp'), may hold values from -6 to 6
- cotangent: bfloat16 [8192, 2048], P('dp'), may hold values from -9 to 9
- head_count: int32 [8192], P('dp'), may hold values from 1 to 16
- width_route: int32 [8192], P('dp'), may hold values from 0 to 3
- forced_width: int32 [64], P('dp'), may hold values from 0 to 4, as said below
- slot_index: int32 [8192], P('dp'), may hold values from -1 to 63, as said below
- qkv_weight: float32 [2048, 3, 16, 128], P('dp', None, 'mp'), may hold values from -0.125 to 0.125
- out_weight: float32 [16, 128, 2048], P('mp', None, 'dp'), may hold values from -0.5 to 0.5
- up_weight: float32 [2048, 8192], P('dp', 'mp'), may hold values from -0.125 to 0.125
- down_weight: float32 [8192, 2048], P('mp', 'dp'), may hold values from -0.1875 to 0.1875
- router_weight: float32 [2048, 4], P('dp'), may hold values from -0.09375 to 0.09375
- norm_gains: float32 [2, 2048], P(None, 'dp'), may hold values from 0.38 to 2.59
- norm_biases: float32 [2, 2048], P(None, 'dp'), may hold values from -1.75 to 1.75
- qkv_first: float32 [2048, 3, 16, 128], P('dp', None, 'mp'), may hold values from -160 to 160
- qkv_second: float32 [2048, 3, 16, 128], P('dp', None, 'mp'), may hold values from 737.28 to 2949.12
- out_first: float32 [16, 128, 2048], P('mp', None, 'dp'), may hold values from -56 to 56
- out_second: float32 [16, 128, 2048], P('mp', None, 'dp'), may hold values from 81.92 to 327.68
- up_first: float32 [2048, 8192], P('dp', 'mp'), may hold values from -112 to 112
- up_second: float32 [2048, 8192], P('dp', 'mp'), may hold values from 327.68 to 1310.72
- down_first: float32 [8192, 2048], P('mp', 'dp'), may hold values from -112 to 112
- down_second: float32 [8192, 2048], P('mp', 'dp'), may hold values from 327.68 to 1310.72
- router_first: float32 [2048, 4], P('dp'), may hold values from -1536 to 1536
- router_second: float32 [2048, 4], P('dp'), may hold values from 73728 to 294912
- norm_first: float32 [4, 2048], P(None, 'dp'), may hold values from -512 to 512
- norm_second: float32 [4, 2048], P(None, 'dp'), may hold values from 8192 to 32768
Outputs:
- block_output: bfloat16 [8192, 2048], P('dp')
- input_grad: float32 [8192, 2048], P('dp')
- qkv_grad: float32 [2048, 3, 16, 128], P('dp', None, 'mp')
- out_grad: float32 [16, 128, 2048], P('mp', None, 'dp')
- up_grad: float32 [2048, 8192], P('dp', 'mp')
- down_grad: float32 [8192, 2048], P('mp', 'dp')
- router_grad: float32 [2048, 4], P('dp')
- norms_grad: float32 [4, 2048], P(None, 'dp')
- qkv_first_new: float32 [2048, 3, 16, 128], P('dp', None, 'mp')
- out_first_new: float32 [16, 128, 2048], P('mp', None, 'dp')
- up_first_new: float32 [2048, 8192], P('dp', 'mp')
- down_first_new: float32 [8192, 2048], P('mp', 'dp')
- router_first_new: float32 [2048, 4], P('dp')
- norms_first_new: float32 [4, 2048], P(None, 'dp')
- qkv_second_new: float32 [2048, 3, 16, 128], P('dp', None, 'mp')
- out_second_new: float32 [16, 128, 2048], P('mp', None, 'dp')
- up_second_new: float32 [2048, 8192], P('dp', 'mp')
- down_second_new: float32 [8192, 2048], P('mp', 'dp')
- router_second_new: float32 [2048, 4], P('dp')
- norms_second_new: float32 [4, 2048], P(None, 'dp')
- qkv_new: float32 [2048, 3, 16, 128], P('dp', None, 'mp')
- out_new: float32 [16, 128, 2048], P('mp', None, 'dp')
- up_new: float32 [2048, 8192], P('dp', 'mp')
- down_new: float32 [8192, 2048], P('mp', 'dp')
- router_new: float32 [2048, 4], P('dp')
- norms_new: float32 [4, 2048], P(None, 'dp')
- qkv_copy: bfloat16 [2048, 3, 16, 128], P('dp', None, 'mp')
- out_copy: bfloat16 [16, 128, 2048], P('mp', None, 'dp')
- up_copy: bfloat16 [2048, 8192], P('dp', 'mp')
- down_copy: bfloat16 [8192, 2048], P('mp', 'dp')
- router_copy: bfloat16 [2048, 4], P('dp')
- norms_copy: bfloat16 [4, 2048], P(None, 'dp')
- lamb_norms: float32 [5, 2], replicated
The draws below stay inside these ranges and needn't reach their ends.
Inputs may be any that keep to these rules, and one draw needn't show every extreme that they name: `forced_width`: A value of 4 leaves the sequence's tokens to width_route; a smaller value sets that bucket for all 128 tokens of the sequence. -1 marks a token that skips the feed-forward; otherwise slot_index = p * 4 + r with p < 16 and r < 4. Within one sequence, tokens with the same bucket have distinct slots, and a token skips only when more than 64 tokens of its sequence share its bucket.
All inputs are finite; a program needn't handle non-finite values.
Results may differ from the reference program's by a relative error of at most 0.02.
The reference program's roundings to bfloat16 on the way count: a program that leaves them out, or rounds other values in their place, can miss the bound.
Values may be sent and summed in bfloat16 or wider, within the bound.
A program may use at most 320 MiB of HBM per device.

```python
import math
import jax
import jax.numpy as jnp
from jax import lax

D = 2048
H = 16
HD = 128
FF = 8192
NB = 4
STEP = 5
TOK_DEV = 128
SEQS = 64
TOKENS = 8192
CAP = 4


def routing(key):
    route_key, force_key, pick_key, slot_key, bucket_key = jax.random.split(key, 5)
    levels = jax.random.randint(route_key, (TOKENS,), 0, 100)
    level = (levels >= 40).astype(jnp.int32) + (levels >= 70).astype(jnp.int32) + (levels >= 90).astype(jnp.int32)
    shuffle = jax.random.permutation(bucket_key, NB)
    route = shuffle[level].astype(jnp.int32)
    forced = jnp.minimum(jax.random.randint(force_key, (SEQS,), 0, 2 * NB), NB)
    chosen_seq = jax.random.randint(pick_key, (), 0, SEQS)
    forced = forced.at[chosen_seq].set(jax.random.randint(jax.random.fold_in(pick_key, 1), (), 0, NB))
    forced = forced.at[(chosen_seq + 1) % SEQS].set(NB).astype(jnp.int32)
    spread_forced = jnp.repeat(forced, TOK_DEV)
    chosen = jnp.where(spread_forced < NB, spread_forced, route).reshape(SEQS, TOK_DEV)
    room = SEQS // NB * CAP

    def assign(bucket_row, key_row):
        order_key, table_key = jax.random.split(key_row)
        priority = jax.random.permutation(order_key, TOK_DEV)
        order = jnp.argsort(bucket_row * TOK_DEV + priority, stable=True)
        ordered = bucket_row[order]
        starts = jnp.sum((ordered[None, :] < jnp.arange(NB)[:, None]).astype(jnp.int32), axis=1)
        position = jnp.arange(TOK_DEV) - starts[ordered]
        tables = jax.vmap(lambda table_seed: jax.random.permutation(table_seed, room))(jax.random.split(table_key, NB))
        value = jnp.where(position < room, tables[ordered, jnp.minimum(position, room - 1)], -1)
        return jnp.zeros((TOK_DEV,), jnp.int32).at[order].set(value.astype(jnp.int32))
    slots = jax.vmap(assign)(chosen, jax.random.split(slot_key, SEQS)).reshape(TOKENS)
    return (route, forced, slots)


def draw_width_route(key, part):
    return routing(key)[0]


def draw_forced_width(key, part):
    return routing(key)[1]


def draw_slot_index(key, part):
    return routing(key)[2]


def ramp_table(start, finish):
    return start + (finish - start) * jnp.arange(D, dtype=jnp.float32) / (D - 1)


def draw_norm_gains(key, part):
    key = jax.random.fold_in(key, 11)
    rising = ramp_table(0.6, 1.8)
    jitter = jax.random.uniform(key, (2, D), jnp.float32, 0.85, 1.15)
    return rising[None, :] * jitter


def draw_cotangent(key, part):
    key = jax.random.fold_in(key, 12)
    base = jnp.clip(jax.random.normal(key, (TOKENS, D), jnp.float32), -5.0, 5.0)
    rising = ramp_table(0.6, 1.8)
    return (base * rising[None, :]).astype(jnp.bfloat16)


def plant(drawn, stream_key, low, high):
    longest = drawn.shape.index(max(drawn.shape))
    spots = []
    for shift in (0, 1):
        where = [jax.random.randint(jax.random.fold_in(stream_key, axis), (), 0, length) for axis, length in enumerate(drawn.shape)]
        where[longest] = (where[longest] + shift) % drawn.shape[longest]
        spots.append(tuple(where))
    return drawn.at[spots[0]].set(low).at[spots[1]].set(high)


def block_scale(key, shape, cuts, low, top_value):
    factor_of = 1.0
    for dim, parts in cuts:
        steps = jax.random.uniform(jax.random.fold_in(jax.random.fold_in(key, 6), dim), (parts,), jnp.float32, low / len(cuts), top_value / len(cuts))
        factor_of = factor_of * jnp.repeat(jnp.exp(steps), shape[dim] // parts).reshape((-1,) + (1,) * (len(shape) - 1 - dim))
    return factor_of


def bell_draw(stream_key, extent, width, reach, shards=(), kind=jnp.bfloat16):
    values = jax.random.normal(stream_key, extent, jnp.float32) * width
    if len(shards) > 0:
        values = block_scale(stream_key, extent, shards, -0.22, 0.18) * values
    return jnp.clip(values, min=-reach, max=reach).astype(kind)


def setup_inputs(seed: int = 0) -> dict:
    streams_of = jax.random.split(jax.random.key(seed), 26)
    return {
        "block_input": bell_draw(streams_of[0], (TOKENS, D), 1.0, 6.0, ((0, 64),)),
        "cotangent": draw_cotangent(jax.random.fold_in(streams_of[25], 71), 0),
        "head_count": plant(jax.random.randint(streams_of[2], (TOKENS,), 1, H + 1), jax.random.fold_in(streams_of[2], 1), 1, H).astype(jnp.int32),
        "width_route": draw_width_route(jax.random.fold_in(streams_of[25], 71), 0),
        "forced_width": draw_forced_width(jax.random.fold_in(streams_of[25], 71), 0),
        "slot_index": draw_slot_index(jax.random.fold_in(streams_of[25], 71), 0),
        "qkv_weight": bell_draw(streams_of[6], (D, 3, H, HD), D ** -0.5, 0.125, ((0, 64), (2, 2)), jnp.float32),
        "out_weight": bell_draw(streams_of[7], (H, HD, D), (D * 8 // TOK_DEV) ** -0.5, 0.5, ((0, 2), (2, 64)), jnp.float32),
        "up_weight": bell_draw(streams_of[8], (D, FF), D ** -0.5, 0.125, ((0, 64), (1, 2)), jnp.float32),
        "down_weight": bell_draw(streams_of[9], (FF, D), (FF // 8) ** -0.5, 0.1875, ((0, 2), (1, 64)), jnp.float32),
        "router_weight": bell_draw(streams_of[10], (D, NB), (2 * D) ** -0.5, 0.09375, ((0, 64),), jnp.float32),
        "norm_gains": draw_norm_gains(jax.random.fold_in(streams_of[25], 71), 0),
        "norm_biases": bell_draw(streams_of[12], (2, D), 0.3, 1.75, ((1, 64),), jnp.float32),
        "qkv_first": bell_draw(streams_of[13], (D, 3, H, HD), (0.3 * TOKENS ** 0.5), 160.0, ((0, 64), (2, 2)), jnp.float32),
        "qkv_second": jnp.clip(jnp.exp(math.log(2949.12) - 1.3862944 * jax.random.uniform(streams_of[14], (D, 3, H, HD), jnp.float32) ** block_scale(streams_of[14], (D, 3, H, HD), ((0, 64), (2, 2)), -0.2, 0.2)), 737.28, 2949.12),
        "out_first": bell_draw(streams_of[15], (H, HD, D), (0.1 * TOKENS ** 0.5), 56.0, ((0, 2), (2, 64)), jnp.float32),
        "out_second": jnp.clip(jnp.exp(math.log(327.68) - 1.3862944 * jax.random.uniform(streams_of[16], (H, HD, D), jnp.float32) ** block_scale(streams_of[16], (H, HD, D), ((0, 2), (2, 64)), -0.2, 0.2)), 81.92, 327.68),
        "up_first": bell_draw(streams_of[17], (D, FF), (0.2 * TOKENS ** 0.5), 112.0, ((0, 64), (1, 2)), jnp.float32),
        "up_second": jnp.clip(jnp.exp(math.log(1310.72) - 1.3862944 * jax.random.uniform(streams_of[18], (D, FF), jnp.float32) ** block_scale(streams_of[18], (D, FF), ((0, 64), (1, 2)), -0.2, 0.2)), 327.68, 1310.72),
        "down_first": bell_draw(streams_of[19], (FF, D), (0.2 * TOKENS ** 0.5), 112.0, ((0, 2), (1, 64)), jnp.float32),
        "down_second": jnp.clip(jnp.exp(math.log(1310.72) - 1.3862944 * jax.random.uniform(streams_of[20], (FF, D), jnp.float32) ** block_scale(streams_of[20], (FF, D), ((0, 2), (1, 64)), -0.2, 0.2)), 327.68, 1310.72),
        "router_first": bell_draw(streams_of[21], (D, NB), (3.0 * TOKENS ** 0.5), 1536.0, ((0, 64),), jnp.float32),
        "router_second": jnp.clip(jnp.exp(math.log(294912.0) - 1.3862944 * jax.random.uniform(streams_of[22], (D, NB), jnp.float32) ** block_scale(streams_of[22], (D, NB), ((0, 64),), -0.2, 0.2)), 73728.0, 294912.0),
        "norm_first": bell_draw(streams_of[23], (4, D), (1.0 * TOKENS ** 0.5), 512.0, ((1, 64),), jnp.float32),
        "norm_second": jnp.clip(jnp.exp(math.log(32768.0) - 1.3862944 * jax.random.uniform(streams_of[24], (4, D), jnp.float32) ** block_scale(streams_of[24], (4, D), ((1, 64),), -0.2, 0.2)), 8192.0, 32768.0),
    }


HIGHEST = lax.Precision.HIGHEST
BETA_ONE = 0.5
BETA_TWO = 0.5
ADAM_EPS = 1e-06
DECAY_RATE = 0.01
LEARN_RATE = 0.5
NORM_RATE = 0.1
NORM_EPS = 1e-05
ROPE_BASE = 10000.0

@jax.custom_vjp
def low(v):
    return lax.optimization_barrier(v.astype(jnp.bfloat16)).astype(jnp.float32)

@jax.custom_vjp
def low_back(v):
    return v

def low_keep(v):
    return (low(v), None)

def low_pass(kept, grad):
    return (grad,)

def back_keep(v):
    return (v, None)

def back_low(kept, grad):
    return (low(grad),)
low.defvjp(low_keep, low_pass)
low_back.defvjp(back_keep, back_low)

def layer_norm(value, gain_row, shift_row):
    centre = value - lax.optimization_barrier(jnp.mean(value, axis=-1, keepdims=True))
    spread = lax.optimization_barrier(jnp.mean(centre * centre, axis=-1, keepdims=True))
    scaled = centre * lax.rsqrt(spread + NORM_EPS)
    return scaled * gain_row + shift_row

def rotary_tables(length, size):
    half_size = size // 2
    frequency = ROPE_BASE ** (-(jnp.arange(half_size, dtype=jnp.float32) * 2.0 / size))
    angles = jnp.arange(length, dtype=jnp.float32)[:, None] * frequency[None, :]
    cosine_table = jnp.concatenate([jnp.cos(angles), jnp.cos(angles)], axis=-1)
    sine_table = jnp.concatenate([jnp.sin(angles), jnp.sin(angles)], axis=-1)
    return (cosine_table[:, None, :], sine_table[:, None, :])

def rotate(value, cosine_table, sine_table):
    half_size = value.shape[-1] // 2
    turned = jnp.concatenate([-value[..., half_size:], value[..., :half_size]], axis=-1)
    return value * cosine_table + turned * sine_table

def soft_choice(logits):
    row_top = lax.optimization_barrier(jnp.max(logits, axis=-1, keepdims=True))
    exponent = jnp.exp(logits - row_top)
    return exponent / lax.optimization_barrier(jnp.sum(exponent, axis=-1, keepdims=True))

def sequence_attention(query_rows, key_rows, value_rows):
    scores = low_back(jnp.einsum('qhk,shk->hqs', query_rows, key_rows, precision=HIGHEST))
    length = query_rows.shape[0]
    causal = jnp.arange(length, dtype=jnp.int32)[:, None] >= jnp.arange(length, dtype=jnp.int32)[None, :]
    scores = jnp.where(causal[None, :, :], scores, -1e+30)
    attn_probs = soft_choice(scores)
    return jnp.einsum('hqs,shk->qhk', low(attn_probs), value_rows, precision=HIGHEST)

def block(params, inputs, heads, bucket, kept_float):
    qkv_full, out_full, up_full, down_full, router_full, gain_rows, shift_rows = [low(member) for member in params]
    row_count = inputs.shape[0]
    sequences = row_count // TOK_DEV
    a_one = low(layer_norm(inputs, gain_rows[0], shift_rows[0]))
    qkv = low_back(jnp.einsum('td,dchk->tchk', a_one, qkv_full, precision=HIGHEST))
    qkv = qkv.reshape(sequences, TOK_DEV, 3, H, HD)
    cosine_table, sine_table = rotary_tables(TOK_DEV, HD)
    query_rows = low(rotate(qkv[:, :, 0], cosine_table, sine_table) * HD ** (-0.5))
    key_rows = low(rotate(qkv[:, :, 1], cosine_table, sine_table))
    value_rows = low(qkv[:, :, 2])
    attended = jax.vmap(sequence_attention)(query_rows, key_rows, value_rows).reshape(row_count, H, HD)
    head_used = (jnp.arange(H, dtype=jnp.int32)[None, :] < heads[:, None]).astype(jnp.float32)
    mixed_heads = low_back(low(attended * head_used[:, :, None]))
    hidden = inputs + low_back(jnp.einsum('thk,hkd->td', mixed_heads, out_full, precision=HIGHEST))
    a_two = low(layer_norm(hidden, gain_rows[1], shift_rows[1]))
    router = soft_choice(jnp.dot(a_two, router_full, precision=HIGHEST))
    bucket_onehot = (bucket[:, None] == jnp.arange(NB, dtype=jnp.int32)[None, :]).astype(jnp.float32)
    gate_value = lax.optimization_barrier(jnp.sum(router * bucket_onehot, axis=-1))
    sent_rows = low_back(a_two)
    up_value = low_back(jnp.dot(sent_rows, up_full, precision=HIGHEST))
    width_limit = (bucket + 1) * (FF // NB)
    active = (jnp.arange(FF, dtype=jnp.int32)[None, :] < width_limit[:, None]).astype(jnp.float32)
    activation = low(jnp.square(jax.nn.relu(up_value)) * active)
    branch = low_back(low(jnp.dot(activation, down_full, precision=HIGHEST))) * kept_float[:, None]
    return hidden + gate_value[:, None] * branch

def moment_step(weight, gradient, first_moment, second_moment, decay_rate):
    first_moment = BETA_ONE * first_moment + (1.0 - BETA_ONE) * gradient
    second_moment = BETA_TWO * second_moment + (1.0 - BETA_TWO) * gradient * gradient
    update = first_moment / (1.0 - BETA_ONE ** STEP) / (jnp.sqrt(second_moment / (1.0 - BETA_TWO ** STEP)) + ADAM_EPS) + decay_rate * weight
    return (first_moment, second_moment, update)

def reference(block_input, cotangent, head_count, width_route, forced_width, slot_index, qkv_weight, out_weight, up_weight, down_weight, router_weight, norm_gains, norm_biases, qkv_first, qkv_second, out_first, out_second, up_first, up_second, down_first, down_second, router_first, router_second, norm_first, norm_second):
    seq_forced = jnp.repeat(forced_width, TOK_DEV)
    bucket = jnp.where(seq_forced < NB, seq_forced, width_route).astype(jnp.int32)
    kept_float = (slot_index >= 0).astype(jnp.float32)
    params = (qkv_weight, out_weight, up_weight, down_weight, router_weight, norm_gains, norm_biases)
    group_size = max(1, min(SEQS, 4096 // TOK_DEV))
    rounds = SEQS // group_size
    row_count = group_size * TOK_DEV

    def to_rounds(array):
        return array.reshape((rounds, row_count) + array.shape[1:])
    sliced = (to_rounds(block_input.astype(jnp.float32)), to_rounds(cotangent.astype(jnp.float32)), to_rounds(head_count), to_rounds(bucket), to_rounds(kept_float))

    def scan_step(running, member):
        inputs, upstream, heads, buckets, kept_rows = member
        produced, pullback = jax.vjp(lambda weights_in, rows_in: block(weights_in, rows_in, heads, buckets, kept_rows), params, inputs)
        weight_grads, row_grads = pullback(upstream)
        running = jax.tree.map(jnp.add, running, weight_grads)
        return (running, (produced, row_grads))
    zero_grads = jax.tree.map(jnp.zeros_like, params)
    grads, (produced, row_grads) = lax.scan(scan_step, zero_grads, sliced)
    block_output = produced.reshape(TOKENS, D).astype(jnp.bfloat16)
    input_grad = row_grads.reshape(TOKENS, D)
    masters = (qkv_weight, out_weight, up_weight, down_weight, router_weight)
    firsts = (qkv_first, out_first, up_first, down_first, router_first)
    seconds = (qkv_second, out_second, up_second, down_second, router_second)
    first_new = []
    second_new = []
    weight_new = []
    norm_rows = []
    for index in range(5):
        first_moment, second_moment, update = moment_step(masters[index], grads[index], firsts[index], seconds[index], DECAY_RATE)
        weight_norm = jnp.sqrt(jnp.sum(masters[index] * masters[index]))
        update_norm = jnp.sqrt(jnp.sum(update * update))
        first_new.append(first_moment)
        second_new.append(second_moment)
        weight_new.append(masters[index] - LEARN_RATE * (weight_norm / update_norm) * update)
        norm_rows.append(jnp.stack([weight_norm, update_norm]))
    norms_grad = jnp.concatenate([grads[5], grads[6]], axis=0)
    norm_master = jnp.concatenate([norm_gains, norm_biases], axis=0)
    norm_moment, norm_square, norm_update = moment_step(norm_master, norms_grad, norm_first, norm_second, 0.0)
    norms_new = norm_master - NORM_RATE * norm_update
    lamb_norms = jnp.stack(norm_rows, axis=0)
    return (block_output, input_grad, grads[0], grads[1], grads[2], grads[3], grads[4], norms_grad, first_new[0], first_new[1], first_new[2], first_new[3], first_new[4], norm_moment, second_new[0], second_new[1], second_new[2], second_new[3], second_new[4], norm_square, weight_new[0], weight_new[1], weight_new[2], weight_new[3], weight_new[4], norms_new, weight_new[0].astype(jnp.bfloat16), weight_new[1].astype(jnp.bfloat16), weight_new[2].astype(jnp.bfloat16), weight_new[3].astype(jnp.bfloat16), weight_new[4].astype(jnp.bfloat16), norms_new.astype(jnp.bfloat16), lamb_norms)
```

```python
from functools import partial

import jax
import jax.numpy as jnp
from jax import lax
from jax.experimental import pallas as pl
from jax.experimental.pallas import tpu as pltpu
from jax.sharding import PartitionSpec as P

STEP = 5

HIGHEST = lax.Precision.HIGHEST
BETA_ONE = 0.5
BETA_TWO = 0.5
ADAM_EPS = 1e-06
DECAY_RATE = 0.01
LEARN_RATE = 0.5
NORM_RATE = 0.1
NORM_EPS = 1e-05
ROPE_BASE = 10000.0

MESH = pl.DeviceIdType.MESH
BF16 = jnp.bfloat16
F32 = jnp.float32
VMEM = pl.BlockSpec(memory_space=pltpu.VMEM)
ANY = pl.BlockSpec(memory_space=pl.ANY)
DMA = pltpu.SemaphoreType.DMA

EXTRA, QKV, OUT, UP, DOWN = (0, 128), (128, 896), (896, 1152), (1152, 2176), (2176, 3200)
WIDE = 3200
SPLIT = 1536


def place():
    index = lax.axis_index("dp")
    return lax.div(index, 16), lax.rem(lax.div(index, 4), 4), lax.rem(index, 4), lax.axis_index("mp")


def ring(value, step):
    return lax.rem(value + (step + 4), 4)


def device(x, y, z, core):
    return (x * 16 + y * 4 + z, core)


def greet(peers):
    barrier = pltpu.get_barrier_semaphore()
    for peer in peers:
        pl.semaphore_signal(barrier, inc=1, device_id=peer, device_id_type=MESH)
    pl.semaphore_wait(barrier, len(peers))


def send(src, dst, send_sem, recv_sem, peer):
    copy = pltpu.make_async_remote_copy(
        src_ref=src, dst_ref=dst, send_sem=send_sem, recv_sem=recv_sem, device_id=peer, device_id_type=MESH
    )
    copy.start()
    return copy


def gather_kernel(packed, meta, full, metas, z_send, z_recv, m_send, m_recv, own_sem, p_send, p_recv):
    x, y, z, core = place()
    z_peers = [device(x, y, ring(z, k), core) for k in (1, 2, 3)]
    xp, xm = device(ring(x, 1), y, z, core), device(ring(x, -1), y, z, core)
    yp, ym = device(x, ring(y, 1), z, core), device(x, ring(y, -1), z, core)
    greet(z_peers + [xp, xm, yp, ym])
    rows = pl.ds(pl.multiple_of(z * 32, 32), 32)
    flying = []
    for k in (2, 1, 3):
        flying.append(
            send(packed.at[ring(z, k)], full.at[x, y, rows, :], z_send.at[k - 1], z_recv.at[k - 1], z_peers[k - 1])
        )
        flying.append(send(meta, metas.at[z], m_send.at[k - 1], m_recv.at[k - 1], z_peers[k - 1]))
    own = pltpu.make_async_copy(packed.at[z], full.at[x, y, rows, :], own_sem.at[0])
    own.start()
    own_meta = pltpu.make_async_copy(meta, metas.at[z], own_sem.at[1])
    own_meta.start()
    for copy in flying:
        copy.wait()
    own.wait()
    own_meta.wait()
    low, high = pl.ds(0, 64), pl.ds(64, 64)
    every = slice(None)
    first, second = pl.ds(0, SPLIT), pl.ds(SPLIT, WIDE - SPLIT)

    def step(number, moves):
        copies = []
        for index, (where, peer) in enumerate(moves):
            part = full.at[where]
            copies.append(send(part, part, p_send.at[number, index], p_recv.at[number, index], peer))
        for copy in copies:
            copy.wait()

    x_before, x_after, y_before, y_after = ring(x, -1), ring(x, 1), ring(y, -1), ring(y, 1)
    step(0, [
        ((x, y, every, first), xp), ((x, y, every, first), xm),
        ((x, y, every, second), yp), ((x, y, every, second), ym),
    ])
    step(1, [
        ((x_before, y, low, first), xp), ((x_after, y, high, first), xm),
        ((x, y_before, low, second), yp), ((x, y_after, high, second), ym),
    ])
    step(2, [
        ((every, y, every, first), yp), ((every, y, every, first), ym),
        ((x, every, every, second), xp), ((x, every, every, second), xm),
    ])
    step(3, [
        ((every, y_before, low, first), yp), ((every, y_after, high, first), ym),
        ((x_before, every, low, second), xp), ((x_after, every, high, second), xm),
    ])


def gather_weights(packed, meta):
    return pl.pallas_call(
        gather_kernel,
        out_shape=(
            jax.ShapeDtypeStruct((4, 4, 128, WIDE), BF16),
            jax.ShapeDtypeStruct((4, 8, 128), F32),
        ),
        in_specs=[ANY, ANY],
        out_specs=(ANY, ANY),
        scratch_shapes=[DMA((3,)), DMA((3,)), DMA((3,)), DMA((3,)), DMA((2,)), DMA((4, 4)), DMA((4, 4))],
        compiler_params=pltpu.CompilerParams(collective_id=0, has_side_effects=True),
        name="gather_weights",
    )(packed, meta)


def add_into(target, target_at, source, source_at, blocks, row, count, columns, width):
    def one(index, carry):
        xi = index // (count // 16)
        step = pl.multiple_of(lax.rem(index, count // 16) * 16, 16)
        to = target_at(xi) + (pl.ds(row + step, 16), columns)
        here = target[to].astype(F32)
        for ref, first_row in source:
            here = here + ref[source_at(xi) + (pl.ds(first_row + step, 16), pl.ds(0, width))].astype(F32)
        target[to] = here.astype(BF16)
        return carry

    lax.fori_loop(0, blocks * (count // 16), one, 0)


def scatter_kernel(
    grads_in, out, grads, one_a, one_b, two_a, two_b, one_c, one_d, two_c, two_d, load_sem, s_send, s_recv, z_send, z_recv, own_sem
):
    x, y, z, core = place()
    z_peers = [device(x, y, ring(z, k), core) for k in (1, 2, 3)]
    xp, xm = device(ring(x, 1), y, z, core), device(ring(x, -1), y, z, core)
    yp, ym = device(x, ring(y, 1), z, core), device(x, ring(y, -1), z, core)
    load = pltpu.make_async_copy(grads_in, grads, load_sem)
    load.start()
    greet(z_peers + [xp, xm, yp, ym])
    load.wait()
    low, high = pl.ds(0, 64), pl.ds(64, 64)
    every = slice(None)
    first, second = pl.ds(0, SPLIT), pl.ds(SPLIT, WIDE - SPLIT)
    wa, wb = SPLIT, WIDE - SPLIT
    x_before, x_after, y_before, y_after = ring(x, -1), ring(x, 1), ring(y, -1), ring(y, 1)
    x_far, y_far = ring(x, 2), ring(y, 2)

    def go(number, index, where, dst, peer):
        return send(grads.at[where], dst, s_send.at[number, index], s_recv.at[number, index], peer)

    halves = [
        go(0, 0, (every, y_far, low, first), one_a.at[0], yp),
        go(0, 1, (every, y_far, high, first), one_a.at[1], ym),
        go(0, 2, (x_far, every, low, second), one_b.at[0], xp),
        go(0, 3, (x_far, every, high, second), one_b.at[1], xm),
    ]
    rest = [
        go(0, 4, (every, y_after, high, first), two_a.at[0, :, high, :], yp),
        go(0, 5, (every, y_before, low, first), two_a.at[1, :, low, :], ym),
        go(0, 6, (x_after, every, high, second), two_b.at[0, :, high, :], xp),
        go(0, 7, (x_before, every, low, second), two_b.at[1, :, low, :], xm),
    ]
    halves[0].wait()
    add_into(grads, lambda i: (i, y_after), [(one_a.at[0], 0)], lambda i: (i,), 4, 0, 64, first, wa)
    last = [go(0, 8, (every, y_after, low, first), two_a.at[0, :, low, :], yp)]
    halves[2].wait()
    add_into(grads, lambda i: (x_after, i), [(one_b.at[0], 0)], lambda i: (i,), 4, 0, 64, second, wb)
    last.append(go(0, 9, (x_after, every, low, second), two_b.at[0, :, low, :], xp))
    halves[1].wait()
    add_into(grads, lambda i: (i, y_before), [(one_a.at[1], 0)], lambda i: (i,), 4, 64, 64, first, wa)
    last.append(go(0, 10, (every, y_before, high, first), two_a.at[1, :, high, :], ym))
    halves[3].wait()
    add_into(grads, lambda i: (x_before, i), [(one_b.at[1], 0)], lambda i: (i,), 4, 64, 64, second, wb)
    last.append(go(0, 11, (x_before, every, high, second), two_b.at[1, :, high, :], xm))
    for copy in rest + last:
        copy.wait()
    add_into(grads, lambda i: (i, y), [(two_a.at[0], 0), (two_a.at[1], 0)], lambda i: (i,), 4, 0, 128, first, wa)
    add_into(grads, lambda i: (x, i), [(two_b.at[0], 0), (two_b.at[1], 0)], lambda i: (i,), 4, 0, 128, second, wb)

    halves = [
        go(1, 0, (x_far, y, low, first), one_c.at[0], xp),
        go(1, 1, (x_far, y, high, first), one_c.at[1], xm),
        go(1, 2, (x, y_far, low, second), one_d.at[0], yp),
        go(1, 3, (x, y_far, high, second), one_d.at[1], ym),
    ]
    rest = [
        go(1, 4, (x_after, y, high, first), two_c.at[0, high, :], xp),
        go(1, 5, (x_before, y, low, first), two_c.at[1, low, :], xm),
        go(1, 6, (x, y_after, high, second), two_d.at[0, high, :], yp),
        go(1, 7, (x, y_before, low, second), two_d.at[1, low, :], ym),
    ]
    halves[0].wait()
    add_into(grads, lambda i: (x_after, y), [(one_c.at[0], 0)], lambda i: (), 1, 0, 64, first, wa)
    last = [go(1, 8, (x_after, y, low, first), two_c.at[0, low, :], xp)]
    halves[2].wait()
    add_into(grads, lambda i: (x, y_after), [(one_d.at[0], 0)], lambda i: (), 1, 0, 64, second, wb)
    last.append(go(1, 9, (x, y_after, low, second), two_d.at[0, low, :], yp))
    halves[1].wait()
    add_into(grads, lambda i: (x_before, y), [(one_c.at[1], 0)], lambda i: (), 1, 64, 64, first, wa)
    last.append(go(1, 10, (x_before, y, high, first), two_c.at[1, high, :], xm))
    halves[3].wait()
    add_into(grads, lambda i: (x, y_before), [(one_d.at[1], 0)], lambda i: (), 1, 64, 64, second, wb)
    last.append(go(1, 11, (x, y_before, high, second), two_d.at[1, high, :], ym))
    for copy in rest + last:
        copy.wait()
    add_into(grads, lambda i: (x, y), [(two_c.at[0], 0), (two_c.at[1], 0)], lambda i: (), 1, 0, 128, first, wa)
    add_into(grads, lambda i: (x, y), [(two_d.at[0], 0), (two_d.at[1], 0)], lambda i: (), 1, 0, 128, second, wb)

    copies = []
    for k in (2, 1, 3):
        rows = pl.ds(pl.multiple_of(ring(z, k) * 32, 32), 32)
        copies.append(send(grads.at[x, y, rows, :], out.at[z], z_send.at[k - 1], z_recv.at[k - 1], z_peers[k - 1]))
    rows = pl.ds(pl.multiple_of(z * 32, 32), 32)
    own = pltpu.make_async_copy(grads.at[x, y, rows, :], out.at[z], own_sem)
    own.start()
    for copy in copies:
        copy.wait()
    own.wait()


def scatter_gradients(grads):
    wa, wb = SPLIT, WIDE - SPLIT
    return pl.pallas_call(
        scatter_kernel,
        out_shape=jax.ShapeDtypeStruct((4, 32, WIDE), BF16),
        in_specs=[ANY],
        out_specs=VMEM,
        scratch_shapes=[
            pltpu.VMEM((4, 4, 128, WIDE), BF16),
            pltpu.VMEM((2, 4, 64, wa), BF16),
            pltpu.VMEM((2, 4, 64, wb), BF16),
            pltpu.VMEM((2, 4, 128, wa), BF16),
            pltpu.VMEM((2, 4, 128, wb), BF16),
            pltpu.VMEM((2, 64, wa), BF16),
            pltpu.VMEM((2, 64, wb), BF16),
            pltpu.VMEM((2, 128, wa), BF16),
            pltpu.VMEM((2, 128, wb), BF16),
            DMA, DMA((2, 12)), DMA((2, 12)), DMA((3,)), DMA((3,)), DMA,
        ],
        compiler_params=pltpu.CompilerParams(collective_id=1, has_side_effects=True, vmem_limit_bytes=56 * 2**20),
        name="scatter_gradients",
    )(grads)


def spread_kernel(count, *refs):
    ins, outs = refs[:count], refs[count : 2 * count]
    own_sem, z_send, z_recv, c_send, c_recv = refs[2 * count :]
    x, y, z, core = place()
    z_peers = [device(x, y, ring(z, k), core) for k in (1, 2, 3)]
    partner = device(x, y, z, 1 - core)
    greet(z_peers + [partner])
    half = pl.ds(pl.multiple_of(core * 1024, 1024), 1024)
    flying, own = [], []
    for a in range(count):
        for k in (2, 1, 3):
            flying.append(
                (a, k, send(ins[a].at[:, half], outs[a].at[z, :, half], z_send.at[a, k - 1], z_recv.at[a, k - 1],
                            z_peers[k - 1]))
            )
    for a in range(count):
        own.append(pltpu.make_async_copy(ins[a], outs[a].at[z], own_sem.at[a]))
        own[-1].start()
    passed = []
    for a, k, copy in flying:
        copy.wait_recv()
        part = outs[a].at[ring(z, -k), :, half]
        passed.append(send(part, part, c_send.at[a, k - 1], c_recv.at[a, k - 1], partner))
    for copy in own:
        copy.wait()
    for _, _, copy in flying:
        copy.wait_send()
    for copy in passed:
        copy.wait()


def spread_rows(number, *arrays):
    count = len(arrays)
    return pl.pallas_call(
        partial(spread_kernel, count),
        out_shape=(jax.ShapeDtypeStruct((4, 128, 2048), BF16),) * count,
        in_specs=[VMEM] * count,
        out_specs=(VMEM,) * count,
        scratch_shapes=[DMA((count,)), DMA((count, 3)), DMA((count, 3)), DMA((count, 3)), DMA((count, 3))],
        compiler_params=pltpu.CompilerParams(
            collective_id=number, has_side_effects=True, vmem_limit_bytes=40 * 2**20
        ),
        name=f"spread_rows_{number}",
    )(*arrays)


def merge_kernel(count, *refs):
    parts, outs = refs[:count], refs[count : 2 * count]
    c_out, c_in, z_out, z_in, kept, c_send, c_recv, z_send, z_recv, e_send, e_recv = refs[2 * count :]
    x, y, z, core = place()
    z_peers = [device(x, y, ring(z, k), core) for k in (1, 2, 3)]
    partner = device(x, y, z, 1 - core)
    mine = pl.ds(pl.multiple_of(core * 1024, 1024), 1024)
    other = pl.ds(pl.multiple_of((1 - core) * 1024, 1024), 1024)
    order = (2, 1, 3, 0)
    for a in range(count):
        for j, k in enumerate(order):
            c_out[a, j] = parts[a][ring(z, k), :, other].astype(BF16)
    greet(z_peers + [partner])
    crossing = [
        [send(c_out.at[a, j], c_in.at[a, j], c_send.at[a, j], c_recv.at[a, j], partner) for j in range(4)]
        for a in range(count)
    ]
    flying = []
    for a in range(count):
        for j, k in enumerate(order):
            crossing[a][j].wait()
            joined = parts[a][ring(z, k), :, mine] + c_in[a, j].astype(F32)
            if k:
                z_out[a, j] = joined.astype(BF16)
                flying.append(
                    (a, j, send(z_out.at[a, j], z_in.at[a, j], z_send.at[a, j], z_recv.at[a, j], z_peers[k - 1]))
                )
            else:
                kept[a] = joined
    ends = []
    for a in range(count):
        for b, j, copy in flying:
            if b == a:
                copy.wait()
        outs[a][:, mine] = kept[a] + z_in[a, 0].astype(F32) + z_in[a, 1].astype(F32) + z_in[a, 2].astype(F32)
        part = outs[a].at[:, mine]
        ends.append(send(part, part, e_send.at[a], e_recv.at[a], partner))
    for copy in ends:
        copy.wait()


def merge_rows(number, *arrays):
    count = len(arrays)
    return pl.pallas_call(
        partial(merge_kernel, count),
        out_shape=(jax.ShapeDtypeStruct((128, 2048), F32),) * count,
        in_specs=[VMEM] * count,
        out_specs=(VMEM,) * count,
        scratch_shapes=[
            pltpu.VMEM((count, 4, 128, 1024), BF16),
            pltpu.VMEM((count, 4, 128, 1024), BF16),
            pltpu.VMEM((count, 3, 128, 1024), BF16),
            pltpu.VMEM((count, 3, 128, 1024), BF16),
            pltpu.VMEM((count, 128, 1024), F32),
            DMA((count, 4)), DMA((count, 4)), DMA((count, 3)), DMA((count, 3)), DMA((count,)), DMA((count,)),
        ],
        compiler_params=pltpu.CompilerParams(
            collective_id=number, has_side_effects=True, vmem_limit_bytes=48 * 2**20
        ),
        name=f"merge_rows_{number}",
    )(*arrays)


def total_kernel(value, out, slots, t_send, t_recv):
    x, y, z, core = place()
    along = (
        [device(x, y, z, 1 - core)],
        [device(x, y, ring(z, k), core) for k in (1, 2, 3)],
        [device(x, ring(y, k), z, core) for k in (1, 2, 3)],
        [device(ring(x, k), y, z, core) for k in (1, 2, 3)],
    )
    greet([peer for peers in along for peer in peers])
    out[...] = value[...]
    for axis, (me, peers) in enumerate(zip((core, z, y, x), along)):
        slots[axis, me] = out[...]
        here = slots.at[axis, me]
        copies = [
            send(here, here, t_send.at[axis, k], t_recv.at[axis, k], peer) for k, peer in enumerate(peers)
        ]
        for copy in copies:
            copy.wait()
        result = slots[axis, 0]
        for k in range(1, len(peers) + 1):
            result = result + slots[axis, k]
        out[...] = result


def total(value):
    return pl.pallas_call(
        total_kernel,
        out_shape=jax.ShapeDtypeStruct((8, 128), F32),
        in_specs=[VMEM],
        out_specs=VMEM,
        scratch_shapes=[pltpu.VMEM((4, 4, 8, 128), F32), DMA((4, 3)), DMA((4, 3))],
        compiler_params=pltpu.CompilerParams(collective_id=2, has_side_effects=True),
        name="total",
    )(value)


def layer_norm(value, gain_row, shift_row):
    centre = value - jnp.mean(value, axis=-1, keepdims=True)
    spread = jnp.mean(centre * centre, axis=-1, keepdims=True)
    inverse = lax.rsqrt(spread + NORM_EPS)
    scaled = centre * inverse
    return (scaled * gain_row + shift_row, scaled, inverse)


def norm_back(scaled, inverse, gain_row, upstream):
    dscaled = upstream * gain_row
    inner = (
        dscaled
        - jnp.mean(dscaled, axis=-1, keepdims=True)
        - scaled * jnp.mean(dscaled * scaled, axis=-1, keepdims=True)
    )
    return (inner * inverse, jnp.sum(upstream * scaled, axis=0), jnp.sum(upstream, axis=0))


def rotary_tables(length, size):
    half_size = size // 2
    frequency = ROPE_BASE ** (-(jnp.arange(half_size, dtype=F32) * 2.0 / size))
    angles = jnp.arange(length, dtype=F32)[:, None] * frequency[None, :]
    cosine_table = jnp.concatenate([jnp.cos(angles), jnp.cos(angles)], axis=-1)
    sine_table = jnp.concatenate([jnp.sin(angles), jnp.sin(angles)], axis=-1)
    return (cosine_table[:, None, :], sine_table[:, None, :])


def rotate(value, cosine_table, sine_table):
    half_size = value.shape[-1] // 2
    turned = jnp.concatenate([-value[..., half_size:], value[..., :half_size]], axis=-1)
    return value * cosine_table + turned * sine_table


def rotate_back(gradient, cosine_table, sine_table):
    half_size = gradient.shape[-1] // 2
    moved = gradient * sine_table
    turned = jnp.concatenate([moved[..., half_size:], -moved[..., :half_size]], axis=-1)
    return gradient * cosine_table + turned


def soft_choice(logits):
    row_top = jnp.max(logits, axis=-1, keepdims=True)
    exponent = jnp.exp(logits - row_top)
    return exponent / jnp.sum(exponent, axis=-1, keepdims=True)


def moment_step(weight, gradient, first_moment, second_moment, decay_rate):
    first_moment = BETA_ONE * first_moment + (1.0 - BETA_ONE) * gradient
    second_moment = BETA_TWO * second_moment + (1.0 - BETA_TWO) * gradient * gradient
    update = (
        first_moment
        / (1.0 - BETA_ONE**STEP)
        / (jnp.sqrt(second_moment / (1.0 - BETA_TWO**STEP)) + ADAM_EPS)
        + decay_rate * weight
    )
    return (first_moment, second_moment, update)


def dot(left, right, dims):
    return lax.dot_general(left, right, ((dims[:1], dims[1:]), ((), ())), preferred_element_type=F32)


def local(
    block_input,
    cotangent,
    head_count,
    width_route,
    forced_width,
    slot_index,
    qkv_weight,
    out_weight,
    up_weight,
    down_weight,
    router_weight,
    norm_gains,
    norm_biases,
    qkv_first,
    qkv_second,
    out_first,
    out_second,
    up_first,
    up_second,
    down_first,
    down_second,
    router_first,
    router_second,
    norm_first,
    norm_second,
):
    core = lax.axis_index("mp")
    z = lax.rem(lax.axis_index("dp"), 4)
    norm_master = jnp.concatenate([norm_gains, norm_biases], axis=0)
    bucket = jnp.where(forced_width[0] < 4, forced_width[0], width_route)
    kept_float = (slot_index >= 0).astype(F32)

    extra = jnp.concatenate([router_weight, norm_master.T, jnp.zeros((32, 120), F32)], axis=1).astype(BF16)
    packed = jnp.concatenate(
        [
            jnp.broadcast_to(extra[None], (4, 32, 128)),
            qkv_weight.astype(BF16).reshape(32, 3, 4, 2, 128).transpose(2, 0, 1, 3, 4).reshape(4, 32, 768),
            out_weight.astype(BF16).transpose(2, 0, 1).reshape(32, 4, 256).transpose(1, 0, 2),
            up_weight.astype(BF16).reshape(32, 4, 1024).transpose(1, 0, 2),
            down_weight.T.astype(BF16).reshape(32, 4, 1024).transpose(1, 0, 2),
        ],
        axis=2,
    )
    meta = jnp.concatenate(
        [head_count.astype(F32)[None], bucket.astype(F32)[None], jnp.zeros((6, 128), F32)], axis=0
    )
    full, metas = gather_weights(packed, meta)
    full = full.reshape(2048, WIDE)
    qkv_full, out_full, up_full, down_full = (full[:, a:b] for a, b in (QKV, OUT, UP, DOWN))
    small = full[:, :8].astype(F32).T
    router_rows, norm_rows = small[:4].astype(BF16), small[4:]
    head_all = metas[:, 0, :].reshape(512)
    bucket_all = metas[:, 1, :].reshape(512)

    inputs = block_input.astype(F32)
    ln_one, scaled_one, inverse_one = layer_norm(inputs, norm_rows[0], norm_rows[2])
    (a_one,) = spread_rows(3, ln_one.astype(BF16))
    a_one = a_one.reshape(512, 2048)
    qkv = dot(a_one, qkv_full, (1, 0)).reshape(4, 128, 3, 2, 128)
    cosine_table, sine_table = rotary_tables(128, 128)
    score_scale = 128 ** (-0.5)
    query_rows = (rotate(qkv[:, :, 0], cosine_table, sine_table) * score_scale).astype(BF16)
    key_rows = rotate(qkv[:, :, 1], cosine_table, sine_table).astype(BF16)
    value_rows = qkv[:, :, 2].astype(BF16)
    positions = jnp.arange(128, dtype=jnp.int32)
    causal = positions[:, None] >= positions[None, :]
    scores = jnp.einsum("nqhk,nshk->nhqs", query_rows, key_rows, preferred_element_type=F32)
    attn_probs = soft_choice(jnp.where(causal, scores, -1e30))
    probs_low = attn_probs.astype(BF16)
    heads_out = jnp.einsum("nhqs,nshk->nqhk", probs_low, value_rows, preferred_element_type=F32)
    head_ids = (core * 8 + z * 2 + jnp.arange(2, dtype=jnp.int32)).astype(F32)
    head_used = (head_ids[None, :] < head_all[:, None]).astype(F32)
    mixed = (heads_out.reshape(512, 2, 128) * head_used[:, :, None]).astype(BF16).reshape(512, 256)
    (attention,) = merge_rows(4, dot(mixed, out_full, (1, 1)).reshape(4, 128, 2048))
    hidden = inputs + attention

    ln_two, scaled_two, inverse_two = layer_norm(hidden, norm_rows[1], norm_rows[3])
    a_two_own = ln_two.astype(BF16)
    router = soft_choice(dot(a_two_own, router_rows, (1, 1)))
    bucket_onehot = (bucket[:, None] == jnp.arange(4, dtype=jnp.int32)[None, :]).astype(F32)
    gate_value = jnp.sum(router * bucket_onehot, axis=-1)
    upstream = cotangent.astype(F32)
    branch_grad = (upstream * gate_value[:, None] * kept_float[:, None]).astype(BF16)
    a_two, branch_rows = spread_rows(5, a_two_own, branch_grad)
    a_two, branch_rows = a_two.reshape(512, 2048), branch_rows.reshape(512, 2048)

    unit_ids = core * 4096 + z * 1024 + jnp.arange(1024, dtype=jnp.int32)
    used = (unit_ids.astype(F32)[None, :] < (bucket_all[:, None] + 1.0) * 2048.0).astype(F32)
    up_value = jax.nn.relu(dot(a_two, up_full, (1, 0))) * used
    activation = jnp.square(up_value).astype(BF16)
    up_low = (dot(branch_rows, down_full, (1, 0)) * 2.0 * up_value).astype(BF16)
    produced = dot(activation, down_full, (1, 1)).reshape(4, 128, 2048)
    row_part = dot(up_low, up_full, (1, 1)).reshape(4, 128, 2048)
    produced, row_sum = merge_rows(6, produced, row_part)
    branch_out = produced.astype(BF16).astype(F32) * kept_float[:, None]
    block_output = (hidden + gate_value[:, None] * branch_out).astype(BF16)
    gate_grad = jnp.sum(upstream * branch_out, axis=-1)
    logit_grad = router * (bucket_onehot - gate_value[:, None]) * gate_grad[:, None]
    ln_two_grad = row_sum.astype(BF16).astype(F32) + jnp.dot(
        logit_grad, router_rows.astype(F32), precision=HIGHEST
    )
    router_grad_w = lax.dot_general(
        logit_grad, a_two_own.astype(F32), (((0,), (0,)), ((), ())), precision=HIGHEST
    )
    norm_in_two, gain_two_grad, bias_two_grad = norm_back(scaled_two, inverse_two, norm_rows[1], ln_two_grad)
    hidden_grad = upstream + norm_in_two
    (hidden_low,) = spread_rows(7, hidden_grad.astype(BF16))
    hidden_low = hidden_low.reshape(512, 2048)

    used_low = head_used.astype(BF16)[:, :, None]
    mixed_grad = (dot(hidden_low, out_full, (1, 0)).astype(BF16).reshape(512, 2, 128) * used_low).reshape(
        4, 128, 2, 128
    )
    value_grad = jnp.einsum("nhqs,nqhk->nshk", probs_low, mixed_grad, preferred_element_type=F32)
    prob_grad = jnp.einsum("nqhk,nshk->nhqs", mixed_grad, value_rows, preferred_element_type=F32)
    inner = jnp.sum(attn_probs * prob_grad, axis=-1, keepdims=True)
    score_grad = (attn_probs * (prob_grad - inner)).astype(BF16)
    query_grad = jnp.einsum("nhqs,nshk->nqhk", score_grad, key_rows, preferred_element_type=F32)
    key_grad = jnp.einsum("nhqs,nqhk->nshk", score_grad, query_rows, preferred_element_type=F32)
    qkv_low = (
        jnp.stack(
            [
                rotate_back(query_grad * score_scale, cosine_table, sine_table),
                rotate_back(key_grad, cosine_table, sine_table),
                value_grad,
            ],
            axis=2,
        )
        .astype(BF16)
        .reshape(512, 768)
    )
    (ln_one_grad,) = merge_rows(8, dot(qkv_low, qkv_full, (1, 1)).reshape(4, 128, 2048))
    norm_in_one, gain_one_grad, bias_one_grad = norm_back(scaled_one, inverse_one, norm_rows[0], ln_one_grad)
    input_grad = hidden_grad + norm_in_one

    small_grad = jnp.concatenate(
        [
            router_grad_w,
            jnp.stack([gain_one_grad, gain_two_grad, bias_one_grad, bias_two_grad], axis=0),
            jnp.zeros((120, 2048), F32),
        ],
        axis=0,
    )
    grads = jnp.concatenate(
        [
            small_grad.astype(BF16).T,
            dot(a_one, qkv_low, (0, 0)).astype(BF16),
            dot(hidden_low, mixed, (0, 0)).astype(BF16),
            dot(a_two, up_low, (0, 0)).astype(BF16),
            dot(branch_rows, activation, (0, 0)).astype(BF16),
        ],
        axis=1,
    )
    own = scatter_gradients(grads.reshape(4, 4, 128, WIDE))
    small_own = jnp.sum(own[:, :, :8].astype(F32), axis=0)
    own_qkv, own_out, own_up, own_down = (own[:, :, a:b].astype(F32) for a, b in (QKV, OUT, UP, DOWN))
    reduced = (
        own_qkv.reshape(4, 32, 3, 2, 128).transpose(1, 2, 0, 3, 4).reshape(32, 3, 8, 128),
        own_out.reshape(4, 32, 2, 128).transpose(0, 2, 3, 1).reshape(8, 128, 32),
        own_up.transpose(1, 0, 2).reshape(32, 4096),
        own_down.transpose(0, 2, 1).reshape(4096, 32),
        small_own[:, :4],
        small_own[:, 4:].T,
    )

    masters = (qkv_weight, out_weight, up_weight, down_weight, router_weight)
    firsts = (qkv_first, out_first, up_first, down_first, router_first)
    seconds = (qkv_second, out_second, up_second, down_second, router_second)
    shares = (1.0, 1.0, 1.0, 1.0, 0.5)
    stepped = [
        moment_step(masters[index], reduced[index], firsts[index], seconds[index], DECAY_RATE)
        for index in range(5)
    ]
    squares = [jnp.sum(masters[index] * masters[index]) * shares[index] for index in range(5)]
    squares += [jnp.sum(stepped[index][2] * stepped[index][2]) * shares[index] for index in range(5)]
    tile = jnp.broadcast_to(jnp.concatenate([jnp.stack(squares), jnp.zeros((118,), F32)])[None], (8, 128))
    norms = jnp.sqrt(total(tile)[0, :10])
    weight_norm, update_norm = norms[:5], norms[5:]
    renewed = [
        masters[index] - LEARN_RATE * (weight_norm[index] / update_norm[index]) * stepped[index][2]
        for index in range(5)
    ]
    norm_moment, norm_square, norm_update = moment_step(norm_master, reduced[5], norm_first, norm_second, 0.0)
    norms_new = norm_master - NORM_RATE * norm_update
    lamb_norms = jnp.stack([weight_norm, update_norm], axis=1)
    return (
        block_output,
        input_grad,
        *reduced,
        *(step[0] for step in stepped),
        norm_moment,
        *(step[1] for step in stepped),
        norm_square,
        *renewed,
        norms_new,
        *(value.astype(BF16) for value in renewed),
        norms_new.astype(BF16),
        lamb_norms,
    )


def solution(mesh):
    qkv, out = P("dp", None, "mp", None), P("mp", None, "dp")
    up, down, router, norms = P("dp", "mp"), P("mp", "dp"), P("dp", None), P(None, "dp")
    rows, tokens = P("dp", None), P("dp")
    matrices = (qkv, out, up, down, router)
    return jax.shard_map(
        local,
        mesh=mesh,
        in_specs=(
            rows, rows, tokens, tokens, tokens, tokens,
            *matrices, norms, norms,
            qkv, qkv, out, out, up, up, down, down, router, router, norms, norms,
        ),
        out_specs=(rows, rows, *((*matrices, norms) * 5), P()),
        check_vma=False,
    )
```

```python
import jax
import jax.numpy as jnp
from jax import lax
from jax.experimental import pallas as pl
from jax.experimental.pallas import tpu as pltpu
from jax.sharding import PartitionSpec as P

STEP = 5

BETA_ONE = 0.5
BETA_TWO = 0.5
ADAM_EPS = 1e-06
DECAY_RATE = 0.01
LEARN_RATE = 0.5
NORM_RATE = 0.1
NORM_EPS = 1e-05
ROPE_BASE = 10000.0

MESH = pl.DeviceIdType.MESH
BF16 = jnp.bfloat16
F32 = jnp.float32
VMEM = pl.BlockSpec(memory_space=pltpu.VMEM)
ANY = pl.BlockSpec(memory_space=pl.ANY)
DMA = pltpu.SemaphoreType.DMA
ALL = slice(None)
LOW, HIGH = pl.ds(0, 64), pl.ds(64, 64)


def place():
    index = lax.axis_index("dp")
    return lax.div(index, 16), lax.rem(lax.div(index, 4), 4), lax.rem(index, 4), lax.axis_index("mp")


def ring(value, step):
    return lax.rem(value + (step + 4), 4)


def device(x, y, z, core):
    return (x * 16 + y * 4 + z, core)


def greet(peers):
    barrier = pltpu.get_barrier_semaphore()
    for peer in peers:
        pl.semaphore_signal(barrier, inc=1, device_id=peer, device_id_type=MESH)
    pl.semaphore_wait(barrier, len(peers))


def send(src, dst, send_sem, recv_sem, peer):
    copy = pltpu.make_async_remote_copy(
        src_ref=src, dst_ref=dst, send_sem=send_sem, recv_sem=recv_sem, device_id=peer, device_id_type=MESH
    )
    copy.start()
    return copy


def span(index, size):
    return pl.ds(pl.multiple_of(index * size, size), size)


def dot(left, right, dims):
    return lax.dot_general(left, right, ((dims[:1], dims[1:]), ((), ())), preferred_element_type=F32)


class Links:
    def __init__(self, send_sems, recv_sems):
        self.x, self.y, self.z, self.core = x, y, z, core = place()
        self.xs = {k: device(ring(x, k), y, z, core) for k in (1, 2, 3)}
        self.ys = {k: device(x, ring(y, k), z, core) for k in (1, 2, 3)}
        self.zs = {k: device(x, y, ring(z, k), core) for k in (1, 2, 3)}
        self.partner = device(x, y, z, 1 - core)
        self.send_sems, self.recv_sems, self.used = send_sems, recv_sems, 0

    def go(self, src, dst, peer):
        number = self.used
        self.used += 1
        return send(src, dst, self.send_sems.at[number], self.recv_sems.at[number], peer)


class Gather:
    def __init__(self, links, first, second):
        self.links, self.parts, self.number, self.copies = links, (first, second), 0, []

    def advance(self):
        for copy in self.copies:
            copy.wait()
        x, y = self.links.x, self.links.y
        xp, xm, yp, ym = self.links.xs[1], self.links.xs[3], self.links.ys[1], self.links.ys[3]
        xb, xa, yb, ya = ring(x, -1), ring(x, 1), ring(y, -1), ring(y, 1)
        moves = {
            0: (((x, y, ALL), xp), ((x, y, ALL), xm), ((x, y, ALL), yp), ((x, y, ALL), ym)),
            1: (((xb, y, LOW), xp), ((xa, y, HIGH), xm), ((x, yb, LOW), yp), ((x, ya, HIGH), ym)),
            2: (((ALL, y, ALL), yp), ((ALL, y, ALL), ym), ((x, ALL, ALL), xp), ((x, ALL, ALL), xm)),
            3: (((ALL, yb, LOW), yp), ((ALL, ya, HIGH), ym), ((xb, ALL, LOW), xp), ((xa, ALL, HIGH), xm)),
        }.get(self.number, ())
        self.number += 1
        self.copies = []
        for index, (where, peer) in enumerate(moves):
            ref, columns = self.parts[index // 2]
            block = ref.at[where + (columns,)]
            self.copies.append(self.links.go(block, block, peer))


def add_into(ref, blocks, columns, sources, row, count):
    steps = count // 16

    def one(index, carry):
        number = lax.div(index, steps)
        step = pl.multiple_of(lax.rem(index, steps) * 16, 16)
        to = blocks[1](number) + (pl.ds(row + step, 16), columns)
        here = ref[to].astype(F32)
        for source, first_row in sources:
            place_in = ((number,) if blocks[0] > 1 else ()) + (pl.ds(first_row + step, 16), ALL)
            here = here + source[place_in].astype(F32)
        ref[to] = here.astype(BF16)
        return carry

    lax.fori_loop(0, blocks[0] * steps, one, 0)


class Scatter:
    def __init__(self, links, first, second, buffers):
        self.links, self.parts = links, (first, second)
        self.buffers = (buffers[:4], buffers[4:])
        self.number, self.halves, self.rest = 0, [], []

    def lanes(self, phase):
        x, y = self.links.x, self.links.y
        found = []
        for part in (0, 1):
            ref, columns = self.parts[part]
            along_y = part == phase
            peers = self.links.ys if along_y else self.links.xs
            if phase == 0 and along_y:
                where, count, each = (lambda k: (ALL, ring(y, k))), 4, (lambda k: lambda i: (i, ring(y, k)))
            elif phase == 0:
                where, count, each = (lambda k: (ring(x, k), ALL)), 4, (lambda k: lambda i: (ring(x, k), i))
            elif along_y:
                where, count, each = (lambda k: (x, ring(y, k))), 1, (lambda k: lambda i: (x, ring(y, k)))
            else:
                where, count, each = (lambda k: (ring(x, k), y)), 1, (lambda k: lambda i: (ring(x, k), y))
            one, two = self.buffers[part][2 * phase : 2 * phase + 2]
            found.append((ref, columns, where, count, each, peers, one, two))
        return found

    def begin(self, phase):
        self.halves, self.rest = [], []
        for ref, columns, where, count, each, peers, one, two in self.lanes(phase):
            lead = (ALL,) if count > 1 else ()
            self.halves.append(self.links.go(ref.at[where(2) + (LOW, columns)], one.at[0], peers[1]))
            self.halves.append(self.links.go(ref.at[where(2) + (HIGH, columns)], one.at[1], peers[3]))
        for ref, columns, where, count, each, peers, one, two in self.lanes(phase):
            lead = (ALL,) if count > 1 else ()
            self.rest.append(
                self.links.go(ref.at[where(1) + (HIGH, columns)], two.at[(0,) + lead + (HIGH,)], peers[1])
            )
            self.rest.append(
                self.links.go(ref.at[where(-1) + (LOW, columns)], two.at[(1,) + lead + (LOW,)], peers[3])
            )

    def middle(self, phase):
        lanes = self.lanes(phase)
        for side in (0, 1):
            for part in (0, 1):
                ref, columns, where, count, each, peers, one, two = lanes[part]
                lead = (ALL,) if count > 1 else ()
                step, rows, row = ((1, LOW, 0), (-1, HIGH, 64))[side]
                self.halves[2 * part + side].wait()
                add_into(ref, (count, each(step)), columns, [(one.at[side], 0)], row, 64)
                self.rest.append(
                    self.links.go(
                        ref.at[where(step) + (rows, columns)], two.at[(side,) + lead + (rows,)], peers[(1, 3)[side]]
                    )
                )

    def end(self, phase):
        for copy in self.rest:
            copy.wait()
        for ref, columns, where, count, each, peers, one, two in self.lanes(phase):
            add_into(ref, (count, each(0)), columns, [(two.at[0], 0), (two.at[1], 0)], 0, 128)

    def advance(self):
        if self.number == 0:
            self.begin(0)
        elif self.number == 1:
            self.middle(0)
        elif self.number == 2:
            self.end(0)
            self.begin(1)
        elif self.number == 3:
            self.middle(1)
        elif self.number == 4:
            self.end(1)
        self.number += 1


class Spread:
    def __init__(self, links, ref):
        self.links, self.ref = links, ref
        self.half = span(links.core, 1024)

    def start(self):
        here = self.ref.at[span(self.links.z, 128), self.half]
        self.flying = [(k, self.links.go(here, here, self.links.zs[k])) for k in (2, 1, 3)]
        return self

    def finish(self):
        passed = []
        for k, copy in self.flying:
            copy.wait_recv()
            block = self.ref.at[span(ring(self.links.z, -k), 128), self.half]
            passed.append(self.links.go(block, block, self.links.partner))
        for _, copy in self.flying:
            copy.wait_send()
        for copy in passed:
            copy.wait()


class Merge:
    def __init__(self, links, left, weights, buffers, out):
        self.links, self.left, self.weights, self.out = links, left, weights, out
        self.c_out, self.c_in, self.z_out, self.z_in, self.kept, self.tmp = buffers
        self.crossing, self.flying = [], []

    def tile(self, half, j):
        rows = self.weights[2 * half + j // 2, 2 * (j % 2) : 2 * (j % 2) + 2]
        return dot(self.left[...], rows.reshape(256, rows.shape[-1]), (1, 1))

    def cross(self):
        for j in range(4):
            columns = pl.ds(256 * j, 256)
            self.c_out[:, columns] = self.tile(1 - self.links.core, j).astype(BF16)
            self.crossing.append(
                self.links.go(self.c_out.at[:, columns], self.c_in.at[:, columns], self.links.partner)
            )
        return self

    def along(self):
        links = self.links
        for j in range(4):
            columns = pl.ds(256 * j, 256)
            value = self.tile(links.core, j)
            self.crossing[j].wait()
            value = value + self.c_in[:, columns].astype(F32)
            self.tmp[...] = value
            self.z_out[:, columns] = value.astype(BF16)
            for k in (2, 1, 3):
                self.flying.append(
                    links.go(
                        self.z_out.at[span(ring(links.z, k), 128), columns],
                        self.z_in.at[k - 1, :, columns],
                        links.zs[k],
                    )
                )
            self.kept[:, columns] = self.tmp[span(links.z, 128), :]
        return self

    def sum(self):
        links = self.links
        for copy in self.flying:
            copy.wait()

        def one(i, carry):
            rows = span(i, 16)
            value = self.kept[rows, :]
            for k in range(3):
                value = value + self.z_in[k, rows, :].astype(F32)
            self.out[rows, span(links.core, 1024)] = value
            return carry

        lax.fori_loop(0, 8, one, 0)
        part = self.out.at[:, span(links.core, 1024)]
        self.last = links.go(part, part, links.partner)
        return self

    def finish(self):
        self.last.wait()


def norm_parts(value):
    centre = value - jnp.mean(value, axis=-1, keepdims=True)
    inverse = lax.rsqrt(jnp.mean(centre * centre, axis=-1, keepdims=True) + NORM_EPS)
    return centre * inverse, inverse


def norm_back(scaled, inverse, gain_row, upstream):
    dscaled = upstream * gain_row
    inner = (
        dscaled
        - jnp.mean(dscaled, axis=-1, keepdims=True)
        - scaled * jnp.mean(dscaled * scaled, axis=-1, keepdims=True)
    )
    return inner * inverse


def fold(value):
    return value[0:8, :] + value[8:16, :]


def columns_tile(columns):
    lane = lax.broadcasted_iota(jnp.int32, (16, 128), 1)
    tile = jnp.zeros((16, 128), F32)
    for index, column in enumerate(columns):
        tile = jnp.where(lane == index, column, tile)
    return tile


def turn(value):
    return pltpu.roll(value, 64, 1)


LINK_COPIES = 400


def layer_kernel(
    qkv_own, out_own, up_own, down_own, small_own, token_in, rows_in, cotangent, cosines, sines,
    block_out, input_grad, qkv_grad, out_grad, up_grad, down_grad, small_grad,
    wq, wo, wu, wd, small_slots, small_grid, small,
    tokens, gates, info,
    a_one, a_two, branch, hidden_low,
    hidden, n_one, n_two, merged, merged_too,
    qkv_wide, qkv, probs, mixed, d_mixed, d_qkv, act, up_low,
    c_out_a, c_in_a, z_out_a, z_in_a, kept_a, c_out_b, c_in_b, z_out_b, z_in_b, kept_b, tmp,
    small_sum, sx_in, sy_in, sz_in,
    *rest,
):
    buffers, (local_sems, send_sems, recv_sems) = rest[:-3], rest[-3:]
    links = Links(send_sems, recv_sems)
    x, y, z, core = links.x, links.y, links.z, links.core
    plane = 4 * x + y
    own_rows, own_32 = span(z, 128), span(z, 32)
    set_a = (c_out_a, c_in_a, z_out_a, z_in_a, kept_a, tmp)
    set_b = (c_out_b, c_in_b, z_out_b, z_in_b, kept_b, tmp)

    local_used = [0]

    def keep(src, dst):
        copy = pltpu.make_async_copy(src, dst, local_sems.at[local_used[0]])
        local_used[0] += 1
        copy.start()
        return copy

    greet([*links.xs.values(), *links.ys.values(), *links.zs.values(), links.partner])

    def to_group(moves):
        copies = []
        for k in (2, 1, 3):
            for src, dst in moves(ring(z, k)):
                copies.append(links.go(src, dst, links.zs[k]))
        for src, dst in moves(z):
            copies.append(keep(src, dst))
        return copies

    def wait(copies):
        for copy in copies:
            copy.wait()

    flying_q = to_group(lambda to: [(qkv_own.at[to], wq.at[x, y, own_32, :])])
    flying_s = []
    small_slots[z] = small_own[...]
    tokens[z] = token_in[...]
    for k in (2, 1, 3):
        flying_s.append(links.go(small_own, small_slots.at[z], links.zs[k]))
    flying_t = [links.go(token_in, tokens.at[z], links.zs[k]) for k in (2, 1, 3)]
    flying_o = to_group(
        lambda to: [(out_own.at[2 * to + h], wo.at[x, y, own_32, pl.ds(128 * h, 128)]) for h in (0, 1)]
    )
    flying_f = to_group(
        lambda to: [
            (up_own.at[:, span(to, 1024)], wu.at[x, y, own_32, :]),
            (down_own.at[:, span(to, 1024)], wd.at[x, y, own_32, :]),
        ]
    )
    wait(flying_q)
    ring_q = Gather(links, (wq, pl.ds(0, 384)), (wq, pl.ds(384, 384)))
    ring_o = Gather(links, (wo, pl.ds(0, 128)), (wo, pl.ds(128, 128)))
    ring_f = Gather(links, (wu, ALL), (wd, ALL))
    ring_q.advance()
    wait(flying_s)
    small_grid[x, y] = small_slots[0] + small_slots[1] + small_slots[2] + small_slots[3]
    here = small_grid.at[x, y]
    wait([links.go(here, here, links.xs[k]) for k in (1, 2, 3)])
    here = small_grid.at[:, y]
    flying_s = [links.go(here, here, links.ys[k]) for k in (1, 2, 3)]
    ring_q.advance()
    wait(flying_s)
    for p in range(16):
        small[:, 128 * p : 128 * p + 128] = small_grid[p // 4, p % 4]

    def norm_one(i, carry):
        rows = span(i, 16)
        scaled, inverse = norm_parts(rows_in[rows, :].astype(F32))
        n_one[rows, :] = scaled
        info[0, rows, :] = columns_tile([inverse])
        a_one[span(z * 8 + i, 16), :] = (scaled * small[4:5, :] + small[6:7, :]).astype(BF16)
        return carry

    lax.fori_loop(0, 8, norm_one, 0)
    rows_one = Spread(links, a_one).start()
    ring_q.advance()
    wait(flying_o)
    ring_o.advance()
    wait(flying_t)
    wait(flying_f)
    rows_one.finish()
    ring_q.advance()
    ring_o.advance()
    branch[own_rows, :] = cotangent[...]
    rows_branch = Spread(links, branch).start()
    ring_q.advance()
    ring_o.advance()
    ring_f.advance()

    for c in range(3):
        part = wq[:, :, :, 256 * c : 256 * c + 256].reshape(2048, 256)
        qkv_wide[:, 256 * c : 256 * c + 256] = dot(a_one[...], part, (1, 0))
    ring_o.advance()
    ring_f.advance()
    lane = lax.broadcasted_iota(jnp.int32, (128, 128), 1)
    causal = lax.broadcasted_iota(jnp.int32, (128, 128), 0) >= lane
    turned_sines = jnp.where(lane < 64, -sines[...], sines[...])
    scale = 128 ** (-0.5)

    def spots(index):
        row, head = lax.div(index, 2), lax.rem(index, 2)
        used = jnp.where((core * 8 + z * 2 + head).astype(F32) < tokens[row][:, 0:1], 1.0, 0.0)
        return span(row, 128), [span(2 * c + head, 128) for c in range(3)], used

    def attend(index, carry):
        rows, (q_at, k_at, v_at), used = spots(index)

        def rotate(value):
            return value * cosines[...] + turn(value) * turned_sines

        q = (rotate(qkv_wide[rows, q_at]) * scale).astype(BF16)
        k = rotate(qkv_wide[rows, k_at]).astype(BF16)
        v = qkv_wide[rows, v_at].astype(BF16)
        qkv[rows, q_at], qkv[rows, k_at], qkv[rows, v_at] = q, k, v
        scores = jnp.where(causal, dot(q, k, (1, 1)), -1e30)
        powers = jnp.exp(scores - jnp.max(scores, axis=-1, keepdims=True))
        share = powers / jnp.sum(powers, axis=-1, keepdims=True)
        probs[index] = share
        mixed[rows, q_at] = (dot(share.astype(BF16), v, (1, 0)) * used).astype(BF16)
        return carry

    lax.fori_loop(0, 8, attend, 0)
    ring_o.advance()
    ring_f.advance()
    merge_one = Merge(links, mixed, wo, set_a, merged).cross().along()
    rows_branch.finish()
    merge_one.sum().finish()

    def norm_two(i, carry):
        rows = span(i, 16)
        value = rows_in[rows, :].astype(F32) + merged[rows, :]
        hidden[rows, :] = value
        scaled, inverse = norm_parts(value)
        n_two[rows, :] = scaled
        low = (scaled * small[5:6, :] + small[7:8, :]).astype(BF16)
        a_two[span(z * 8 + i, 16), :] = low
        low = low.astype(F32)
        logits = [jnp.sum(low * small[b : b + 1, :], axis=-1, keepdims=True) for b in range(4)]
        top = jnp.maximum(jnp.maximum(logits[0], logits[1]), jnp.maximum(logits[2], logits[3]))
        powers = [jnp.exp(logit - top) for logit in logits]
        whole = powers[0] + powers[1] + powers[2] + powers[3]
        chances = [power / whole for power in powers]
        own = token_in[rows, :]
        bucket, kept = own[:, 1:2], own[:, 2:3]
        gate = jnp.zeros_like(bucket)
        for b in range(4):
            gate = jnp.where(bucket == b, chances[b], gate)
        info[1, rows, :] = columns_tile([inverse, gate, *chances])
        gates[z, rows, :] = columns_tile([gate * kept])
        return carry

    lax.fori_loop(0, 8, norm_two, 0)
    rows_two = Spread(links, a_two).start()
    here = gates.at[z]
    flying_g = [links.go(here, here, links.zs[k]) for k in (2, 1, 3)]
    ring_f.advance()
    rows_two.finish()
    wait(flying_g)

    def branch_rows(i, carry):
        rows = span(i, 16)
        gate = gates[lax.div(i, 8), span(lax.rem(i, 8), 16), :][:, 0:1]
        branch[rows, :] = (branch[rows, :].astype(F32) * gate).astype(BF16)
        return carry

    lax.fori_loop(0, 32, branch_rows, 0)
    ring_f.advance()

    quarter = (core * 2 + lax.div(z, 2)).astype(F32)
    used_units = tokens[...].reshape(512, 128)[:, 1:2] >= quarter

    def units(t, carry):
        at = span(t, 256)
        up = dot(a_two[...], wu[:, :, :, at].reshape(2048, 256), (1, 0))
        up = jnp.where(used_units, jnp.maximum(up, 0.0), 0.0)
        act[:, at] = (up * up).astype(BF16)
        back = dot(branch[...], wd[:, :, :, at].reshape(2048, 256), (1, 0))
        up_low[:, at] = (back * 2.0 * up).astype(BF16)
        return carry

    lax.fori_loop(0, 4, units, 0)
    merge_f = Merge(links, act, wd, set_a, merged).cross()
    merge_u = Merge(links, up_low, wu, set_b, merged_too).cross()
    merge_f.along()
    merge_u.along()

    def outer(left, right, target):
        def one(i, carry):
            value = dot(left[:, span(i, 256)], right[...], (0, 0)).astype(BF16)
            row, first = lax.div(i, 2), lax.rem(i, 2) * 2
            target[row, first] = value[0:128]
            target[row, first + 1] = value[128:256]
            return carry

        lax.fori_loop(0, 8, one, 0)

    outer(a_two, up_low, wu)
    outer(branch, act, wd)
    sums_f = Scatter(links, (wu, ALL), (wd, ALL), buffers[0:8])
    sums_f.advance()
    merge_f.sum()
    merge_u.sum()
    merge_f.finish()
    merge_u.finish()

    def back_two(i, carry):
        rows = span(i, 16)
        upstream = cotangent[rows, :].astype(F32)
        own, tile = token_in[rows, :], info[1, rows, :]
        bucket, kept = own[:, 1:2], own[:, 2:3]
        inverse, gate = tile[:, 0:1], tile[:, 1:2]
        produced = merged[rows, :].astype(BF16).astype(F32) * kept
        block_out[rows, :] = (hidden[rows, :] + gate * produced).astype(BF16)
        gate_grad = jnp.sum(upstream * produced, axis=-1, keepdims=True)
        low = a_two[span(z * 8 + i, 16), :].astype(F32)
        grad = merged_too[rows, :].astype(BF16).astype(F32)
        for b in range(4):
            hot = jnp.where(bucket == b, 1.0, 0.0)
            logit_grad = tile[:, 2 + b : 3 + b] * (hot - gate) * gate_grad
            grad = grad + logit_grad * small[b : b + 1, :]
            small_sum[b] += fold(logit_grad * low)
        scaled = n_two[rows, :]
        small_sum[5] += fold(grad * scaled)
        small_sum[7] += fold(grad)
        back = upstream + norm_back(scaled, inverse, small[5:6, :], grad)
        hidden[rows, :] = back
        hidden_low[span(z * 8 + i, 16), :] = back.astype(BF16)
        return carry

    small_sum[...] = jnp.zeros_like(small_sum)
    lax.fori_loop(0, 8, back_two, 0)
    rows_back = Spread(links, hidden_low).start()
    sums_f.advance()
    rows_back.finish()

    d_mixed[...] = dot(hidden_low[...], wo[...].reshape(2048, 256), (1, 0)).astype(BF16)
    sums_f.advance()

    def attend_back(index, carry):
        rows, (q_at, k_at, v_at), used = spots(index)
        share = probs[index]
        q, k, v = qkv[rows, q_at], qkv[rows, k_at], qkv[rows, v_at]
        grad = (d_mixed[rows, q_at].astype(F32) * used).astype(BF16)
        value_grad = dot(share.astype(BF16), grad, (0, 0))
        share_grad = dot(grad, v, (1, 1))
        inner = jnp.sum(share * share_grad, axis=-1, keepdims=True)
        score_grad = (share * (share_grad - inner)).astype(BF16)

        def rotate_back(value):
            return value * cosines[...] - turn(value * sines[...]) * jnp.where(lane < 64, -1.0, 1.0)

        d_qkv[rows, q_at] = rotate_back(dot(score_grad, k, (1, 0)) * scale).astype(BF16)
        d_qkv[rows, k_at] = rotate_back(dot(score_grad, q, (0, 0))).astype(BF16)
        d_qkv[rows, v_at] = value_grad.astype(BF16)
        return carry

    lax.fori_loop(0, 8, attend_back, 0)
    sums_f.advance()
    merge_q = Merge(links, d_qkv, wq, set_a, merged).cross().along()
    outer(a_one, d_qkv, wq)
    outer(hidden_low, mixed, wo)
    sums_q = Scatter(links, (wq, pl.ds(0, 384)), (wq, pl.ds(384, 384)), buffers[8:16])
    sums_o = Scatter(links, (wo, pl.ds(0, 128)), (wo, pl.ds(128, 128)), buffers[16:24])
    sums_f.advance()
    sums_q.advance()
    sums_o.advance()

    def to_owner(moves):
        copies = []
        for k in (2, 1, 3):
            for src, dst in moves(ring(z, k)):
                copies.append(links.go(src, dst, links.zs[k]))
        for src, dst in moves(z):
            copies.append(keep(src, dst))
        return copies

    moved = to_owner(
        lambda to: [
            (wu.at[x, y, span(to, 32), :], up_grad.at[:, span(z, 1024)]),
            (wd.at[x, y, span(to, 32), :], down_grad.at[:, span(z, 1024)]),
        ]
    )
    merge_q.sum().finish()

    def back_one(i, carry):
        rows = span(i, 16)
        grad = merged[rows, :]
        scaled, inverse = n_one[rows, :], info[0, rows, :][:, 0:1]
        small_sum[4] += fold(grad * scaled)
        small_sum[6] += fold(grad)
        input_grad[rows, :] = hidden[rows, :] + norm_back(scaled, inverse, small[4:5, :], grad)
        return carry

    lax.fori_loop(0, 8, back_one, 0)
    for r in range(8):
        small[r : r + 1, :] = jnp.sum(small_sum[r], axis=0, keepdims=True)

    def of_x(to):
        return small.at[:, span(to, 512)]

    copies = [links.go(of_x(ring(x, k)), sx_in.at[k], links.xs[k]) for k in (1, 2, 3)]
    sums_q.advance()
    sums_o.advance()
    wait(copies)
    sx_in[0] = small[:, span(x, 512)]
    sx_in[0] = sx_in[0] + sx_in[1] + sx_in[2] + sx_in[3]
    copies = [
        links.go(sx_in.at[0, :, span(ring(y, k), 128)], sy_in.at[k], links.ys[k]) for k in (1, 2, 3)
    ]
    wait(copies)
    sz_in[z] = sx_in[0, :, span(y, 128)] + sy_in[1] + sy_in[2] + sy_in[3]
    here = sz_in.at[z]
    copies = [links.go(here, here, links.zs[k]) for k in (1, 2, 3)]
    sums_q.advance()
    sums_o.advance()
    wait(copies)
    small_grad[...] = sz_in[0] + sz_in[1] + sz_in[2] + sz_in[3]
    sums_q.advance()
    sums_o.advance()
    sums_q.advance()
    sums_o.advance()
    moved += to_owner(
        lambda to: [
            (wq.at[x, y, span(to, 32), :], qkv_grad.at[z]),
            *((wo.at[x, y, span(to, 32), pl.ds(128 * h, 128)], out_grad.at[2 * z + h]) for h in (0, 1)),
        ]
    )
    wait(moved)


def layer(*operands):
    def vmem(*shape, kind=BF16):
        return pltpu.VMEM(shape, kind)

    def merge_buffers():
        return [vmem(512, 1024), vmem(512, 1024), vmem(512, 1024), vmem(3, 128, 1024), vmem(128, 1024, kind=F32)]

    def sum_buffers(width):
        return [
            vmem(2, 4, 64, width), vmem(2, 4, 128, width), vmem(2, 64, width), vmem(2, 128, width),
        ] * 2

    wide = vmem(128, 2048, kind=F32)
    return pl.pallas_call(
        layer_kernel,
        out_shape=(
            jax.ShapeDtypeStruct((128, 2048), BF16),
            jax.ShapeDtypeStruct((128, 2048), F32),
            jax.ShapeDtypeStruct((4, 32, 768), BF16),
            jax.ShapeDtypeStruct((8, 32, 128), BF16),
            jax.ShapeDtypeStruct((32, 4096), BF16),
            jax.ShapeDtypeStruct((32, 4096), BF16),
            jax.ShapeDtypeStruct((8, 128), F32),
        ),
        in_specs=[ANY] * 4 + [VMEM] * 6,
        out_specs=(VMEM, VMEM, ANY, ANY, ANY, ANY, VMEM),
        scratch_shapes=[
            vmem(4, 4, 128, 768), vmem(4, 4, 128, 256), vmem(4, 4, 128, 1024), vmem(4, 4, 128, 1024),
            vmem(4, 8, 128, kind=F32), vmem(4, 4, 8, 128, kind=F32), vmem(8, 2048, kind=F32),
            vmem(4, 128, 128, kind=F32), vmem(4, 128, 128, kind=F32), vmem(2, 128, 128, kind=F32),
            vmem(512, 2048), vmem(512, 2048), vmem(512, 2048), vmem(512, 2048),
            wide, wide, wide, wide, wide,
            vmem(512, 768, kind=F32), vmem(512, 768), vmem(8, 128, 128, kind=F32),
            vmem(512, 256), vmem(512, 256), vmem(512, 768), vmem(512, 1024), vmem(512, 1024),
            *merge_buffers(), *merge_buffers(), vmem(512, 256, kind=F32),
            vmem(8, 8, 2048, kind=F32), vmem(4, 8, 512, kind=F32), vmem(4, 8, 128, kind=F32),
            vmem(4, 8, 128, kind=F32),
            *sum_buffers(1024), *sum_buffers(384), *sum_buffers(128),
            DMA((20,)), DMA((LINK_COPIES,)), DMA((LINK_COPIES,)),
        ],
        compiler_params=pltpu.CompilerParams(
            collective_id=0, has_side_effects=True, vmem_limit_bytes=63 * 2**20
        ),
        name="layer",
    )(*operands)


def total_kernel(value, out, slots, t_send, t_recv):
    x, y, z, core = place()
    along = (
        [device(x, y, z, 1 - core)],
        [device(x, y, ring(z, k), core) for k in (1, 2, 3)],
        [device(x, ring(y, k), z, core) for k in (1, 2, 3)],
        [device(ring(x, k), y, z, core) for k in (1, 2, 3)],
    )
    greet([peer for peers in along for peer in peers])
    out[...] = value[...]
    for axis, (me, peers) in enumerate(zip((core, z, y, x), along)):
        slots[axis, me] = out[...]
        here = slots.at[axis, me]
        copies = [
            send(here, here, t_send.at[axis, k], t_recv.at[axis, k], peer) for k, peer in enumerate(peers)
        ]
        for copy in copies:
            copy.wait()
        result = slots[axis, 0]
        for k in range(1, len(peers) + 1):
            result = result + slots[axis, k]
        out[...] = result


def total(value):
    return pl.pallas_call(
        total_kernel,
        out_shape=jax.ShapeDtypeStruct((8, 128), F32),
        in_specs=[VMEM],
        out_specs=VMEM,
        scratch_shapes=[pltpu.VMEM((4, 4, 8, 128), F32), DMA((4, 3)), DMA((4, 3))],
        compiler_params=pltpu.CompilerParams(collective_id=2, has_side_effects=True),
        name="total",
    )(value)


def rotary_tables(length, size):
    half_size = size // 2
    frequency = ROPE_BASE ** (-(jnp.arange(half_size, dtype=F32) * 2.0 / size))
    angles = jnp.arange(length, dtype=F32)[:, None] * frequency[None, :]
    cosine_table = jnp.concatenate([jnp.cos(angles), jnp.cos(angles)], axis=-1)
    sine_table = jnp.concatenate([jnp.sin(angles), jnp.sin(angles)], axis=-1)
    return (cosine_table, sine_table)


def moment_step(weight, gradient, first_moment, second_moment, decay_rate):
    first_moment = BETA_ONE * first_moment + (1.0 - BETA_ONE) * gradient
    second_moment = BETA_TWO * second_moment + (1.0 - BETA_TWO) * gradient * gradient
    update = (
        first_moment
        / (1.0 - BETA_ONE**STEP)
        / (jnp.sqrt(second_moment / (1.0 - BETA_TWO**STEP)) + ADAM_EPS)
        + decay_rate * weight
    )
    return (first_moment, second_moment, update)


def local(
    block_input,
    cotangent,
    head_count,
    width_route,
    forced_width,
    slot_index,
    qkv_weight,
    out_weight,
    up_weight,
    down_weight,
    router_weight,
    norm_gains,
    norm_biases,
    qkv_first,
    qkv_second,
    out_first,
    out_second,
    up_first,
    up_second,
    down_first,
    down_second,
    router_first,
    router_second,
    norm_first,
    norm_second,
):
    z = lax.rem(lax.axis_index("dp"), 4)
    norm_master = jnp.concatenate([norm_gains, norm_biases], axis=0)
    bucket = jnp.where(forced_width[0] < 4, forced_width[0], width_route)

    small = jnp.concatenate([router_weight.T, norm_master], axis=0).astype(BF16).astype(F32)
    small = lax.dynamic_update_slice(jnp.zeros((8, 128), F32), small, (0, 32 * z))
    token = jnp.stack([head_count, bucket, (slot_index >= 0).astype(jnp.int32)], axis=1).astype(F32)
    token = jnp.pad(token, ((0, 0), (0, 125)))
    block_output, input_grad, own_qkv, own_out, own_up, own_down, own_small = layer(
        qkv_weight.astype(BF16).reshape(32, 3, 4, 2, 128).transpose(2, 0, 1, 3, 4).reshape(4, 32, 768),
        out_weight.astype(BF16).transpose(0, 2, 1),
        up_weight.astype(BF16),
        down_weight.astype(BF16).T,
        small,
        token,
        block_input,
        cotangent,
        *rotary_tables(128, 128),
    )
    own_small = lax.dynamic_slice(own_small, (0, 32 * z), (8, 32))
    reduced = (
        own_qkv.astype(F32).reshape(4, 32, 3, 2, 128).transpose(1, 2, 0, 3, 4).reshape(32, 3, 8, 128),
        own_out.astype(F32).transpose(0, 2, 1),
        own_up.astype(F32),
        own_down.astype(F32).T,
        own_small[:4].T,
        own_small[4:],
    )

    masters = (qkv_weight, out_weight, up_weight, down_weight, router_weight)
    firsts = (qkv_first, out_first, up_first, down_first, router_first)
    seconds = (qkv_second, out_second, up_second, down_second, router_second)
    shares = (1.0, 1.0, 1.0, 1.0, 0.5)
    stepped = [
        moment_step(masters[index], reduced[index], firsts[index], seconds[index], DECAY_RATE)
        for index in range(5)
    ]
    squares = [jnp.sum(masters[index] * masters[index]) * shares[index] for index in range(5)]
    squares += [jnp.sum(stepped[index][2] * stepped[index][2]) * shares[index] for index in range(5)]
    tile = jnp.broadcast_to(jnp.concatenate([jnp.stack(squares), jnp.zeros((118,), F32)])[None], (8, 128))
    norms = jnp.sqrt(total(tile)[0, :10])
    weight_norm, update_norm = norms[:5], norms[5:]
    renewed = [
        masters[index] - LEARN_RATE * (weight_norm[index] / update_norm[index]) * stepped[index][2]
        for index in range(5)
    ]
    norm_moment, norm_square, norm_update = moment_step(norm_master, reduced[5], norm_first, norm_second, 0.0)
    norms_new = norm_master - NORM_RATE * norm_update
    lamb_norms = jnp.stack([weight_norm, update_norm], axis=1)
    return (
        block_output,
        input_grad,
        *reduced,
        *(step[0] for step in stepped),
        norm_moment,
        *(step[1] for step in stepped),
        norm_square,
        *renewed,
        norms_new,
        *(value.astype(BF16) for value in renewed),
        norms_new.astype(BF16),
        lamb_norms,
    )


def solution(mesh):
    qkv, out = P("dp", None, "mp", None), P("mp", None, "dp")
    up, down, router, norms = P("dp", "mp"), P("mp", "dp"), P("dp", None), P(None, "dp")
    rows, tokens = P("dp", None), P("dp")
    matrices = (qkv, out, up, down, router)
    return jax.shard_map(
        local,
        mesh=mesh,
        in_specs=(
            rows, rows, tokens, tokens, tokens, tokens,
            *matrices, norms, norms,
            qkv, qkv, out, out, up, up, down, down, router, router, norms, norms,
        ),
        out_specs=(rows, rows, *((*matrices, norms) * 5), P()),
        check_vma=False,
    )
```

```python
import jax
import jax.numpy as jnp
import numpy as np
from jax import lax
from jax.experimental import pallas as pl
from jax.experimental.pallas import tpu as pltpu
from jax.sharding import PartitionSpec as P

STEP = 5

BETA_ONE = 0.5
BETA_TWO = 0.5
ADAM_EPS = 1e-06
DECAY_RATE = 0.01
LEARN_RATE = 0.5
NORM_RATE = 0.1
NORM_EPS = 1e-05
ROPE_BASE = 10000.0

MESH = pl.DeviceIdType.MESH
BF16 = jnp.bfloat16
F32 = jnp.float32
VMEM = pl.BlockSpec(memory_space=pltpu.VMEM)
ANY = pl.BlockSpec(memory_space=pl.ANY)
DMA = pltpu.SemaphoreType.DMA
ALL = slice(None)
LOW, HIGH = pl.ds(0, 64), pl.ds(64, 64)


def place():
    index = lax.axis_index("dp")
    return lax.div(index, 16), lax.rem(lax.div(index, 4), 4), lax.rem(index, 4), lax.axis_index("mp")


def ring(value, step):
    return lax.rem(value + (step + 4), 4)


def device(x, y, z, core):
    return (x * 16 + y * 4 + z, core)


def greet(peers):
    barrier = pltpu.get_barrier_semaphore()
    for peer in peers:
        pl.semaphore_signal(barrier, inc=1, device_id=peer, device_id_type=MESH)
    return lambda: pl.semaphore_wait(barrier, len(peers))


def send(src, dst, send_sem, recv_sem, peer):
    copy = pltpu.make_async_remote_copy(
        src_ref=src, dst_ref=dst, send_sem=send_sem, recv_sem=recv_sem, device_id=peer, device_id_type=MESH
    )
    copy.start()
    return copy


def span(index, size):
    return pl.ds(pl.multiple_of(index * size, size), size)


def dot(left, right, dims):
    return lax.dot_general(left, right, ((dims[:1], dims[1:]), ((), ())), preferred_element_type=F32)


class Links:
    def __init__(self, send_sems, recv_sems):
        self.x, self.y, self.z, self.core = x, y, z, core = place()
        self.xs = {k: device(ring(x, k), y, z, core) for k in (1, 2, 3)}
        self.ys = {k: device(x, ring(y, k), z, core) for k in (1, 2, 3)}
        self.zs = {k: device(x, y, ring(z, k), core) for k in (1, 2, 3)}
        self.partner = device(x, y, z, 1 - core)
        self.send_sems, self.recv_sems, self.used = send_sems, recv_sems, 0

    def go(self, src, dst, peer):
        number = self.used
        self.used += 1
        return send(src, dst, self.send_sems.at[number], self.recv_sems.at[number], peer)


class Gather:
    def __init__(self, links, first, second):
        self.links, self.parts, self.number, self.copies = links, (first, second), 0, []

    def advance(self):
        for copy in self.copies:
            copy.wait()
        x, y = self.links.x, self.links.y
        xp, xm, yp, ym = self.links.xs[1], self.links.xs[3], self.links.ys[1], self.links.ys[3]
        xb, xa, yb, ya = ring(x, -1), ring(x, 1), ring(y, -1), ring(y, 1)
        moves = {
            0: (((x, y, ALL), xp), ((x, y, ALL), xm), ((x, y, ALL), yp), ((x, y, ALL), ym)),
            1: (((xb, y, LOW), xp), ((xa, y, HIGH), xm), ((x, yb, LOW), yp), ((x, ya, HIGH), ym)),
            2: (((ALL, y, ALL), yp), ((ALL, y, ALL), ym), ((x, ALL, ALL), xp), ((x, ALL, ALL), xm)),
            3: (((ALL, yb, LOW), yp), ((ALL, ya, HIGH), ym), ((xb, ALL, LOW), xp), ((xa, ALL, HIGH), xm)),
        }.get(self.number, ())
        self.number += 1
        self.copies = []
        for index, (where, peer) in enumerate(moves):
            ref, columns = self.parts[index // 2]
            block = ref.at[where + (columns,)]
            self.copies.append(self.links.go(block, block, peer))


def add_into(ref, blocks, columns, sources, row, count):
    steps = count // 16

    def one(index, carry):
        number = lax.div(index, steps)
        step = pl.multiple_of(lax.rem(index, steps) * 16, 16)
        to = blocks[1](number) + (pl.ds(row + step, 16), columns)
        here = ref[to].astype(F32)
        for source, first_row in sources:
            place_in = ((number,) if blocks[0] > 1 else ()) + (pl.ds(first_row + step, 16), ALL)
            here = here + source[place_in].astype(F32)
        ref[to] = here.astype(BF16)
        return carry

    lax.fori_loop(0, blocks[0] * steps, one, 0)


class Scatter:
    def __init__(self, links, first, second, buffers):
        self.links, self.parts = links, (first, second)
        self.buffers = (buffers[:4], buffers[4:])
        self.number, self.halves, self.rest = 0, [], []

    def lanes(self, phase):
        x, y = self.links.x, self.links.y
        found = []
        for part in (0, 1):
            ref, columns = self.parts[part]
            along_y = part == phase
            peers = self.links.ys if along_y else self.links.xs
            if phase == 0 and along_y:
                where, count, each = (lambda k: (ALL, ring(y, k))), 4, (lambda k: lambda i: (i, ring(y, k)))
            elif phase == 0:
                where, count, each = (lambda k: (ring(x, k), ALL)), 4, (lambda k: lambda i: (ring(x, k), i))
            elif along_y:
                where, count, each = (lambda k: (x, ring(y, k))), 1, (lambda k: lambda i: (x, ring(y, k)))
            else:
                where, count, each = (lambda k: (ring(x, k), y)), 1, (lambda k: lambda i: (ring(x, k), y))
            one, two = self.buffers[part][2 * phase : 2 * phase + 2]
            found.append((ref, columns, where, count, each, peers, one, two))
        return found

    def begin(self, phase):
        self.halves, self.rest = [], []
        for ref, columns, where, count, each, peers, one, two in self.lanes(phase):
            self.halves.append(self.links.go(ref.at[where(2) + (LOW, columns)], one.at[0], peers[1]))
            self.halves.append(self.links.go(ref.at[where(2) + (HIGH, columns)], one.at[1], peers[3]))
        for ref, columns, where, count, each, peers, one, two in self.lanes(phase):
            lead = (ALL,) if count > 1 else ()
            self.rest.append(
                self.links.go(ref.at[where(1) + (HIGH, columns)], two.at[(0,) + lead + (HIGH,)], peers[1])
            )
            self.rest.append(
                self.links.go(ref.at[where(-1) + (LOW, columns)], two.at[(1,) + lead + (LOW,)], peers[3])
            )

    def middle(self, phase):
        lanes = self.lanes(phase)
        for side in (0, 1):
            for part in (0, 1):
                ref, columns, where, count, each, peers, one, two = lanes[part]
                lead = (ALL,) if count > 1 else ()
                step, rows, row = ((1, LOW, 0), (-1, HIGH, 64))[side]
                self.halves[2 * part + side].wait()
                add_into(ref, (count, each(step)), columns, [(one.at[side], 0)], row, 64)
                self.rest.append(
                    self.links.go(
                        ref.at[where(step) + (rows, columns)], two.at[(side,) + lead + (rows,)], peers[(1, 3)[side]]
                    )
                )

    def end(self, phase):
        for copy in self.rest:
            copy.wait()
        for ref, columns, where, count, each, peers, one, two in self.lanes(phase):
            add_into(ref, (count, each(0)), columns, [(two.at[0], 0), (two.at[1], 0)], 0, 128)

    def advance(self):
        if self.number == 0:
            self.begin(0)
        elif self.number == 1:
            self.middle(0)
        elif self.number == 2:
            self.end(0)
            self.begin(1)
        elif self.number == 3:
            self.middle(1)
        elif self.number == 4:
            self.end(1)
        self.number += 1


class Spread:
    def __init__(self, links, ref):
        self.links, self.ref = links, ref
        self.half = span(links.core, 1024)

    def start(self):
        here = self.ref.at[span(self.links.z, 128), self.half]
        self.flying = [(k, self.links.go(here, here, self.links.zs[k])) for k in (2, 1, 3)]
        return self

    def finish(self):
        passed = []
        for k, copy in self.flying:
            copy.wait_recv()
            block = self.ref.at[span(ring(self.links.z, -k), 128), self.half]
            passed.append(self.links.go(block, block, self.links.partner))
        for _, copy in self.flying:
            copy.wait_send()
        for copy in passed:
            copy.wait()


class Merge:
    def __init__(self, links, left, weights, buffers, out):
        self.links, self.left, self.weights, self.out = links, left, weights, out
        self.near, self.near_in, self.far_in, self.tmp = buffers
        self.crossing, self.flying = [], []

    def tile(self, half, j):
        rows = self.weights[2 * half + j // 2, 2 * (j % 2) : 2 * (j % 2) + 2]
        return dot(self.left[...], rows.reshape(256, rows.shape[-1]), (1, 1))

    def cross(self):
        for j in range(4):
            columns = pl.ds(256 * j, 256)
            self.near[:, columns] = self.tile(1 - self.links.core, j).astype(BF16)
            self.crossing.append(
                self.links.go(self.near.at[:, columns], self.near_in.at[:, columns], self.links.partner)
            )
        return self

    def along(self, leave=True):
        for j in range(4):
            columns = pl.ds(256 * j, 256)
            value = self.tile(self.links.core, j)
            self.crossing[j].wait()
            value = value + self.near_in[:, columns].astype(F32)
            self.tmp[...] = value
            self.near[:, columns] = value.astype(BF16)
            if leave:
                self.leave(columns)
            self.out[:, span(self.links.core * 4 + j, 256)] = self.tmp[span(self.links.z, 128), :]
        return self

    def leave(self, columns=ALL):
        links = self.links
        for k in (2, 1, 3):
            self.flying.append(
                links.go(
                    self.near.at[span(ring(links.z, k), 128), columns], self.far_in.at[k - 1, :, columns], links.zs[k]
                )
            )

    def sum(self):
        links = self.links
        for copy in self.flying:
            copy.wait()

        def one(i, carry):
            rows, half = span(i, 16), span(links.core, 1024)
            value = self.out[rows, half]
            for k in range(3):
                value = value + self.far_in[k, rows, :].astype(F32)
            self.out[rows, half] = value
            return carry

        lax.fori_loop(0, 8, one, 0)
        part = self.out.at[:, span(links.core, 1024)]
        self.last = links.go(part, part, links.partner)
        return self

    def finish(self):
        self.last.wait()


def norm_parts(value):
    centre = value - jnp.mean(value, axis=-1, keepdims=True)
    inverse = lax.rsqrt(jnp.mean(centre * centre, axis=-1, keepdims=True) + NORM_EPS)
    return centre * inverse, inverse


def norm_back(scaled, inverse, gain_row, upstream):
    dscaled = upstream * gain_row
    inner = (
        dscaled
        - jnp.mean(dscaled, axis=-1, keepdims=True)
        - scaled * jnp.mean(dscaled * scaled, axis=-1, keepdims=True)
    )
    return inner * inverse


def fold(value):
    return value[0:8, :] + value[8:16, :]


def fold_lanes(value):
    total = None
    for row in range(0, value.shape[0], 8):
        for lane in range(0, value.shape[1], 128):
            part = value[row : row + 8, lane : lane + 128]
            total = part if total is None else total + part
    return total


def columns_tile(columns):
    lane = lax.broadcasted_iota(jnp.int32, (16, 128), 1)
    tile = jnp.zeros((16, 128), F32)
    for index, column in enumerate(columns):
        tile = jnp.where(lane == index, column, tile)
    return tile


def as_columns(rows):
    return jnp.concatenate([rows, jnp.zeros((120, 128), F32)], axis=0).T


def turn(value):
    return pltpu.roll(value, 64, 1)


def moment_step(weight, gradient, first_moment, second_moment, decay_rate):
    first_moment = BETA_ONE * first_moment + (1.0 - BETA_ONE) * gradient
    second_moment = BETA_TWO * second_moment + (1.0 - BETA_TWO) * gradient * gradient
    update = (
        first_moment
        / (1.0 - BETA_ONE**STEP)
        / (jnp.sqrt(second_moment / (1.0 - BETA_TWO**STEP)) + ADAM_EPS)
        + decay_rate * weight
    )
    return (first_moment, second_moment, update)


LINK_COPIES = 400


def layer_kernel(
    qkv_w, out_w, up_w, down_w, qkv_m, qkv_v, out_m, out_v, up_m, up_v, down_m, down_v,
    router_w, router_m, router_v, gains, biases, head_count, width_route, forced_width, slot_index,
    rows_in, cotangent, cosines, sines,
    block_out, input_grad, qkv_grad, out_grad, up_grad, down_grad, small_grad, norms,
    own_q, own_o, own_u, own_d, pack_q, pack_o, pack_u, pack_d, mom_q, mom_o, mom_f,
    wq, wo, wu, wd, small_slots, small_grid, small,
    token_rows, tokens, gate_rows, gates, info,
    a_one, a_two, branch, hidden_low,
    hidden, n_one, n_two, merged, merged_too,
    wide, qkv, probs, mixed, d_mixed, d_qkv, act, up_low,
    near_a, near_in_a, far_in_a, near_b, near_in_b, far_in_b, tmp,
    gate_part, gate_near, gate_far, small_sum, sx_in, sy_in, sz_in, got_q, squares, slots,
    *rest,
):
    buffers, (local_sems, send_sems, recv_sems) = rest[:-3], rest[-3:]
    links = Links(send_sems, recv_sems)
    x, y, z, core = links.x, links.y, links.z, links.core
    own_rows, own_32 = span(z, 128), span(z, 32)
    set_a = (near_a, near_in_a, far_in_a, tmp)
    set_b = (near_b, near_in_b, far_in_b, tmp)
    local_used = [0]

    def keep(src, dst):
        copy = pltpu.make_async_copy(src, dst, local_sems.at[local_used[0]])
        local_used[0] += 1
        copy.start()
        return copy

    def wait(copies):
        for copy in copies:
            copy.wait()

    greeted = greet([*links.xs.values(), *links.ys.values(), *links.zs.values(), links.partner])

    loads = [keep(qkv_w, own_q), keep(out_w, own_o), keep(up_w, own_u), keep(down_w, own_d)]
    later = [
        keep(up_m, mom_f.at[0]), keep(up_v, mom_f.at[1]), keep(qkv_m, mom_q.at[0]), keep(qkv_v, mom_q.at[1]),
        keep(out_m, mom_o.at[0]), keep(out_v, mom_o.at[1]),
    ]
    small_slots[z] = jnp.zeros((8, 128), F32)
    small_slots[z, 0:4, 0:32] = router_w[...].astype(BF16).astype(F32)
    small_slots[z, 4:6, 0:32] = gains[...].astype(BF16).astype(F32)
    small_slots[z, 6:8, 0:32] = biases[...].astype(BF16).astype(F32)
    small_slots[z] = pltpu.roll(small_slots[z], 32 * z, 1)
    bucket_row = jnp.where(forced_width[...] < 4, forced_width[...], width_route[...])
    token_rows[z] = jnp.zeros((8, 128), F32)
    token_rows[z, 0:1, :] = head_count[...].astype(F32)
    token_rows[z, 1:2, :] = bucket_row.astype(F32)
    token_rows[z, 2:3, :] = jnp.where(slot_index[...] >= 0, 1.0, 0.0)
    loads[0].wait()
    for c in range(3):
        for head in range(8):
            at = 256 * c + 128 * (head % 2)
            pack_q[head // 2, :, at : at + 128] = own_q[:, c, head, :].astype(BF16)
    wait(loads[1:])

    def pack(i, carry):
        rows = span(i, 16)
        pack_u[rows, :] = own_u[rows, :].astype(BF16)
        pack_d[rows, :] = own_d[rows, :].astype(BF16)
        for head in range(8):
            pack_o[head, rows, :] = own_o[head, rows, :].astype(BF16)
        return carry

    lax.fori_loop(0, 2, pack, 0)
    greeted()

    def to_group(moves):
        copies = []
        for k in (2, 1, 3):
            for src, dst in moves(ring(z, k)):
                copies.append(links.go(src, dst, links.zs[k]))
        for src, dst in moves(z):
            copies.append(keep(src, dst))
        return copies

    def to_all(ref, peers):
        return [links.go(ref, ref, peers[k]) for k in (1, 2, 3)]

    flying_q = to_group(lambda to: [(pack_q.at[to], wq.at[x, y, own_32, :])])
    flying_s = to_all(small_slots.at[z], links.zs)
    flying_t = to_all(token_rows.at[z], links.zs)
    flying_o = to_group(
        lambda to: [(pack_o.at[2 * to + h], wo.at[x, y, own_32, pl.ds(128 * h, 128)]) for h in (0, 1)]
    )
    flying_f = to_group(
        lambda to: [
            (pack_d.at[:, span(to, 1024)], wd.at[x, y, own_32, :]),
            (pack_u.at[:, span(to, 1024)], wu.at[x, y, own_32, :]),
        ]
    )
    ring_q = Gather(links, (wq, pl.ds(0, 384)), (wq, pl.ds(384, 384)))
    ring_o = Gather(links, (wo, pl.ds(0, 128)), (wo, pl.ds(128, 128)))
    ring_d = Gather(links, (wd, pl.ds(0, 512)), (wd, pl.ds(512, 512)))
    ring_u = Gather(links, (wu, pl.ds(0, 512)), (wu, pl.ds(512, 512)))
    wait(flying_q)
    ring_q.advance()
    wait(flying_s)
    small_grid[x, y] = small_slots[0] + small_slots[1] + small_slots[2] + small_slots[3]
    wait(to_all(small_grid.at[x, y], links.xs))
    flying_s = to_all(small_grid.at[:, y], links.ys)
    ring_q.advance()
    wait(flying_s)
    for p in range(16):
        small[:, 128 * p : 128 * p + 128] = small_grid[p // 4, p % 4]
    ring_q.advance()

    def norm_one(i, carry):
        rows = span(i, 16)
        scaled, inverse = norm_parts(rows_in[rows, :].astype(F32))
        n_one[rows, :] = scaled
        info[0, rows, :] = columns_tile([inverse])
        a_one[span(z * 8 + i, 16), :] = (scaled * small[4:5, :] + small[6:7, :]).astype(BF16)
        return carry

    lax.fori_loop(0, 8, norm_one, 0)
    rows_one = Spread(links, a_one).start()
    branch[own_rows, :] = cotangent[...]
    wait(flying_t)
    for row in range(4):
        tokens[row] = as_columns(token_rows[row])
    ring_q.advance()
    wait(flying_o)
    wait(flying_f)
    ring_o.advance()
    ring_d.advance()
    rows_one.finish()
    rows_branch = Spread(links, branch).start()
    ring_q.advance()
    ring_o.advance()
    ring_d.advance()
    ring_u.advance()

    for c in range(3):
        part = wq[:, :, :, 256 * c : 256 * c + 256].reshape(2048, 256)
        wide[:, 256 * c : 256 * c + 256] = dot(a_one[...], part, (1, 0))
    ring_o.advance()
    ring_d.advance()
    lane = lax.broadcasted_iota(jnp.int32, (128, 128), 1)
    causal = lax.broadcasted_iota(jnp.int32, (128, 128), 0) >= lane
    turned_sines = jnp.where(lane < 64, -sines[...], sines[...])
    scale = 128 ** (-0.5)

    def spots(index):
        row, head = lax.div(index, 2), lax.rem(index, 2)
        used = jnp.where((core * 8 + z * 2 + head).astype(F32) < tokens[row][:, 0:1], 1.0, 0.0)
        return span(row, 128), [span(2 * c + head, 128) for c in range(3)], used

    def attend(index, carry):
        rows, (q_at, k_at, v_at), used = spots(index)

        def rotate(value):
            return value * cosines[...] + turn(value) * turned_sines

        q = (rotate(wide[rows, q_at]) * scale).astype(BF16)
        k = rotate(wide[rows, k_at]).astype(BF16)
        v = wide[rows, v_at].astype(BF16)
        qkv[rows, q_at], qkv[rows, k_at], qkv[rows, v_at] = q, k, v
        scores = jnp.where(causal, dot(q, k, (1, 1)), -1e30)
        powers = jnp.exp(scores - jnp.max(scores, axis=-1, keepdims=True))
        share = powers / jnp.sum(powers, axis=-1, keepdims=True)
        probs[index] = share
        mixed[rows, q_at] = (dot(share.astype(BF16), v, (1, 0)) * used).astype(BF16)
        return carry

    lax.fori_loop(0, 4, attend, 0)
    ring_o.advance()
    ring_u.advance()
    lax.fori_loop(4, 8, attend, 0)
    ring_o.advance()
    merge_one = Merge(links, mixed, wo, set_a, merged).cross().along()
    rows_branch.finish()
    ring_d.advance()
    ring_u.advance()
    merge_one.sum().finish()

    def norm_two(i, carry):
        rows = span(i, 16)
        value = rows_in[rows, :].astype(F32) + merged[rows, :]
        hidden[rows, :] = value
        scaled, inverse = norm_parts(value)
        n_two[rows, :] = scaled
        low = (scaled * small[5:6, :] + small[7:8, :]).astype(BF16)
        a_two[span(z * 8 + i, 16), :] = low
        low = low.astype(F32)
        logits = [jnp.sum(low * small[b : b + 1, :], axis=-1, keepdims=True) for b in range(4)]
        top = jnp.maximum(jnp.maximum(logits[0], logits[1]), jnp.maximum(logits[2], logits[3]))
        powers = [jnp.exp(logit - top) for logit in logits]
        whole = powers[0] + powers[1] + powers[2] + powers[3]
        chances = [power / whole for power in powers]
        own = tokens[z, rows, :]
        bucket, kept = own[:, 1:2], own[:, 2:3]
        gate = jnp.zeros_like(bucket)
        for b in range(4):
            gate = jnp.where(bucket == b, chances[b], gate)
        info[1, rows, :] = columns_tile([inverse, gate, *chances])
        gates[z, rows, :] = columns_tile([gate * kept])
        return carry

    lax.fori_loop(0, 8, norm_two, 0)
    rows_two = Spread(links, a_two).start()
    gate_rows[z] = gates[z].T[0:8, :]
    flying_g = to_all(gate_rows.at[z], links.zs)
    ring_d.advance()

    def units_back(t, carry):
        at = span(t, 256)
        wide[:, at] = dot(branch[...], wd[:, :, :, at].reshape(2048, 256), (1, 0))
        return carry

    lax.fori_loop(0, 4, units_back, 0)
    ring_u.advance()
    rows_two.finish()
    wait(flying_g)
    for row in range(4):
        gates[row] = as_columns(gate_rows[row])
    ring_u.advance()
    quarter = (core * 2 + lax.div(z, 2)).astype(F32)
    used_units = tokens[...].reshape(512, 128)[:, 1:2] >= quarter
    gate_all = gates[...].reshape(512, 128)[:, 0:1]
    gate_part[...] = jnp.zeros((8, 512), F32)

    def units(t, carry):
        at = span(t, 256)
        up = dot(a_two[...], wu[:, :, :, at].reshape(2048, 256), (1, 0))
        up = jnp.where(used_units, jnp.maximum(up, 0.0), 0.0)
        low = (up * up).astype(BF16)
        act[:, at] = low
        back = wide[:, at]
        up_low[:, at] = (back * gate_all * 2.0 * up).astype(BF16)
        pairs = (low.astype(F32) * back).astype(BF16)
        gate_part[...] += dot(jnp.ones((8, 256), BF16), pairs, (1, 1))
        return carry

    lax.fori_loop(0, 4, units, 0)
    crossing_g = links.go(gate_part, gate_near, links.partner)
    merge_u = Merge(links, up_low, wu, set_b, merged_too).cross()
    crossing_g.wait()
    gate_part[...] = gate_part[...] + gate_near[...]
    flying_g = [
        links.go(gate_part.at[:, span(ring(z, k), 128)], gate_far.at[k - 1], links.zs[k]) for k in (1, 2, 3)
    ]
    merge_u.along()

    def outer(left, right, target):
        def one(i, carry):
            value = dot(left[:, span(i, 256)], right[...], (0, 0)).astype(BF16)
            row, first = lax.div(i, 2), lax.rem(i, 2) * 2
            target[row, first] = value[0:128]
            target[row, first + 1] = value[128:256]
            return carry

        lax.fori_loop(0, 8, one, 0)

    outer(a_two, up_low, wu)
    sums_u = Scatter(links, (wu, pl.ds(0, 512)), (wu, pl.ds(512, 512)), buffers[0:8])
    sums_d = Scatter(links, (wd, pl.ds(0, 512)), (wd, pl.ds(512, 512)), buffers[8:16])
    sums_q = Scatter(links, (wq, pl.ds(0, 384)), (wq, pl.ds(384, 384)), buffers[16:24])
    sums_o = Scatter(links, (wo, pl.ds(0, 128)), (wo, pl.ds(128, 128)), buffers[24:32])
    sums_u.advance()
    merge_f = Merge(links, act, wd, set_a, merged).cross().along(leave=False)
    wait(flying_g)
    gate_far[3] = gate_part[:, own_rows] + gate_far[0] + gate_far[1] + gate_far[2]
    gate_grads = as_columns(gate_far[3])
    sums_u.advance()
    merge_u.sum()
    info[2] = gate_grads
    small_sum[...] = jnp.zeros_like(small_sum)
    merge_u.finish()

    def back_two(i, carry):
        rows = span(i, 16)
        upstream = cotangent[rows, :].astype(F32)
        own, tile = tokens[z, rows, :], info[1, rows, :]
        bucket, kept = own[:, 1:2], own[:, 2:3]
        inverse, gate = tile[:, 0:1], tile[:, 1:2]
        gate_grad = info[2, rows, :][:, 0:1] * kept
        low = a_two[span(z * 8 + i, 16), :].astype(F32)
        grad = merged_too[rows, :].astype(BF16).astype(F32)
        for b in range(4):
            hot = jnp.where(bucket == b, 1.0, 0.0)
            logit_grad = tile[:, 2 + b : 3 + b] * (hot - gate) * gate_grad
            grad = grad + logit_grad * small[b : b + 1, :]
            small_sum[b] += fold(logit_grad * low)
        scaled = n_two[rows, :]
        small_sum[5] += fold(grad * scaled)
        small_sum[7] += fold(grad)
        back = upstream + norm_back(scaled, inverse, small[5:6, :], grad)
        n_two[rows, :] = back
        hidden_low[span(z * 8 + i, 16), :] = back.astype(BF16)
        return carry

    lax.fori_loop(0, 8, back_two, 0)
    rows_back = Spread(links, hidden_low).start()

    def branch_rows(i, carry):
        rows = span(i, 16)
        gate = gates[lax.div(i, 8), span(lax.rem(i, 8), 16), :][:, 0:1]
        branch[rows, :] = (branch[rows, :].astype(F32) * gate).astype(BF16)
        return carry

    lax.fori_loop(0, 32, branch_rows, 0)
    outer(branch, act, wd)
    sums_d.advance()
    sums_u.advance()
    rows_back.finish()
    merge_f.leave()

    d_mixed[...] = dot(hidden_low[...], wo[...].reshape(2048, 256), (1, 0)).astype(BF16)
    outer(hidden_low, mixed, wo)
    sums_o.advance()
    sums_u.advance()

    def attend_back(index, carry):
        rows, (q_at, k_at, v_at), used = spots(index)
        share = probs[index]
        q, k, v = qkv[rows, q_at], qkv[rows, k_at], qkv[rows, v_at]
        grad = (d_mixed[rows, q_at].astype(F32) * used).astype(BF16)
        value_grad = dot(share.astype(BF16), grad, (0, 0))
        share_grad = dot(grad, v, (1, 1))
        inner = jnp.sum(share * share_grad, axis=-1, keepdims=True)
        score_grad = (share * (share_grad - inner)).astype(BF16)

        def rotate_back(value):
            return value * cosines[...] - turn(value * sines[...]) * jnp.where(lane < 64, -1.0, 1.0)

        d_qkv[rows, q_at] = rotate_back(dot(score_grad, k, (1, 0)) * scale).astype(BF16)
        d_qkv[rows, k_at] = rotate_back(dot(score_grad, q, (0, 0))).astype(BF16)
        d_qkv[rows, v_at] = value_grad.astype(BF16)
        return carry

    lax.fori_loop(0, 8, attend_back, 0)
    sums_u.advance()
    sums_d.advance()
    merge_f.sum()
    merge_q = Merge(links, d_qkv, wq, set_b, merged_too).cross().along()
    outer(a_one, d_qkv, wq)
    sums_q.advance()
    moved_u = to_group(lambda to: [(wu.at[x, y, span(to, 32), :], up_grad.at[:, span(z, 1024)])])
    sums_d.advance()
    sums_o.advance()
    merge_f.finish()

    def output_rows(i, carry):
        rows = span(i, 16)
        tile, kept = info[1, rows, :], tokens[z, rows, :][:, 2:3]
        produced = merged[rows, :].astype(BF16).astype(F32) * kept
        block_out[rows, :] = (hidden[rows, :] + tile[:, 1:2] * produced).astype(BF16)
        return carry

    lax.fori_loop(0, 8, output_rows, 0)
    wait(moved_u)
    wait(later)

    def add_squares(number, weight, update):
        squares[2 * number] += fold_lanes(weight * weight)
        squares[2 * number + 1] += fold_lanes(update * update)

    squares[...] = jnp.zeros_like(squares)

    def squares_wide(number, weights, grads):
        def one(i, carry):
            at = lax.div(i, 4), lax.rem(i, 4)
            rows, columns = span(at[0], 16), span(at[1], 1024)
            weight = weights[rows, columns]
            _, _, update = moment_step(
                weight, grads[rows, columns].astype(F32), mom_f[0, rows, columns], mom_f[1, rows, columns], DECAY_RATE
            )
            add_squares(number, weight, update)
            return carry

        lax.fori_loop(0, 8, one, 0)

    squares_wide(2, own_u, up_grad)
    later = [keep(down_m, mom_f.at[0]), keep(down_v, mom_f.at[1])]
    merge_q.sum().finish()

    def back_one(i, carry):
        rows = span(i, 16)
        grad = merged_too[rows, :]
        scaled, inverse = n_one[rows, :], info[0, rows, :][:, 0:1]
        small_sum[4] += fold(grad * scaled)
        small_sum[6] += fold(grad)
        input_grad[rows, :] = n_two[rows, :] + norm_back(scaled, inverse, small[4:5, :], grad)
        return carry

    lax.fori_loop(0, 8, back_one, 0)
    for r in range(8):
        small[r : r + 1, :] = jnp.sum(small_sum[r], axis=0, keepdims=True)

    copies = [links.go(small.at[:, span(ring(x, k), 512)], sx_in.at[k], links.xs[k]) for k in (1, 2, 3)]
    sums_q.advance()
    sums_d.advance()
    sums_o.advance()
    wait(copies)
    sx_in[0] = small[:, span(x, 512)] + sx_in[1] + sx_in[2] + sx_in[3]
    copies = [
        links.go(sx_in.at[0, :, span(ring(y, k), 128)], sy_in.at[k], links.ys[k]) for k in (1, 2, 3)
    ]
    sums_d.advance()
    moved_d = to_group(lambda to: [(wd.at[x, y, span(to, 32), :], down_grad.at[:, span(z, 1024)])])
    wait(copies)
    sz_in[z] = sx_in[0, :, span(y, 128)] + sy_in[1] + sy_in[2] + sy_in[3]
    flying_s = to_all(sz_in.at[z], links.zs)
    sums_q.advance()
    sums_o.advance()
    sums_q.advance()
    sums_o.advance()
    moved_o = to_group(
        lambda to: [
            (wo.at[x, y, span(to, 32), pl.ds(128 * h, 128)], out_grad.at[2 * z + h]) for h in (0, 1)
        ]
    )
    wait(moved_d)
    wait(later)
    squares_wide(3, own_d, down_grad)
    wait(flying_s)
    small_slots[0] = pltpu.roll(sz_in[0] + sz_in[1] + sz_in[2] + sz_in[3], 128 - 32 * z, 1)
    small_grad[...] = small_slots[0]
    sums_q.advance()
    moved_q = to_group(lambda to: [(wq.at[x, y, span(to, 32), :], got_q.at[z])])
    wait(moved_o)

    def squares_out(head, carry):
        _, _, update = moment_step(
            own_o[head], out_grad[head].astype(F32), mom_o[0, head], mom_o[1, head], DECAY_RATE
        )
        add_squares(1, own_o[head], update)
        return carry

    lax.fori_loop(0, 8, squares_out, 0)
    _, _, update = moment_step(
        router_w[...], small_slots[0, 0:4, 0:32], router_m[...], router_v[...], DECAY_RATE
    )
    squares[8, 0:4, 0:32] = 0.5 * router_w[...] * router_w[...]
    squares[9, 0:4, 0:32] = 0.5 * update * update
    wait(moved_q)
    for c in range(3):
        for head in range(8):
            at = 256 * c + 128 * (head % 2)
            qkv_grad[:, c, head, :] = got_q[head // 2, :, at : at + 128].astype(F32)

    def squares_qkv(i, carry):
        rows = pl.ds(i * 4, 4)
        _, _, update = moment_step(
            own_q[rows], qkv_grad[rows], mom_q[0, rows], mom_q[1, rows], DECAY_RATE
        )
        squares[0] += jnp.sum(jnp.sum(own_q[rows] * own_q[rows], axis=0), axis=0)
        squares[1] += jnp.sum(jnp.sum(update * update, axis=0), axis=0)
        return carry

    lax.fori_loop(0, 8, squares_qkv, 0)

    lanes = lax.broadcasted_iota(jnp.int32, (8, 128), 1)
    tile = jnp.zeros((8, 128), F32)
    for number in range(10):
        value = jnp.sum(jnp.sum(squares[number], axis=0, keepdims=True), axis=1, keepdims=True)
        tile = jnp.where(lanes == number // 2 + 5 * (number % 2), value, tile)
    for axis, (me, peers) in enumerate(
        ((core, {1: links.partner}), (z, links.zs), (y, links.ys), (x, links.xs))
    ):
        slots[axis, me] = tile
        here = slots.at[axis, me]
        wait([links.go(here, here, peer) for peer in peers.values()])
        tile = slots[axis, 0] + slots[axis, 1]
        if axis:
            tile = tile + slots[axis, 2] + slots[axis, 3]
    norms[...] = tile


def layer(*operands):
    def vmem(*shape, kind=BF16):
        return pltpu.VMEM(shape, kind)

    def merge_buffers():
        return [vmem(512, 1024), vmem(512, 1024), vmem(3, 128, 1024)]

    def sum_buffers(width):
        return [
            vmem(2, 4, 64, width), vmem(2, 4, 128, width), vmem(2, 64, width), vmem(2, 128, width),
        ] * 2

    rows = vmem(128, 2048, kind=F32)
    return pl.pallas_call(
        layer_kernel,
        out_shape=(
            jax.ShapeDtypeStruct((128, 2048), BF16),
            jax.ShapeDtypeStruct((128, 2048), F32),
            jax.ShapeDtypeStruct((32, 3, 8, 128), F32),
            jax.ShapeDtypeStruct((8, 32, 128), BF16),
            jax.ShapeDtypeStruct((32, 4096), BF16),
            jax.ShapeDtypeStruct((32, 4096), BF16),
            jax.ShapeDtypeStruct((8, 128), F32),
            jax.ShapeDtypeStruct((8, 128), F32),
        ),
        in_specs=[ANY] * 12 + [VMEM] * 13,
        out_specs=(VMEM,) * 8,
        scratch_shapes=[
            vmem(32, 3, 8, 128, kind=F32), vmem(8, 32, 128, kind=F32), vmem(32, 4096, kind=F32),
            vmem(32, 4096, kind=F32),
            vmem(4, 32, 768), vmem(8, 32, 128), vmem(32, 4096), vmem(32, 4096),
            vmem(2, 32, 3, 8, 128, kind=F32), vmem(2, 8, 32, 128, kind=F32), vmem(2, 32, 4096, kind=F32),
            vmem(4, 4, 128, 768), vmem(4, 4, 128, 256), vmem(4, 4, 128, 1024), vmem(4, 4, 128, 1024),
            vmem(4, 8, 128, kind=F32), vmem(4, 4, 8, 128, kind=F32), vmem(8, 2048, kind=F32),
            vmem(4, 8, 128, kind=F32), vmem(4, 128, 128, kind=F32), vmem(4, 8, 128, kind=F32),
            vmem(4, 128, 128, kind=F32), vmem(3, 128, 128, kind=F32),
            vmem(512, 2048), vmem(512, 2048), vmem(512, 2048), vmem(512, 2048),
            rows, rows, rows, rows, rows,
            vmem(512, 1024, kind=F32), vmem(512, 768), vmem(8, 128, 128, kind=F32),
            vmem(512, 256), vmem(512, 256), vmem(512, 768), vmem(512, 1024), vmem(512, 1024),
            *merge_buffers(), *merge_buffers(), vmem(512, 256, kind=F32),
            vmem(8, 512, kind=F32), vmem(8, 512, kind=F32), vmem(4, 8, 128, kind=F32),
            vmem(8, 8, 2048, kind=F32), vmem(4, 8, 512, kind=F32), vmem(4, 8, 128, kind=F32),
            vmem(4, 8, 128, kind=F32), vmem(4, 32, 768), vmem(10, 8, 128, kind=F32), vmem(4, 4, 8, 128, kind=F32),
            *sum_buffers(512), *sum_buffers(512), *sum_buffers(384), *sum_buffers(128),
            DMA((40,)), DMA((LINK_COPIES,)), DMA((LINK_COPIES,)),
        ],
        compiler_params=pltpu.CompilerParams(
            collective_id=0, has_side_effects=True, vmem_limit_bytes=63 * 2**20
        ),
        name="layer",
    )(*operands)


def renew_kernel(norms, small_grad, gains, biases, norm_m, norm_v, *refs):
    ins, outs = refs[:20], refs[20:]
    sums = norms[0:1, :]
    for index in range(5):
        weight, grad, m, v = (ref[...] for ref in ins[4 * index : 4 * index + 4])
        grad = grad[0:4, 0:32] if index == 4 else grad.astype(F32)
        first, second, update = moment_step(weight, grad, m, v, DECAY_RATE)
        ratio = LEARN_RATE * (jnp.sqrt(sums[:, index : index + 1]) / jnp.sqrt(sums[:, index + 5 : index + 6]))
        ratio = ratio.reshape((1,) * weight.ndim)
        new = weight - ratio * update
        for ref, value in zip(outs[5 * index : 5 * index + 5], (grad, first, second, new, new.astype(BF16))):
            ref[...] = value
    grad = small_grad[4:8, 0:32]
    master = jnp.concatenate([gains[...], biases[...]], axis=0)
    first, second, update = moment_step(master, grad, norm_m[...], norm_v[...], 0.0)
    new = master - NORM_RATE * update
    for ref, value in zip(outs[25:30], (grad, first, second, new, new.astype(BF16))):
        ref[...] = value
    row = lax.broadcasted_iota(jnp.int32, (8, 128), 0)
    lane = lax.broadcasted_iota(jnp.int32, (8, 128), 1)
    tile = jnp.zeros((8, 128), F32)
    for index in range(10):
        here = (row == index % 5) & (lane == index // 5)
        tile = jnp.where(here, jnp.sqrt(sums[:, index : index + 1]), tile)
    outs[30][...] = tile[0:5, 0:2]


def renew(norms, small_grad, gains, biases, norm_m, norm_v, *matrices):
    steps = 4

    def whole(shape):
        return pl.BlockSpec(shape, lambda i: (0,) * len(shape))

    blocks = (
        pl.BlockSpec((32 // steps, 3, 8, 128), lambda i: (i, 0, 0, 0)),
        pl.BlockSpec((8 // steps, 32, 128), lambda i: (i, 0, 0)),
        pl.BlockSpec((32, 4096 // steps), lambda i: (0, i)),
        pl.BlockSpec((32, 4096 // steps), lambda i: (0, i)),
        whole((4, 32)),
    )
    shapes = ((32, 3, 8, 128), (8, 32, 128), (32, 4096), (32, 4096), (4, 32), (4, 32))
    in_specs = [whole((8, 128)), whole((8, 128)), whole((2, 32)), whole((2, 32)), whole((4, 32)), whole((4, 32))]
    out_specs, out_shape = [], []
    for index, block in enumerate(blocks):
        in_specs += [block, whole((8, 128)) if index == 4 else block, block, block]
    for block, shape in zip((*blocks, whole((4, 32))), shapes):
        out_specs += [block] * 5
        out_shape += [jax.ShapeDtypeStruct(shape, kind) for kind in (F32, F32, F32, F32, BF16)]
    out_specs.append(whole((5, 2)))
    out_shape.append(jax.ShapeDtypeStruct((5, 2), F32))
    return pl.pallas_call(
        renew_kernel,
        grid=(steps,),
        in_specs=in_specs,
        out_specs=out_specs,
        out_shape=out_shape,
        compiler_params=pltpu.CompilerParams(vmem_limit_bytes=63 * 2**20),
        name="renew",
    )(norms, small_grad, gains, biases, norm_m, norm_v, *matrices)


def rotary_tables(length, size):
    half_size = size // 2
    frequency = ROPE_BASE ** (-(np.arange(half_size) * 2.0 / size))
    angles = np.arange(length)[:, None] * frequency[None, :]
    cosine_table = np.concatenate([np.cos(angles), np.cos(angles)], axis=-1)
    sine_table = np.concatenate([np.sin(angles), np.sin(angles)], axis=-1)
    return (cosine_table.astype(np.float32), sine_table.astype(np.float32))


def local(
    block_input,
    cotangent,
    head_count,
    width_route,
    forced_width,
    slot_index,
    qkv_weight,
    out_weight,
    up_weight,
    down_weight,
    router_weight,
    norm_gains,
    norm_biases,
    qkv_first,
    qkv_second,
    out_first,
    out_second,
    up_first,
    up_second,
    down_first,
    down_second,
    router_first,
    router_second,
    norm_first,
    norm_second,
):
    def turned(value):
        return value.transpose(0, 2, 1)

    out = turned(out_weight), turned(out_first), turned(out_second)
    down = down_weight.T, down_first.T, down_second.T
    router = router_weight.T, router_first.T, router_second.T
    block_output, input_grad, *grads, small_grad, norms = layer(
        qkv_weight, out[0], up_weight, down[0],
        qkv_first, qkv_second, *out[1:], up_first, up_second, *down[1:],
        *router, norm_gains, norm_biases,
        *(value.reshape(1, -1) for value in (head_count, width_route, forced_width, slot_index)),
        block_input, cotangent, *rotary_tables(128, 128),
    )
    *results, lamb_norms = renew(
        norms, small_grad, norm_gains, norm_biases, norm_first, norm_second,
        qkv_weight, grads[0], qkv_first, qkv_second,
        out[0], grads[1], *out[1:],
        up_weight, grads[2], up_first, up_second,
        down[0], grads[3], *down[1:],
        router[0], small_grad, *router[1:],
    )
    kinds = []
    for kind in range(5):
        qkv, out, up, down, router, norm = (results[5 * index + kind] for index in range(6))
        kinds += [qkv, turned(out), up, down.T, router.T, norm]
    return (block_output, input_grad, *kinds, lamb_norms)


def solution(mesh):
    qkv, out = P("dp", None, "mp", None), P("mp", None, "dp")
    up, down, router, norms = P("dp", "mp"), P("mp", "dp"), P("dp", None), P(None, "dp")
    rows, tokens = P("dp", None), P("dp")
    matrices = (qkv, out, up, down, router)
    return jax.shard_map(
        local,
        mesh=mesh,
        in_specs=(
            rows, rows, tokens, tokens, tokens, tokens,
            *matrices, norms, norms,
            qkv, qkv, out, out, up, up, down, down, router, router, norms, norms,
        ),
        out_specs=(rows, rows, *((*matrices, norms) * 5), P()),
        check_vma=False,
    )
```

```python
import jax
import jax.numpy as jnp
import numpy as np
from jax import lax
from jax.experimental import pallas as pl
from jax.experimental.pallas import tpu as pltpu
from jax.sharding import PartitionSpec as P

STEP = 5

BETA_ONE = 0.5
BETA_TWO = 0.5
ADAM_EPS = 1e-06
DECAY_RATE = 0.01
LEARN_RATE = 0.5
NORM_RATE = 0.1
NORM_EPS = 1e-05
ROPE_BASE = 10000.0

MESH = pl.DeviceIdType.MESH
BF16 = jnp.bfloat16
F32 = jnp.float32
VMEM = pl.BlockSpec(memory_space=pltpu.VMEM)
ANY = pl.BlockSpec(memory_space=pl.ANY)
DMA = pltpu.SemaphoreType.DMA
ALL = slice(None)
LOW, HIGH = pl.ds(0, 64), pl.ds(64, 64)


def place():
    index = lax.axis_index("dp")
    return lax.div(index, 16), lax.rem(lax.div(index, 4), 4), lax.rem(index, 4), lax.axis_index("mp")


def ring(value, step):
    return lax.rem(value + (step + 4), 4)


def device(x, y, z, core):
    return (x * 16 + y * 4 + z, core)


def greet(peers):
    barrier = pltpu.get_barrier_semaphore()
    for peer in peers:
        pl.semaphore_signal(barrier, inc=1, device_id=peer, device_id_type=MESH)
    return lambda: pl.semaphore_wait(barrier, len(peers))


def send(src, dst, send_sem, recv_sem, peer):
    copy = pltpu.make_async_remote_copy(
        src_ref=src, dst_ref=dst, send_sem=send_sem, recv_sem=recv_sem, device_id=peer, device_id_type=MESH
    )
    copy.start()
    return copy


def span(index, size):
    return pl.ds(pl.multiple_of(index * size, size), size)


def dot(left, right, dims):
    return lax.dot_general(left, right, ((dims[:1], dims[1:]), ((), ())), preferred_element_type=F32)


class Links:
    def __init__(self, send_sems, recv_sems):
        self.x, self.y, self.z, self.core = x, y, z, core = place()
        self.xs = {k: device(ring(x, k), y, z, core) for k in (1, 2, 3)}
        self.ys = {k: device(x, ring(y, k), z, core) for k in (1, 2, 3)}
        self.zs = {k: device(x, y, ring(z, k), core) for k in (1, 2, 3)}
        self.others = {k: device(x, y, ring(z, k), 1 - core) for k in (1, 2, 3)}
        self.partner = device(x, y, z, 1 - core)
        self.send_sems, self.recv_sems, self.used = send_sems, recv_sems, 0

    def go(self, src, dst, peer):
        number = self.used
        self.used += 1
        return send(src, dst, self.send_sems.at[number], self.recv_sems.at[number], peer)


class Gather:
    def __init__(self, links, first, second):
        self.links, self.parts, self.number, self.copies = links, (first, second), 0, []

    def advance(self):
        for copy in self.copies:
            copy.wait()
        x, y = self.links.x, self.links.y
        xp, xm, yp, ym = self.links.xs[1], self.links.xs[3], self.links.ys[1], self.links.ys[3]
        xb, xa, yb, ya = ring(x, -1), ring(x, 1), ring(y, -1), ring(y, 1)
        moves = {
            0: (((x, y, ALL), xp), ((x, y, ALL), xm), ((x, y, ALL), yp), ((x, y, ALL), ym)),
            1: (((xb, y, LOW), xp), ((xa, y, HIGH), xm), ((x, yb, LOW), yp), ((x, ya, HIGH), ym)),
            2: (((ALL, y, ALL), yp), ((ALL, y, ALL), ym), ((x, ALL, ALL), xp), ((x, ALL, ALL), xm)),
            3: (((ALL, yb, LOW), yp), ((ALL, ya, HIGH), ym), ((xb, ALL, LOW), xp), ((xa, ALL, HIGH), xm)),
        }.get(self.number, ())
        self.number += 1
        self.copies = []
        for index, (where, peer) in enumerate(moves):
            ref, columns = self.parts[index // 2]
            block = ref.at[where + (columns,)]
            self.copies.append(self.links.go(block, block, peer))


def add_into(ref, blocks, columns, sources, row, count):
    steps = count // 16

    def one(index, carry):
        number = lax.div(index, steps)
        step = pl.multiple_of(lax.rem(index, steps) * 16, 16)
        to = blocks[1](number) + (pl.ds(row + step, 16), columns)
        here = ref[to].astype(F32)
        for source, first_row in sources:
            place_in = ((number,) if blocks[0] > 1 else ()) + (pl.ds(first_row + step, 16), ALL)
            here = here + source[place_in].astype(F32)
        ref[to] = here.astype(BF16)
        return carry

    lax.fori_loop(0, blocks[0] * steps, one, 0)


class Scatter:
    def __init__(self, links, first, second, buffers):
        self.links, self.parts = links, (first, second)
        self.buffers = (buffers[:4], buffers[4:])
        self.number, self.halves, self.rest = 0, [], []

    def lanes(self, phase):
        x, y = self.links.x, self.links.y
        found = []
        for part in (0, 1):
            ref, columns = self.parts[part]
            along_y = part == phase
            peers = self.links.ys if along_y else self.links.xs
            if phase == 0 and along_y:
                where, count, each = (lambda k: (ALL, ring(y, k))), 4, (lambda k: lambda i: (i, ring(y, k)))
            elif phase == 0:
                where, count, each = (lambda k: (ring(x, k), ALL)), 4, (lambda k: lambda i: (ring(x, k), i))
            elif along_y:
                where, count, each = (lambda k: (x, ring(y, k))), 1, (lambda k: lambda i: (x, ring(y, k)))
            else:
                where, count, each = (lambda k: (ring(x, k), y)), 1, (lambda k: lambda i: (ring(x, k), y))
            one, two = self.buffers[part][2 * phase : 2 * phase + 2]
            found.append((ref, columns, where, count, each, peers, one, two))
        return found

    def begin(self, phase):
        self.halves, self.rest = [], []
        for ref, columns, where, count, each, peers, one, two in self.lanes(phase):
            self.halves.append(self.links.go(ref.at[where(2) + (LOW, columns)], one.at[0], peers[1]))
            self.halves.append(self.links.go(ref.at[where(2) + (HIGH, columns)], one.at[1], peers[3]))
        for ref, columns, where, count, each, peers, one, two in self.lanes(phase):
            lead = (ALL,) if count > 1 else ()
            self.rest.append(
                self.links.go(ref.at[where(1) + (HIGH, columns)], two.at[(0,) + lead + (HIGH,)], peers[1])
            )
            self.rest.append(
                self.links.go(ref.at[where(-1) + (LOW, columns)], two.at[(1,) + lead + (LOW,)], peers[3])
            )

    def middle(self, phase):
        lanes = self.lanes(phase)
        for side in (0, 1):
            for part in (0, 1):
                ref, columns, where, count, each, peers, one, two = lanes[part]
                lead = (ALL,) if count > 1 else ()
                step, rows, row = ((1, LOW, 0), (-1, HIGH, 64))[side]
                self.halves[2 * part + side].wait()
                add_into(ref, (count, each(step)), columns, [(one.at[side], 0)], row, 64)
                self.rest.append(
                    self.links.go(
                        ref.at[where(step) + (rows, columns)], two.at[(side,) + lead + (rows,)], peers[(1, 3)[side]]
                    )
                )

    def end(self, phase):
        for copy in self.rest:
            copy.wait()
        for ref, columns, where, count, each, peers, one, two in self.lanes(phase):
            add_into(ref, (count, each(0)), columns, [(two.at[0], 0), (two.at[1], 0)], 0, 128)

    def advance(self):
        if self.number == 0:
            self.begin(0)
        elif self.number == 1:
            self.middle(0)
        elif self.number == 2:
            self.end(0)
            self.begin(1)
        elif self.number == 3:
            self.middle(1)
        elif self.number == 4:
            self.end(1)
        self.number += 1


class Spread:
    def __init__(self, links, ref):
        self.links, self.ref = links, ref

    def start(self, own=True):
        links = self.links
        here = self.ref.at[links.z, links.core]
        self.passed = [links.go(here, here, links.partner)] if own else []
        self.flying = [links.go(here, here, links.zs[k]) for k in (1, 3)]

    def relay(self):
        links = self.links
        self.far = []
        for side, k, rows in ((0, 1, pl.ds(0, 32)), (1, 3, pl.ds(32, 32))):
            self.flying[side].wait_recv()
            block = self.ref.at[ring(links.z, -k), links.core]
            half = block.at[rows]
            self.far.append(links.go(half, half, links.zs[k]))
            self.passed.append(links.go(block, block, links.partner))

    def finish(self):
        links = self.links
        for copy in self.far:
            copy.wait_recv()
        block = self.ref.at[ring(links.z, 2), links.core]
        self.passed.append(links.go(block, block, links.partner))
        for copy in self.flying + self.far:
            copy.wait_send()
        for copy in self.passed:
            copy.wait()


TILES, TILE = 4, 512


class Merge:
    def __init__(self, links, left, weights, buffers, out):
        self.links, self.left, self.weights, self.out = links, left, weights, out
        self.near, self.near_in, self.far_in, self.tmp = buffers
        self.crossing, self.flying = [], []

    def tile(self, half, j):
        rows = self.weights[j]
        left = self.left[:, half]
        return dot(left.reshape(256, left.shape[-1]), rows.reshape(TILE, rows.shape[-1]), (1, 1))

    def cross(self):
        for j in range(TILES):
            self.near[j] = self.tile(1 - self.links.core, j).astype(BF16).reshape(4, 64, TILE)
            self.crossing.append(self.links.go(self.near.at[j], self.near_in.at[j], self.links.partner))

    def along(self, leave=True):
        for j in range(TILES):
            value = self.tile(self.links.core, j)
            self.crossing[j].wait()
            value = value + self.near_in[j].astype(F32).reshape(256, TILE)
            self.tmp[...] = value
            self.near[j] = value.astype(BF16).reshape(4, 64, TILE)
            if leave:
                self.leave(j)
            self.out[:, TILE * j : TILE * j + TILE] = self.tmp[span(self.links.z, 64), :]

    def leave(self, j=None):
        links = self.links
        for k in (2, 1, 3):
            if j is None:
                src, dst = self.near.at[:, ring(links.z, k)], self.far_in.at[k - 1]
            else:
                src, dst = self.near.at[j, ring(links.z, k)], self.far_in.at[k - 1, j]
            self.flying.append(links.go(src, dst, links.zs[k]))

    def arrive(self):
        for copy in self.flying:
            copy.wait()

    def rows(self, rows):
        value = self.out[rows, :]
        for k in range(3):
            parts = [self.far_in[k, j, rows, :] for j in range(TILES)]
            value = value + jnp.concatenate(parts, axis=1).astype(F32)
        return value


def norm_parts(value):
    centre = value - jnp.mean(value, axis=-1, keepdims=True)
    inverse = lax.rsqrt(jnp.mean(centre * centre, axis=-1, keepdims=True) + NORM_EPS)
    return centre * inverse, inverse


def norm_back(scaled, inverse, gain_row, upstream):
    dscaled = upstream * gain_row
    inner = (
        dscaled
        - jnp.mean(dscaled, axis=-1, keepdims=True)
        - scaled * jnp.mean(dscaled * scaled, axis=-1, keepdims=True)
    )
    return inner * inverse


def fold(value):
    return value[0:8, :] + value[8:16, :]


def fold_lanes(value):
    total = None
    for row in range(0, value.shape[0], 8):
        for lane in range(0, value.shape[1], 128):
            part = value[row : row + 8, lane : lane + 128]
            total = part if total is None else total + part
    return total


def columns_tile(columns):
    lane = lax.broadcasted_iota(jnp.int32, (16, 128), 1)
    tile = jnp.zeros((16, 128), F32)
    for index, column in enumerate(columns):
        tile = jnp.where(lane == index, column, tile)
    return tile


def as_columns(rows):
    return jnp.concatenate([rows, jnp.zeros((120, 128), F32)], axis=0).T


def turn(value):
    return pltpu.roll(value, 64, 1)


def moment_step(weight, gradient, first_moment, second_moment, decay_rate):
    first_moment = BETA_ONE * first_moment + (1.0 - BETA_ONE) * gradient
    second_moment = BETA_TWO * second_moment + (1.0 - BETA_TWO) * gradient * gradient
    update = (
        first_moment
        / (1.0 - BETA_ONE**STEP)
        / (jnp.sqrt(second_moment / (1.0 - BETA_TWO**STEP)) + ADAM_EPS)
        + decay_rate * weight
    )
    return (first_moment, second_moment, update)


LINK_COPIES = 324
LOCAL_COPIES = 28


def layer_kernel(
    qkv_w, out_w, up_w, down_w, qkv_m, qkv_v, out_m, out_v, up_m, up_v, down_m, down_v, block_in, cotangent,
    router_w, router_m, router_v, gains, biases, head_count, width_route, forced_width, slot_index, cosines, sines,
    block_out, input_grad, qkv_grad, out_grad, up_grad, down_grad, small_grad, norms,
    own_q, own_o, own_u, own_d, pack_q, pack_o, pack_u, pack_d, mom_q, mom_o, mom_f,
    wq, wo, wu, wd, small_slots, small_grid, small, small_near,
    token_rows, tokens, gate_slots, gates, info,
    a_one, a_two, branch, hidden_low,
    rows_in, upstream_in, hidden, n_one, n_two, merged, merged_too, out_rows, grad_rows,
    wide, qkv, probs, mixed, d_mixed, d_qkv, act, up_low,
    near_a, near_in_a, far_in_a, near_b, near_in_b, far_in_b, tmp,
    gate_part, gate_near, gate_far, small_sum, sx_in, sy_in, sz_in, got_q, squares, slots,
    *rest,
):
    buffers, (local_sems, send_sems, recv_sems) = rest[:-3], rest[-3:]
    links = Links(send_sems, recv_sems)
    x, y, z, core = links.x, links.y, links.z, links.core
    own_32, own_64 = span(z, 32), span(core, 64)
    set_a = (near_a, near_in_a, far_in_a, tmp)
    set_b = (near_b, near_in_b, far_in_b, tmp)
    local_used, pending = [0], {}

    def keep(src, dst):
        copy = pltpu.make_async_copy(src, dst, local_sems.at[local_used[0]])
        local_used[0] += 1
        copy.start()
        return copy

    def wait(name):
        for copy in pending.pop(name):
            copy.wait()

    def in_blocks(count, step):
        def one(i, carry):
            step(i, span(i, 16))
            return carry

        lax.fori_loop(0, count, one, 0)

    def to_group(moves):
        copies = []
        for k in (2, 1, 3):
            for src, dst in moves(ring(z, k)):
                copies.append(links.go(src, dst, links.zs[k]))
        for src, dst in moves(z):
            copies.append(keep(src, dst))
        return copies

    def to_all(ref, *sets):
        return [links.go(ref, ref, peer) for peers in sets for peer in peers.values()]

    def begin():
        greeted = greet(
            [*links.xs.values(), *links.ys.values(), *links.zs.values(), *links.others.values(), links.partner]
        )
        loads = [keep(qkv_w, own_q), keep(out_w, own_o), keep(up_w, own_u), keep(down_w, own_d)]
        pending["rows"] = [keep(block_in.at[own_64], rows_in), keep(cotangent.at[own_64], upstream_in)]
        pending["branch"] = [keep(cotangent.at[pl.ds(64 * h, 64)], branch.at[z, h]) for h in (0, 1)]
        pending["mom_u"] = [keep(up_m, mom_f.at[0]), keep(up_v, mom_f.at[1])]
        pending["mom_q"] = [keep(qkv_m, mom_q.at[0]), keep(qkv_v, mom_q.at[1])]
        pending["mom_o"] = [keep(out_m, mom_o.at[0]), keep(out_v, mom_o.at[1])]
        small_slots[z] = jnp.zeros((8, 128), F32)
        small_slots[z, 0:4, 0:32] = router_w[...].astype(BF16).astype(F32)
        small_slots[z, 4:6, 0:32] = gains[...].astype(BF16).astype(F32)
        small_slots[z, 6:8, 0:32] = biases[...].astype(BF16).astype(F32)
        small_slots[z] = pltpu.roll(small_slots[z], 32 * z, 1)
        bucket_row = jnp.where(forced_width[...] < 4, forced_width[...], width_route[...])
        token_rows[z] = jnp.zeros((8, 128), F32)
        token_rows[z, 0:1, :] = head_count[...].astype(F32)
        token_rows[z, 1:2, :] = bucket_row.astype(F32)
        token_rows[z, 2:3, :] = jnp.where(slot_index[...] >= 0, 1.0, 0.0)
        gates[z] = jnp.zeros((128, 128), F32)
        gate_part[...] = jnp.zeros_like(gate_part)
        small_sum[...] = jnp.zeros_like(small_sum)
        squares[...] = jnp.zeros_like(squares)
        loads[0].wait()
        for c in range(3):
            for head in range(8):
                at = 256 * c + 128 * (head % 2)
                pack_q[head // 2, :, at : at + 128] = own_q[:, c, head, :].astype(BF16)
        for load in loads[1:]:
            load.wait()

        def pack(i, rows):
            pack_u[rows, :] = own_u[rows, :].astype(BF16)
            pack_d[rows, :] = own_d[rows, :].astype(BF16)
            for head in range(8):
                pack_o[head, rows, :] = own_o[head, rows, :].astype(BF16)

        in_blocks(2, pack)
        wait("rows")
        wait("branch")
        greeted()

    ring_q = Gather(links, (wq, pl.ds(0, 384)), (wq, pl.ds(384, 384)))
    ring_o = Gather(links, (wo, pl.ds(0, 128)), (wo, pl.ds(128, 128)))
    ring_d = Gather(links, (wd, pl.ds(0, 512)), (wd, pl.ds(512, 512)))
    ring_u = Gather(links, (wu, pl.ds(0, 512)), (wu, pl.ds(512, 512)))

    def slices_q():
        pending["q"] = to_group(lambda to: [(pack_q.at[to], wq.at[x, y, own_32, :])])
        pending["small"] = to_all(small_slots.at[z], links.zs)
        pending["tokens"] = to_all(token_rows.at[z], links.zs)

    def slices_o():
        pending["o"] = to_group(
            lambda to: [(pack_o.at[2 * to + h], wo.at[x, y, own_32, pl.ds(128 * h, 128)]) for h in (0, 1)]
        )

    def slices_d():
        pending["d"] = to_group(lambda to: [(pack_d.at[:, span(to, 1024)], wd.at[x, y, own_32, :])])

    def slices_u():
        pending["u"] = to_group(lambda to: [(pack_u.at[:, span(to, 1024)], wu.at[x, y, own_32, :])])

    def small_x():
        wait("small")
        small_grid[x, y] = small_slots[0] + small_slots[1] + small_slots[2] + small_slots[3]
        pending["small"] = to_all(small_grid.at[x, y], links.xs)

    def small_y():
        wait("small")
        pending["small"] = to_all(small_grid.at[:, y], links.ys)

    def small_rows():
        wait("small")
        for p in range(16):
            small[:, 128 * p : 128 * p + 128] = small_grid[p // 4, p % 4]

    def token_columns():
        wait("tokens")
        for row in range(4):
            tokens[row] = as_columns(token_rows[row])

    rows_one, rows_branch = Spread(links, a_one), Spread(links, branch)
    rows_two, rows_back = Spread(links, a_two), Spread(links, hidden_low)

    def norm_one():
        def step(i, rows):
            scaled, inverse = norm_parts(rows_in[rows, :].astype(F32))
            n_one[rows, :] = scaled
            info[0, rows, :] = columns_tile([inverse])

        in_blocks(4, step)

    def rows_one_start():
        def step(i, rows):
            a_one[z, core, rows, :] = (n_one[rows, :] * small[4:5, :] + small[6:7, :]).astype(BF16)

        in_blocks(4, step)
        rows_one.start()

    lane = lax.broadcasted_iota(jnp.int32, (128, 128), 1)
    causal = lax.broadcasted_iota(jnp.int32, (128, 128), 0) >= lane
    scale = 128 ** (-0.5)

    def queries():
        for c in range(3):
            part = wq[:, :, :, 256 * c : 256 * c + 256].reshape(2048, 256)
            wide[:, 256 * c : 256 * c + 256] = dot(a_one[...].reshape(512, 2048), part, (1, 0))

    def spots(index):
        row, head = lax.div(index, 2), lax.rem(index, 2)
        used = jnp.where((core * 8 + z * 2 + head).astype(F32) < tokens[row][:, 0:1], 1.0, 0.0)
        return row, span(row, 128), [span(2 * c + head, 128) for c in range(3)], used

    def attend(first, last):
        turned_sines = jnp.where(lane < 64, -sines[...], sines[...])

        def one(index, carry):
            row, rows, (q_at, k_at, v_at), used = spots(index)

            def rotate(value):
                return value * cosines[...] + turn(value) * turned_sines

            q = (rotate(wide[rows, q_at]) * scale).astype(BF16)
            k = rotate(wide[rows, k_at]).astype(BF16)
            v = wide[rows, v_at].astype(BF16)
            qkv[rows, q_at], qkv[rows, k_at], qkv[rows, v_at] = q, k, v
            scores = jnp.where(causal, dot(q, k, (1, 1)), -1e30)
            powers = jnp.exp(scores - jnp.max(scores, axis=-1, keepdims=True))
            share = powers / jnp.sum(powers, axis=-1, keepdims=True)
            probs[index] = share
            mixed[row, :, :, q_at] = (dot(share.astype(BF16), v, (1, 0)) * used).astype(BF16).reshape(2, 64, 128)
            return carry

        lax.fori_loop(first, last, one, 0)

    merge_one = Merge(links, mixed, wo, set_a, merged)

    def norm_two():
        def step(i, rows):
            value = rows_in[rows, :].astype(F32) + merge_one.rows(rows)
            hidden[rows, :] = value
            scaled, inverse = norm_parts(value)
            n_two[rows, :] = scaled
            low = (scaled * small[5:6, :] + small[7:8, :]).astype(BF16)
            a_two[z, core, rows, :] = low
            low = low.astype(F32)
            logits = [jnp.sum(low * small[b : b + 1, :], axis=-1, keepdims=True) for b in range(4)]
            top = jnp.maximum(jnp.maximum(logits[0], logits[1]), jnp.maximum(logits[2], logits[3]))
            powers = [jnp.exp(logit - top) for logit in logits]
            whole = powers[0] + powers[1] + powers[2] + powers[3]
            chances = [power / whole for power in powers]
            at = span(core * 4 + i, 16)
            own = tokens[z, at, :]
            bucket, kept = own[:, 1:2], own[:, 2:3]
            gate = jnp.zeros_like(bucket)
            for b in range(4):
                gate = jnp.where(bucket == b, chances[b], gate)
            info[1, rows, :] = columns_tile([inverse, gate, *chances])
            gates[z, at, :] = columns_tile([gate * kept])

        in_blocks(4, step)

    def rows_two_start():
        rows_two.start()
        gate_slots[z, core] = gates[z].T[0:8, :]
        pending["gates"] = to_all(gate_slots.at[z, core], links.zs, links.others, {0: links.partner})

    def rows_two_finish():
        rows_two.finish()
        wait("gates")
        for row in range(4):
            gates[row] = as_columns(gate_slots[row, 0] + gate_slots[row, 1])

    def units_back():
        def one(t, carry):
            at = span(t, 256)
            wide[:, at] = dot(branch[...].reshape(512, 2048), wd[:, :, :, at].reshape(2048, 256), (1, 0))
            return carry

        lax.fori_loop(0, 4, one, 0)

    def units():
        quarter = (core * 2 + lax.div(z, 2)).astype(F32)
        used_units = tokens[...].reshape(512, 128)[:, 1:2] >= quarter
        gate_all = gates[...].reshape(512, 128)[:, 0:1]

        def one(t, carry):
            at = span(t, 256)
            up = dot(a_two[...].reshape(512, 2048), wu[:, :, :, at].reshape(2048, 256), (1, 0))
            up = jnp.where(used_units, jnp.maximum(up, 0.0), 0.0)
            low = (up * up).astype(BF16)
            act[:, :, :, at] = low.reshape(4, 2, 64, 256)
            back = wide[:, at]
            up_low[:, :, :, at] = (back * gate_all * 2.0 * up).astype(BF16).reshape(4, 2, 64, 256)
            pairs = (low.astype(F32) * back).astype(BF16)
            gate_part[...] += dot(jnp.ones((8, 256), BF16), pairs, (1, 1))
            return carry

        lax.fori_loop(0, 4, one, 0)
        pending["gate"] = [links.go(gate_part, gate_near, links.partner)]

    merge_u = Merge(links, up_low, wu, set_b, merged_too)
    merge_f = Merge(links, act, wd, set_a, merged)

    def merge_u_out():
        merge_u.cross()
        wait("gate")
        gate_part[...] = gate_part[...] + gate_near[...]
        pending["gate"] = [
            links.go(gate_part.at[:, span(ring(z, k), 128)], gate_far.at[k - 1], links.zs[k]) for k in (1, 2, 3)
        ]
        merge_u.along()

    def merge_u_in():
        wait("gate")
        gate_far[3] = gate_part[:, span(z, 128)] + gate_far[0] + gate_far[1] + gate_far[2]
        info[2] = as_columns(gate_far[3])
        merge_u.arrive()

    def branch_rows():
        def step(i, rows):
            token = lax.rem(i, 8)
            gate = gates[lax.div(i, 8), span(token, 16), :][:, 0:1]
            at = (lax.div(i, 8), lax.div(token, 4), span(lax.rem(token, 4), 16))
            branch[at] = (branch[at].astype(F32) * gate).astype(BF16)

        in_blocks(32, step)

    def outer(left, right, target):
        def one(i, carry):
            part = left[:, :, :, span(i, 256)].reshape(512, 256)
            value = dot(part, right[...].reshape(512, right.shape[-1]), (0, 0)).astype(BF16)
            row, first = lax.div(i, 2), lax.rem(i, 2) * 2
            target[row, first] = value[0:128]
            target[row, first + 1] = value[128:256]
            return carry

        lax.fori_loop(0, 8, one, 0)

    def back_two():
        def step(i, rows):
            at = span(core * 4 + i, 16)
            upstream = upstream_in[rows, :].astype(F32)
            own, tile = tokens[z, at, :], info[1, rows, :]
            bucket, kept = own[:, 1:2], own[:, 2:3]
            inverse, gate = tile[:, 0:1], tile[:, 1:2]
            gate_grad = info[2, at, :][:, 0:1] * kept
            low = a_two[z, core, rows, :].astype(F32)
            grad = merge_u.rows(rows).astype(BF16).astype(F32)
            for b in range(4):
                hot = jnp.where(bucket == b, 1.0, 0.0)
                logit_grad = tile[:, 2 + b : 3 + b] * (hot - gate) * gate_grad
                grad = grad + logit_grad * small[b : b + 1, :]
                small_sum[b] += fold(logit_grad * low)
            scaled = n_two[rows, :]
            small_sum[5] += fold(grad * scaled)
            small_sum[7] += fold(grad)
            back = upstream + norm_back(scaled, inverse, small[5:6, :], grad)
            n_two[rows, :] = back
            hidden_low[z, core, rows, :] = back.astype(BF16)

        in_blocks(4, step)

    def mixed_back():
        d_mixed[...] = dot(hidden_low[...].reshape(512, 2048), wo[...].reshape(2048, 256), (1, 0)).astype(BF16)

    def attend_back():
        def one(index, carry):
            row, rows, (q_at, k_at, v_at), used = spots(index)
            share = probs[index]
            q, k, v = qkv[rows, q_at], qkv[rows, k_at], qkv[rows, v_at]
            grad = (d_mixed[rows, q_at].astype(F32) * used).astype(BF16)
            value_grad = dot(share.astype(BF16), grad, (0, 0))
            share_grad = dot(grad, v, (1, 1))
            inner = jnp.sum(share * share_grad, axis=-1, keepdims=True)
            score_grad = (share * (share_grad - inner)).astype(BF16)

            def rotate_back(value):
                return value * cosines[...] - turn(value * sines[...]) * jnp.where(lane < 64, -1.0, 1.0)

            def put(at, value):
                d_qkv[row, :, :, at] = value.astype(BF16).reshape(2, 64, 128)

            put(q_at, rotate_back(dot(score_grad, k, (1, 0)) * scale))
            put(k_at, rotate_back(dot(score_grad, q, (0, 0))))
            put(v_at, value_grad)
            return carry

        lax.fori_loop(0, 8, one, 0)

    merge_q = Merge(links, d_qkv, wq, set_b, merged_too)
    sums_u = Scatter(links, (wu, pl.ds(0, 512)), (wu, pl.ds(512, 512)), buffers[0:8])
    sums_d = Scatter(links, (wd, pl.ds(0, 512)), (wd, pl.ds(512, 512)), buffers[8:16])
    sums_q = Scatter(links, (wq, pl.ds(0, 384)), (wq, pl.ds(384, 384)), buffers[16:24])
    sums_o = Scatter(links, (wo, pl.ds(0, 128)), (wo, pl.ds(128, 128)), buffers[24:32])

    def output_rows():
        merge_f.arrive()

        def step(i, rows):
            kept = tokens[z, span(core * 4 + i, 16), :][:, 2:3]
            produced = merge_f.rows(rows).astype(BF16).astype(F32) * kept
            out_rows[rows, :] = (hidden[rows, :] + info[1, rows, :][:, 1:2] * produced).astype(BF16)

        in_blocks(4, step)
        here = block_out.at[own_64]
        pending["output"] = [keep(out_rows, here), links.go(out_rows, here, links.partner)]

    def back_one():
        merge_q.arrive()

        def step(i, rows):
            grad = merge_q.rows(rows)
            scaled, inverse = n_one[rows, :], info[0, rows, :][:, 0:1]
            small_sum[4] += fold(grad * scaled)
            small_sum[6] += fold(grad)
            grad_rows[rows, :] = n_two[rows, :] + norm_back(scaled, inverse, small[4:5, :], grad)

        in_blocks(4, step)
        for r in range(8):
            small[r : r + 1, :] = jnp.sum(small_sum[r], axis=0, keepdims=True)
        pending["small"] = [links.go(small, small_near, links.partner)]
        here = input_grad.at[own_64]
        pending["input"] = [keep(grad_rows, here), links.go(grad_rows, here, links.partner)]

    def small_to_x():
        wait("small")
        small[...] = small[...] + small_near[...]
        pending["small"] = [
            links.go(small.at[:, span(ring(x, k), 512)], sx_in.at[k], links.xs[k]) for k in (1, 2, 3)
        ]

    def small_to_y():
        wait("small")
        sx_in[0] = small[:, span(x, 512)] + sx_in[1] + sx_in[2] + sx_in[3]
        pending["small"] = [
            links.go(sx_in.at[0, :, span(ring(y, k), 128)], sy_in.at[k], links.ys[k]) for k in (1, 2, 3)
        ]

    def small_to_z():
        wait("small")
        sz_in[z] = sx_in[0, :, span(y, 128)] + sy_in[1] + sy_in[2] + sy_in[3]
        pending["small"] = to_all(sz_in.at[z], links.zs)

    def small_done():
        wait("small")
        small_grad[...] = pltpu.roll(sz_in[0] + sz_in[1] + sz_in[2] + sz_in[3], 128 - 32 * z, 1)
        _, _, update = moment_step(
            router_w[...], small_grad[0:4, 0:32], router_m[...], router_v[...], DECAY_RATE
        )
        squares[8, 0:4, 0:32] = 0.5 * router_w[...] * router_w[...]
        squares[9, 0:4, 0:32] = 0.5 * update * update

    def owners_u():
        pending["own_u"] = to_group(lambda to: [(wu.at[x, y, span(to, 32), :], up_grad.at[:, span(z, 1024)])])

    def owners_d():
        pending["own_d"] = to_group(lambda to: [(wd.at[x, y, span(to, 32), :], down_grad.at[:, span(z, 1024)])])

    def owners_o():
        pending["own_o"] = to_group(
            lambda to: [
                (wo.at[x, y, span(to, 32), pl.ds(128 * h, 128)], out_grad.at[2 * z + h]) for h in (0, 1)
            ]
        )

    def owners_q():
        pending["own_q"] = to_group(lambda to: [(wq.at[x, y, span(to, 32), :], got_q.at[z])])

    def squares_wide(number, weights, grads):
        def one(i, carry):
            rows, columns = span(lax.div(i, 4), 16), span(lax.rem(i, 4), 1024)
            weight = weights[rows, columns]
            _, _, update = moment_step(
                weight, grads[rows, columns].astype(F32), mom_f[0, rows, columns], mom_f[1, rows, columns], DECAY_RATE
            )
            squares[2 * number] += fold_lanes(weight * weight)
            squares[2 * number + 1] += fold_lanes(update * update)
            return carry

        lax.fori_loop(0, 8, one, 0)

    def squares_u():
        wait("own_u")
        wait("mom_u")
        squares_wide(2, own_u, up_grad)
        pending["mom_d"] = [keep(down_m, mom_f.at[0]), keep(down_v, mom_f.at[1])]

    def squares_d():
        wait("own_d")
        wait("mom_d")
        squares_wide(3, own_d, down_grad)

    def squares_o():
        wait("own_o")
        wait("mom_o")

        def one(head, carry):
            weight = own_o[head]
            _, _, update = moment_step(
                weight, out_grad[head].astype(F32), mom_o[0, head], mom_o[1, head], DECAY_RATE
            )
            squares[2] += fold_lanes(weight * weight)
            squares[3] += fold_lanes(update * update)
            return carry

        lax.fori_loop(0, 8, one, 0)

    def squares_q():
        wait("own_q")
        wait("mom_q")
        for c in range(3):
            for head in range(8):
                at = 256 * c + 128 * (head % 2)
                qkv_grad[:, c, head, :] = got_q[head // 2, :, at : at + 128].astype(F32)

        def one(i, carry):
            rows = pl.ds(i * 4, 4)
            weight = own_q[rows]
            _, _, update = moment_step(weight, qkv_grad[rows], mom_q[0, rows], mom_q[1, rows], DECAY_RATE)
            squares[0] += jnp.sum(jnp.sum(weight * weight, axis=0), axis=0)
            squares[1] += jnp.sum(jnp.sum(update * update, axis=0), axis=0)
            return carry

        lax.fori_loop(0, 8, one, 0)

    def totals():
        lanes = lax.broadcasted_iota(jnp.int32, (8, 128), 1)
        tile = jnp.zeros((8, 128), F32)
        for number in range(10):
            value = jnp.sum(jnp.sum(squares[number], axis=0, keepdims=True), axis=1, keepdims=True)
            tile = jnp.where(lanes == number // 2 + 5 * (number % 2), value, tile)
        here = 4 * core + z
        sets = ((links.zs, links.others, {0: links.partner}), (links.ys,), (links.xs,))
        for axis, (me, peers) in enumerate(zip((here, y, x), sets)):
            slots[axis, me] = tile
            for copy in to_all(slots.at[axis, me], *peers):
                copy.wait()
            tile = slots[axis, 0]
            for k in range(1, 8 if axis == 0 else 4):
                tile = tile + slots[axis, k]
        norms[...] = tile

    begin()
    slices_q()
    small_x()
    wait("q")
    ring_q.advance()
    slices_o()
    wait("o")
    ring_o.advance()
    slices_u()
    rows_branch.start(own=False)
    slices_d()
    ring_q.advance()
    norm_one()
    small_y()
    ring_o.advance()
    ring_q.advance()
    small_rows()
    rows_one_start()
    token_columns()
    wait("d")
    ring_d.advance()
    ring_q.advance()
    rows_one.relay()
    ring_d.advance()
    ring_o.advance()
    ring_q.advance()
    wait("u")
    ring_u.advance()
    rows_one.finish()
    rows_branch.relay()
    queries()
    ring_o.advance()
    ring_d.advance()
    attend(0, 4)
    ring_u.advance()
    attend(4, 8)
    ring_o.advance()
    merge_one.cross()
    merge_one.along()
    ring_u.advance()
    merge_one.arrive()
    ring_d.advance()
    norm_two()
    rows_two_start()
    rows_branch.finish()
    ring_u.advance()
    rows_two.relay()
    ring_d.advance()
    units_back()
    rows_two_finish()
    ring_u.advance()
    units()
    merge_u_out()
    outer(a_two, up_low, wu)
    sums_u.advance()
    merge_f.cross()
    merge_f.along(leave=False)
    merge_u_in()
    back_two()
    rows_back.start()
    branch_rows()
    outer(branch, act, wd)
    sums_d.advance()
    rows_back.relay()
    rows_back.finish()
    mixed_back()
    sums_u.advance()
    attend_back()
    sums_d.advance()
    merge_q.cross()
    merge_q.along()
    sums_u.advance()
    outer(a_one, d_qkv, wq)
    sums_q.advance()
    back_one()
    merge_f.leave()
    sums_d.advance()
    outer(hidden_low, mixed, wo)
    small_to_x()
    sums_q.advance()
    sums_u.advance()
    sums_u.advance()
    sums_o.advance()
    sums_d.advance()
    small_to_y()
    sums_q.advance()
    owners_u()
    sums_o.advance()
    sums_d.advance()
    owners_d()
    sums_q.advance()
    sums_o.advance()
    small_to_z()
    output_rows()
    sums_q.advance()
    owners_q()
    small_done()
    sums_o.advance()
    squares_u()
    sums_o.advance()
    owners_o()
    squares_d()
    squares_q()
    squares_o()
    totals()
    wait("output")
    wait("input")


def layer(*operands):
    def vmem(*shape, kind=BF16):
        return pltpu.VMEM(shape, kind)

    def merge_buffers():
        return [vmem(TILES, 4, 64, TILE), vmem(TILES, 4, 64, TILE), vmem(3, TILES, 64, TILE)]

    def sum_buffers(width):
        return [
            vmem(2, 4, 64, width), vmem(2, 4, 128, width), vmem(2, 64, width), vmem(2, 128, width),
        ] * 2

    rows, rows_low, tokens = vmem(64, 2048, kind=F32), vmem(64, 2048), vmem(4, 2, 64, 2048)
    tile = vmem(4, 8, 128, kind=F32)
    return pl.pallas_call(
        layer_kernel,
        out_shape=(
            jax.ShapeDtypeStruct((128, 2048), BF16),
            jax.ShapeDtypeStruct((128, 2048), F32),
            jax.ShapeDtypeStruct((32, 3, 8, 128), F32),
            jax.ShapeDtypeStruct((8, 32, 128), BF16),
            jax.ShapeDtypeStruct((32, 4096), BF16),
            jax.ShapeDtypeStruct((32, 4096), BF16),
            jax.ShapeDtypeStruct((8, 128), F32),
            jax.ShapeDtypeStruct((8, 128), F32),
        ),
        in_specs=[ANY] * 14 + [VMEM] * 11,
        out_specs=(ANY, ANY) + (VMEM,) * 6,
        scratch_shapes=[
            vmem(32, 3, 8, 128, kind=F32), vmem(8, 32, 128, kind=F32), vmem(32, 4096, kind=F32),
            vmem(32, 4096, kind=F32),
            vmem(4, 32, 768), vmem(8, 32, 128), vmem(32, 4096), vmem(32, 4096),
            vmem(2, 32, 3, 8, 128, kind=F32), vmem(2, 8, 32, 128, kind=F32), vmem(2, 32, 4096, kind=F32),
            vmem(4, 4, 128, 768), vmem(4, 4, 128, 256), vmem(4, 4, 128, 1024), vmem(4, 4, 128, 1024),
            tile, vmem(4, 4, 8, 128, kind=F32), vmem(8, 2048, kind=F32), vmem(8, 2048, kind=F32),
            tile, vmem(4, 128, 128, kind=F32), vmem(4, 2, 8, 128, kind=F32), vmem(4, 128, 128, kind=F32),
            vmem(3, 128, 128, kind=F32),
            tokens, tokens, tokens, tokens,
            rows_low, rows_low, rows, rows, rows, rows, rows, rows_low, rows,
            vmem(512, 1024, kind=F32), vmem(512, 768), vmem(8, 128, 128, kind=F32),
            vmem(4, 2, 64, 256), vmem(512, 256), vmem(4, 2, 64, 768), vmem(4, 2, 64, 1024), vmem(4, 2, 64, 1024),
            *merge_buffers(), *merge_buffers(), vmem(256, TILE, kind=F32),
            vmem(8, 512, kind=F32), vmem(8, 512, kind=F32), tile,
            vmem(8, 8, 2048, kind=F32), vmem(4, 8, 512, kind=F32), tile, tile,
            vmem(4, 32, 768), vmem(10, 8, 128, kind=F32), vmem(3, 8, 8, 128, kind=F32),
            *sum_buffers(512), *sum_buffers(512), *sum_buffers(384), *sum_buffers(128),
            DMA((LOCAL_COPIES,)), DMA((LINK_COPIES,)), DMA((LINK_COPIES,)),
        ],
        compiler_params=pltpu.CompilerParams(
            collective_id=0, has_side_effects=True, vmem_limit_bytes=63 * 2**20
        ),
        name="layer",
    )(*operands)


def renew_kernel(norms, small_grad, gains, biases, norm_m, norm_v, *refs):
    ins, outs = refs[:20], refs[20:]
    sums = norms[0:1, :]
    for index in range(5):
        weight, grad, m, v = (ref[...] for ref in ins[4 * index : 4 * index + 4])
        grad = grad[0:4, 0:32] if index == 4 else grad.astype(F32)
        first, second, update = moment_step(weight, grad, m, v, DECAY_RATE)
        ratio = LEARN_RATE * (jnp.sqrt(sums[:, index : index + 1]) / jnp.sqrt(sums[:, index + 5 : index + 6]))
        ratio = ratio.reshape((1,) * weight.ndim)
        new = weight - ratio * update
        for ref, value in zip(outs[5 * index : 5 * index + 5], (grad, first, second, new, new.astype(BF16))):
            ref[...] = value
    grad = small_grad[4:8, 0:32]
    master = jnp.concatenate([gains[...], biases[...]], axis=0)
    first, second, update = moment_step(master, grad, norm_m[...], norm_v[...], 0.0)
    new = master - NORM_RATE * update
    for ref, value in zip(outs[25:30], (grad, first, second, new, new.astype(BF16))):
        ref[...] = value
    row = lax.broadcasted_iota(jnp.int32, (8, 128), 0)
    lane = lax.broadcasted_iota(jnp.int32, (8, 128), 1)
    tile = jnp.zeros((8, 128), F32)
    for index in range(10):
        here = (row == index % 5) & (lane == index // 5)
        tile = jnp.where(here, jnp.sqrt(sums[:, index : index + 1]), tile)
    outs[30][...] = tile[0:5, 0:2]


def renew(norms, small_grad, gains, biases, norm_m, norm_v, *matrices):
    steps = 4

    def whole(shape):
        return pl.BlockSpec(shape, lambda i: (0,) * len(shape))

    blocks = (
        pl.BlockSpec((32 // steps, 3, 8, 128), lambda i: (i, 0, 0, 0)),
        pl.BlockSpec((8 // steps, 32, 128), lambda i: (i, 0, 0)),
        pl.BlockSpec((32, 4096 // steps), lambda i: (0, i)),
        pl.BlockSpec((32, 4096 // steps), lambda i: (0, i)),
        whole((4, 32)),
    )
    shapes = ((32, 3, 8, 128), (8, 32, 128), (32, 4096), (32, 4096), (4, 32), (4, 32))
    in_specs = [whole((8, 128)), whole((8, 128)), whole((2, 32)), whole((2, 32)), whole((4, 32)), whole((4, 32))]
    out_specs, out_shape = [], []
    for index, block in enumerate(blocks):
        in_specs += [block, whole((8, 128)) if index == 4 else block, block, block]
    for block, shape in zip((*blocks, whole((4, 32))), shapes):
        out_specs += [block] * 5
        out_shape += [jax.ShapeDtypeStruct(shape, kind) for kind in (F32, F32, F32, F32, BF16)]
    out_specs.append(whole((5, 2)))
    out_shape.append(jax.ShapeDtypeStruct((5, 2), F32))
    return pl.pallas_call(
        renew_kernel,
        grid=(steps,),
        in_specs=in_specs,
        out_specs=out_specs,
        out_shape=out_shape,
        compiler_params=pltpu.CompilerParams(vmem_limit_bytes=63 * 2**20),
        name="renew",
    )(norms, small_grad, gains, biases, norm_m, norm_v, *matrices)


def rotary_tables(length, size):
    half_size = size // 2
    frequency = ROPE_BASE ** (-(np.arange(half_size) * 2.0 / size))
    angles = np.arange(length)[:, None] * frequency[None, :]
    cosine_table = np.concatenate([np.cos(angles), np.cos(angles)], axis=-1)
    sine_table = np.concatenate([np.sin(angles), np.sin(angles)], axis=-1)
    return (cosine_table.astype(np.float32), sine_table.astype(np.float32))


def local(
    block_input,
    cotangent,
    head_count,
    width_route,
    forced_width,
    slot_index,
    qkv_weight,
    out_weight,
    up_weight,
    down_weight,
    router_weight,
    norm_gains,
    norm_biases,
    qkv_first,
    qkv_second,
    out_first,
    out_second,
    up_first,
    up_second,
    down_first,
    down_second,
    router_first,
    router_second,
    norm_first,
    norm_second,
):
    def turned(value):
        return value.transpose(0, 2, 1)

    out = turned(out_weight), turned(out_first), turned(out_second)
    down = down_weight.T, down_first.T, down_second.T
    router = router_weight.T, router_first.T, router_second.T
    block_output, input_grad, *grads, small_grad, norms = layer(
        qkv_weight, out[0], up_weight, down[0],
        qkv_first, qkv_second, *out[1:], up_first, up_second, *down[1:],
        block_input, cotangent, *router, norm_gains, norm_biases,
        *(value.reshape(1, -1) for value in (head_count, width_route, forced_width, slot_index)),
        *rotary_tables(128, 128),
    )
    *results, lamb_norms = renew(
        norms, small_grad, norm_gains, norm_biases, norm_first, norm_second,
        qkv_weight, grads[0], qkv_first, qkv_second,
        out[0], grads[1], *out[1:],
        up_weight, grads[2], up_first, up_second,
        down[0], grads[3], *down[1:],
        router[0], small_grad, *router[1:],
    )
    kinds = []
    for kind in range(5):
        qkv, out, up, down, router, norm = (results[5 * index + kind] for index in range(6))
        kinds += [qkv, turned(out), up, down.T, router.T, norm]
    return (block_output, input_grad, *kinds, lamb_norms)


def solution(mesh):
    qkv, out = P("dp", None, "mp", None), P("mp", None, "dp")
    up, down, router, norms = P("dp", "mp"), P("mp", "dp"), P("dp", None), P(None, "dp")
    rows, tokens = P("dp", None), P("dp")
    matrices = (qkv, out, up, down, router)
    return jax.shard_map(
        local,
        mesh=mesh,
        in_specs=(
            rows, rows, tokens, tokens, tokens, tokens,
            *matrices, norms, norms,
            qkv, qkv, out, out, up, up, down, down, router, router, norms, norms,
        ),
        out_specs=(rows, rows, *((*matrices, norms) * 5), P()),
        check_vma=False,
    )
```

```python
import jax
import jax.numpy as jnp
import numpy as np
from jax import lax
from jax.experimental import pallas as pl
from jax.experimental.pallas import tpu as pltpu
from jax.sharding import PartitionSpec as P

STEP = 5

BETA_ONE = 0.5
BETA_TWO = 0.5
ADAM_EPS = 1e-06
DECAY_RATE = 0.01
LEARN_RATE = 0.5
NORM_RATE = 0.1
NORM_EPS = 1e-05
ROPE_BASE = 10000.0

MESH = pl.DeviceIdType.MESH
BF16 = jnp.bfloat16
F32 = jnp.float32
VMEM = pl.BlockSpec(memory_space=pltpu.VMEM)
ANY = pl.BlockSpec(memory_space=pl.ANY)
DMA = pltpu.SemaphoreType.DMA
ALL = slice(None)
LOW, HIGH = pl.ds(0, 64), pl.ds(64, 64)


def place():
    index = lax.axis_index("dp")
    return lax.div(index, 16), lax.rem(lax.div(index, 4), 4), lax.rem(index, 4), lax.axis_index("mp")


def ring(value, step):
    return lax.rem(value + (step + 4), 4)


def device(x, y, z, core):
    return (x * 16 + y * 4 + z, core)


def greet(peers):
    barrier = pltpu.get_barrier_semaphore()
    for peer in peers:
        pl.semaphore_signal(barrier, inc=1, device_id=peer, device_id_type=MESH)
    return lambda: pl.semaphore_wait(barrier, len(peers))


def send(src, dst, send_sem, recv_sem, peer):
    copy = pltpu.make_async_remote_copy(
        src_ref=src, dst_ref=dst, send_sem=send_sem, recv_sem=recv_sem, device_id=peer, device_id_type=MESH
    )
    copy.start()
    return copy


def span(index, size):
    return pl.ds(pl.multiple_of(index * size, size), size)


def dot(left, right, dims):
    return lax.dot_general(left, right, ((dims[:1], dims[1:]), ((), ())), preferred_element_type=F32)


class Links:
    def __init__(self, send_sems, recv_sems):
        self.x, self.y, self.z, self.core = x, y, z, core = place()
        self.xs = {k: device(ring(x, k), y, z, core) for k in (1, 2, 3)}
        self.ys = {k: device(x, ring(y, k), z, core) for k in (1, 2, 3)}
        self.zs = {k: device(x, y, ring(z, k), core) for k in (1, 2, 3)}
        self.others = {k: device(x, y, ring(z, k), 1 - core) for k in (1, 2, 3)}
        self.partner = device(x, y, z, 1 - core)
        self.send_sems, self.recv_sems, self.used = send_sems, recv_sems, 0

    def go(self, src, dst, peer):
        number = self.used
        self.used += 1
        return send(src, dst, self.send_sems.at[number], self.recv_sems.at[number], peer)

    def together(self, moves, whole):
        number = self.used
        self.used += 1
        sems = self.send_sems.at[number], self.recv_sems.at[number]
        for src, dst, peer in moves:
            send(src, dst, *sems, peer)
        return Bundle(whole, *sems)


class Bundle:
    def __init__(self, whole, *sems):
        self.whole, self.sems = whole, sems

    def wait(self):
        for sem in self.sems:
            pltpu.make_async_copy(self.whole, self.whole, sem).wait()


class Gather:
    def __init__(self, links, first, second):
        self.links, self.parts, self.number, self.copies = links, (first, second), 0, []

    def advance(self):
        for copy in self.copies:
            copy.wait()
        x, y = self.links.x, self.links.y
        xp, xm, yp, ym = self.links.xs[1], self.links.xs[3], self.links.ys[1], self.links.ys[3]
        xb, xa, yb, ya = ring(x, -1), ring(x, 1), ring(y, -1), ring(y, 1)
        moves = {
            0: (((x, y, ALL), xp), ((x, y, ALL), xm), ((x, y, ALL), yp), ((x, y, ALL), ym)),
            1: (((xb, y, LOW), xp), ((xa, y, HIGH), xm), ((x, yb, LOW), yp), ((x, ya, HIGH), ym)),
            2: (((ALL, y, ALL), yp), ((ALL, y, ALL), ym), ((x, ALL, ALL), xp), ((x, ALL, ALL), xm)),
            3: (((ALL, yb, LOW), yp), ((ALL, ya, HIGH), ym), ((xb, ALL, LOW), xp), ((xa, ALL, HIGH), xm)),
        }.get(self.number, ())
        if moves:
            pairs = [(self.parts[index // 2][0].at[where + (self.parts[index // 2][1],)], peer)
                     for index, (where, peer) in enumerate(moves)]
            ref, columns = self.parts[0]
            whole = (
                ref.at[0, :, :, columns], ref.at[0, pl.ds(0, 2), :, columns],
                ref.at[:, :, :, columns], ref.at[pl.ds(0, 2), :, :, columns],
            )[self.number]
            self.copies = [self.links.together([(block, block, peer) for block, peer in pairs], whole)]
        else:
            self.copies = []
        self.number += 1


def add_into(ref, blocks, columns, sources, row, count):
    steps = count // 16

    def one(index, carry):
        number = lax.div(index, steps)
        step = pl.multiple_of(lax.rem(index, steps) * 16, 16)
        to = blocks[1](number) + (pl.ds(row + step, 16), columns)
        here = ref[to].astype(F32)
        for source, first_row in sources:
            place_in = ((number,) if blocks[0] > 1 else ()) + (pl.ds(first_row + step, 16), ALL)
            here = here + source[place_in].astype(F32)
        ref[to] = here.astype(BF16)
        return carry

    lax.fori_loop(0, blocks[0] * steps, one, 0)


class Scatter:
    def __init__(self, links, first, second, buffers):
        self.links, self.parts = links, (first, second)
        self.buffers = (buffers[:4], buffers[4:])
        self.number, self.halves, self.rest = 0, [], []

    def lanes(self, phase):
        x, y = self.links.x, self.links.y
        found = []
        for part in (0, 1):
            ref, columns = self.parts[part]
            along_y = part == phase
            peers = self.links.ys if along_y else self.links.xs
            if phase == 0 and along_y:
                where, count, each = (lambda k: (ALL, ring(y, k))), 4, (lambda k: lambda i: (i, ring(y, k)))
            elif phase == 0:
                where, count, each = (lambda k: (ring(x, k), ALL)), 4, (lambda k: lambda i: (ring(x, k), i))
            elif along_y:
                where, count, each = (lambda k: (x, ring(y, k))), 1, (lambda k: lambda i: (x, ring(y, k)))
            else:
                where, count, each = (lambda k: (ring(x, k), y)), 1, (lambda k: lambda i: (ring(x, k), y))
            one, two = self.buffers[part][2 * phase : 2 * phase + 2]
            found.append((ref, columns, where, count, each, peers, one, two))
        return found

    def begin(self, phase):
        self.halves, self.rest = [], []
        links = self.links
        for ref, columns, where, count, each, peers, one, two in self.lanes(phase):
            self.halves.append(links.go(ref.at[where(2) + (LOW, columns)], one.at[0], peers[1]))
            self.halves.append(links.go(ref.at[where(2) + (HIGH, columns)], one.at[1], peers[3]))
        moves = []
        for ref, columns, where, count, each, peers, one, two in self.lanes(phase):
            lead = (ALL,) if count > 1 else ()
            moves.append((ref.at[where(1) + (HIGH, columns)], two.at[(0,) + lead + (HIGH,)], peers[1]))
            moves.append((ref.at[where(-1) + (LOW, columns)], two.at[(1,) + lead + (LOW,)], peers[3]))
        self.rest.append(links.together(moves, self.buffers[0][2 * phase + 1]))

    def middle(self, phase):
        lanes, self.last = self.lanes(phase), []
        for side in (0, 1):
            for part in (0, 1):
                ref, columns, where, count, each, peers, one, two = lanes[part]
                lead = (ALL,) if count > 1 else ()
                step, rows, row = ((1, LOW, 0), (-1, HIGH, 64))[side]
                self.halves[2 * part + side].wait()
                add_into(ref, (count, each(step)), columns, [(one.at[side], 0)], row, 64)
                self.last.append(
                    self.links.go(
                        ref.at[where(step) + (rows, columns)], two.at[(side,) + lead + (rows,)], peers[(1, 3)[side]]
                    )
                )

    def end(self, phase):
        for copy in self.rest + self.last:
            copy.wait()
        for ref, columns, where, count, each, peers, one, two in self.lanes(phase):
            add_into(ref, (count, each(0)), columns, [(two.at[0], 0), (two.at[1], 0)], 0, 128)

    def advance(self):
        if self.number == 0:
            self.begin(0)
        elif self.number == 1:
            self.middle(0)
        elif self.number == 2:
            self.end(0)
            self.begin(1)
        elif self.number == 3:
            self.middle(1)
        elif self.number == 4:
            self.end(1)
        self.number += 1


class Spread:
    def __init__(self, links, ref):
        self.links, self.ref = links, ref

    def start(self, own=True):
        links = self.links
        here = self.ref.at[links.z, links.core]
        self.passed = [links.go(here, here, links.partner)] if own else []
        self.flying = [links.go(here, here, links.zs[k]) for k in (1, 3)]

    def relay(self):
        links = self.links
        self.far = []
        for side, k, rows in ((0, 1, pl.ds(0, 32)), (1, 3, pl.ds(32, 32))):
            self.flying[side].wait_recv()
            block = self.ref.at[ring(links.z, -k), links.core]
            half = block.at[rows]
            self.far.append(links.go(half, half, links.zs[k]))
            self.passed.append(links.go(block, block, links.partner))

    def finish(self):
        links = self.links
        for copy in self.far:
            copy.wait_recv()
        block = self.ref.at[ring(links.z, 2), links.core]
        self.passed.append(links.go(block, block, links.partner))
        for copy in self.flying + self.far:
            copy.wait_send()
        for copy in self.passed:
            copy.wait()


TILES, TILE = 4, 512


class Merge:
    def __init__(self, links, left, weights, buffers, out):
        self.links, self.left, self.weights, self.out = links, left, weights, out
        self.near, self.near_in, self.far_in, self.tmp = buffers
        self.crossing, self.flying = [], []

    def tile(self, half, j):
        rows = self.weights[j]
        left = self.left[:, half]
        return dot(left.reshape(256, left.shape[-1]), rows.reshape(TILE, rows.shape[-1]), (1, 1))

    def cross(self):
        for j in range(TILES):
            self.near[j] = self.tile(1 - self.links.core, j).astype(BF16).reshape(4, 64, TILE)
            self.crossing.append(self.links.go(self.near.at[j], self.near_in.at[j], self.links.partner))

    def along(self, leave=True):
        for j in range(TILES):
            value = self.tile(self.links.core, j)
            self.crossing[j].wait()
            value = value + self.near_in[j].astype(F32).reshape(256, TILE)
            self.tmp[0:256, 0:TILE] = value
            self.near[j] = value.astype(BF16).reshape(4, 64, TILE)
            if leave:
                self.leave(j)
            self.out[:, TILE * j : TILE * j + TILE] = self.tmp[span(self.links.z, 64), 0:TILE]

    def leave(self, j=ALL):
        links = self.links
        whole = self.far_in.at[:, j]
        moves = [(self.near.at[j, ring(links.z, k)], self.far_in.at[k - 1, j], links.zs[k]) for k in (2, 1, 3)]
        self.flying.append(links.together(moves, whole))

    def arrive(self):
        for copy in self.flying:
            copy.wait()

    def rows(self, rows):
        value = self.out[rows, :]
        for k in range(3):
            parts = [self.far_in[k, j, rows, :] for j in range(TILES)]
            value = value + jnp.concatenate(parts, axis=1).astype(F32)
        return value


def norm_parts(value):
    centre = value - jnp.mean(value, axis=-1, keepdims=True)
    inverse = lax.rsqrt(jnp.mean(centre * centre, axis=-1, keepdims=True) + NORM_EPS)
    return centre * inverse, inverse


def norm_back(scaled, inverse, gain_row, upstream):
    dscaled = upstream * gain_row
    inner = (
        dscaled
        - jnp.mean(dscaled, axis=-1, keepdims=True)
        - scaled * jnp.mean(dscaled * scaled, axis=-1, keepdims=True)
    )
    return inner * inverse


def fold(value):
    return value[0:8, :] + value[8:16, :]


def fold_lanes(value):
    total = None
    for row in range(0, value.shape[0], 8):
        for lane in range(0, value.shape[1], 128):
            part = value[row : row + 8, lane : lane + 128]
            total = part if total is None else total + part
    return total


def columns_tile(columns):
    lane = lax.broadcasted_iota(jnp.int32, (16, 128), 1)
    tile = jnp.zeros((16, 128), F32)
    for index, column in enumerate(columns):
        tile = jnp.where(lane == index, column, tile)
    return tile


def as_columns(rows):
    return jnp.concatenate([rows, jnp.zeros((120, 128), F32)], axis=0).T


def turn(value):
    return pltpu.roll(value, 64, 1)


def moment_step(weight, gradient, first_moment, second_moment, decay_rate):
    first_moment = BETA_ONE * first_moment + (1.0 - BETA_ONE) * gradient
    second_moment = BETA_TWO * second_moment + (1.0 - BETA_TWO) * gradient * gradient
    one, two = 1.0 / (1.0 - BETA_ONE**STEP), 1.0 / (1.0 - BETA_TWO**STEP)
    update = (first_moment * one) / (jnp.sqrt(second_moment * two) + ADAM_EPS) + decay_rate * weight
    return (first_moment, second_moment, update)


LINK_COPIES = 194
LOCAL_COPIES = 43


def layer_kernel(
    qkv_w, out_w, up_w, down_w, qkv_m, qkv_v, out_m, out_v, up_m, up_v, down_m, down_v, block_in, cotangent,
    router_w, router_m, router_v, gains, biases, head_count, width_route, forced_width, slot_index, cosines, sines,
    block_out, input_grad, qkv_grad, out_grad, up_grad, down_grad, small_grad, norms,
    own_q, own_o, own_u, own_d, pack_q, pack_o, pack_u, pack_d, mom_q, mom_o,
    wq, wo, wu, wd, grad_q, grad_d, small_slots, small_grid, small, small_near,
    token_rows, tokens, gate_slots, gates, info,
    a_one, a_two, branch, hidden_low,
    rows_in, upstream_in, hidden, n_one, n_two, merged, merged_too, out_rows,
    wide, qkv, probs, mixed, d_mixed, d_qkv, act, act_gated, up_low,
    near_a, near_in_a, far_in_a, near_b, near_in_b, far_in_b,
    gate_part, gate_near, gate_far, small_sum, sx_in, sy_in, sz_in, squares, slots,
    *rest,
):
    buffers, (local_sems, send_sems, recv_sems) = rest[:-3], rest[-3:]
    links = Links(send_sems, recv_sems)
    x, y, z, core = links.x, links.y, links.z, links.core
    own_32, own_64 = span(z, 32), span(core, 64)
    set_a = (near_a, near_in_a, far_in_a, wide)
    set_b = (near_b, near_in_b, far_in_b, wide)
    local_used, pending = [0], {}

    def keep(src, dst):
        copy = pltpu.make_async_copy(src, dst, local_sems.at[local_used[0]])
        local_used[0] += 1
        copy.start()
        return copy

    def wait(name):
        for copy in pending.pop(name):
            copy.wait()

    def in_blocks(count, step):
        def one(i, carry):
            step(i, span(i, 16))
            return carry

        lax.fori_loop(0, count, one, 0)

    def to_group(moves):
        copies = []
        for k in (2, 1, 3):
            for src, dst in moves(ring(z, k)):
                copies.append(links.go(src, dst, links.zs[k]))
        for src, dst in moves(z):
            copies.append(keep(src, dst))
        return copies

    def to_all(here, whole, *sets):
        return [links.together([(here, here, peer) for peers in sets for peer in peers.values()], whole)]

    def begin():
        greeted = greet(
            [*links.xs.values(), *links.ys.values(), *links.zs.values(), *links.others.values(), links.partner]
        )
        loads = [keep(qkv_w, own_q), keep(out_w, own_o), keep(up_w, own_u), keep(down_w, own_d)]
        pending["rows"] = [keep(block_in.at[own_64], rows_in), keep(cotangent.at[own_64], upstream_in)]
        pending["branch"] = [keep(cotangent.at[pl.ds(64 * h, 64)], branch.at[z, h]) for h in (0, 1)]
        pending["mom_q"] = [keep(qkv_m, mom_q.at[0]), keep(qkv_v, mom_q.at[1])]
        pending["mom_o"] = [keep(out_m, mom_o.at[0]), keep(out_v, mom_o.at[1])]
        small_slots[z] = jnp.zeros((8, 128), F32)
        small_slots[z, 0:4, 0:32] = router_w[...].astype(BF16).astype(F32)
        small_slots[z, 4:6, 0:32] = gains[...].astype(BF16).astype(F32)
        small_slots[z, 6:8, 0:32] = biases[...].astype(BF16).astype(F32)
        small_slots[z] = pltpu.roll(small_slots[z], 32 * z, 1)
        bucket_row = jnp.where(forced_width[...] < 4, forced_width[...], width_route[...])
        token_rows[z] = jnp.zeros((8, 128), F32)
        token_rows[z, 0:1, :] = head_count[...].astype(F32)
        token_rows[z, 1:2, :] = bucket_row.astype(F32)
        token_rows[z, 2:3, :] = jnp.where(slot_index[...] >= 0, 1.0, 0.0)
        gates[z] = jnp.zeros((128, 128), F32)
        gate_part[...] = jnp.zeros_like(gate_part)
        small_sum[...] = jnp.zeros_like(small_sum)
        squares[...] = jnp.zeros_like(squares)
        loads[0].wait()
        for c in range(3):
            for head in range(8):
                at = 256 * c + 128 * (head % 2)
                pack_q[head // 2, :, at : at + 128] = own_q[:, c, head, :].astype(BF16)
        for load in loads[1:]:
            load.wait()

        def pack(i, rows):
            pack_u[rows, :] = own_u[rows, :].astype(BF16)
            pack_d[rows, :] = own_d[rows, :].astype(BF16)
            for head in range(8):
                pack_o[head, rows, :] = own_o[head, rows, :].astype(BF16)

        in_blocks(2, pack)
        wait("rows")
        wait("branch")
        greeted()

    ring_q = Gather(links, (wq, pl.ds(0, 384)), (wq, pl.ds(384, 384)))
    ring_o = Gather(links, (wo, pl.ds(0, 128)), (wo, pl.ds(128, 128)))
    ring_d = Gather(links, (wd, pl.ds(0, 512)), (wd, pl.ds(512, 512)))
    ring_u = Gather(links, (wu, pl.ds(0, 512)), (wu, pl.ds(512, 512)))

    def slices_q():
        pending["q"] = to_group(lambda to: [(pack_q.at[to], wq.at[x, y, own_32, :])])
        pending["small"] = to_all(small_slots.at[z], small_slots.at[pl.ds(0, 3)], links.zs)
        pending["tokens"] = to_all(token_rows.at[z], token_rows.at[pl.ds(0, 3)], links.zs)

    def slices_o():
        pending["o"] = to_group(
            lambda to: [(pack_o.at[2 * to + h], wo.at[x, y, own_32, pl.ds(128 * h, 128)]) for h in (0, 1)]
        )

    def slices_d():
        pending["d"] = to_group(lambda to: [(pack_d.at[:, span(to, 1024)], wd.at[x, y, own_32, :])])

    def slices_u():
        pending["u"] = to_group(lambda to: [(pack_u.at[:, span(to, 1024)], wu.at[x, y, own_32, :])])

    def small_x():
        wait("small")
        small_grid[x, y] = small_slots[0] + small_slots[1] + small_slots[2] + small_slots[3]
        pending["small"] = to_all(small_grid.at[x, y], small_grid.at[0, pl.ds(0, 3)], links.xs)

    def small_y():
        wait("small")
        pending["small"] = to_all(small_grid.at[:, y], small_grid.at[:, pl.ds(0, 3)], links.ys)

    def small_rows():
        wait("small")
        for p in range(16):
            small[:, 128 * p : 128 * p + 128] = small_grid[p // 4, p % 4]

    def token_columns():
        wait("tokens")
        for row in range(4):
            tokens[row] = as_columns(token_rows[row])

    rows_one, rows_branch = Spread(links, a_one), Spread(links, branch)
    rows_two, rows_back = Spread(links, a_two), Spread(links, hidden_low)

    def norm_one():
        def step(i, rows):
            scaled, inverse = norm_parts(rows_in[rows, :].astype(F32))
            n_one[rows, :] = scaled
            info[0, rows, :] = columns_tile([inverse])

        in_blocks(4, step)

    def rows_one_start():
        def step(i, rows):
            a_one[z, core, rows, :] = (n_one[rows, :] * small[4:5, :] + small[6:7, :]).astype(BF16)

        in_blocks(4, step)
        rows_one.start()

    lane = lax.broadcasted_iota(jnp.int32, (128, 128), 1)
    causal = lax.broadcasted_iota(jnp.int32, (128, 128), 0) >= lane
    scale = 128 ** (-0.5)

    def queries():
        for c in range(3):
            part = wq[:, :, :, 256 * c : 256 * c + 256].reshape(2048, 256)
            wide[:, 256 * c : 256 * c + 256] = dot(a_one[...].reshape(512, 2048), part, (1, 0))

    def spots(index):
        row, head = lax.div(index, 2), lax.rem(index, 2)
        used = jnp.where((core * 8 + z * 2 + head).astype(F32) < tokens[row][:, 0:1], 1.0, 0.0)
        return row, span(row, 128), [span(2 * c + head, 128) for c in range(3)], used

    def attend(first, last):
        turned_sines = jnp.where(lane < 64, -sines[...], sines[...])

        def one(index, carry):
            row, rows, (q_at, k_at, v_at), used = spots(index)

            def rotate(value):
                return value * cosines[...] + turn(value) * turned_sines

            q = (rotate(wide[rows, q_at]) * scale).astype(BF16)
            k = rotate(wide[rows, k_at]).astype(BF16)
            v = wide[rows, v_at].astype(BF16)
            qkv[rows, q_at], qkv[rows, k_at], qkv[rows, v_at] = q, k, v
            scores = jnp.where(causal, dot(q, k, (1, 1)), -1e30)
            powers = jnp.exp(scores - jnp.max(scores, axis=-1, keepdims=True))
            share = powers / jnp.sum(powers, axis=-1, keepdims=True)
            probs[index] = share
            mixed[row, :, :, q_at] = (dot(share.astype(BF16), v, (1, 0)) * used).astype(BF16).reshape(2, 64, 128)
            return carry

        lax.fori_loop(first, last, one, 0)

    merge_one = Merge(links, mixed, wo, set_a, merged)

    def norm_two():
        def step(i, rows):
            value = rows_in[rows, :].astype(F32) + merge_one.rows(rows)
            hidden[rows, :] = value
            scaled, inverse = norm_parts(value)
            n_two[rows, :] = scaled
            low = (scaled * small[5:6, :] + small[7:8, :]).astype(BF16)
            a_two[z, core, rows, :] = low
            low = low.astype(F32)
            logits = [jnp.sum(low * small[b : b + 1, :], axis=-1, keepdims=True) for b in range(4)]
            top = jnp.maximum(jnp.maximum(logits[0], logits[1]), jnp.maximum(logits[2], logits[3]))
            powers = [jnp.exp(logit - top) for logit in logits]
            whole = powers[0] + powers[1] + powers[2] + powers[3]
            chances = [power / whole for power in powers]
            at = span(core * 4 + i, 16)
            own = tokens[z, at, :]
            bucket, kept = own[:, 1:2], own[:, 2:3]
            gate = jnp.zeros_like(bucket)
            for b in range(4):
                gate = jnp.where(bucket == b, chances[b], gate)
            info[1, rows, :] = columns_tile([inverse, gate, *chances])
            gates[z, at, :] = columns_tile([gate * kept])

        in_blocks(4, step)

    def rows_two_start():
        rows_two.start()
        gate_slots[z, core] = gates[z].T[0:8, :]
        whole = slots.at[0, pl.ds(0, 7), pl.ds(0, 8)]
        pending["gates"] = to_all(gate_slots.at[z, core], whole, links.zs, links.others, {0: links.partner})

    def rows_two_finish():
        rows_two.finish()
        wait("gates")
        for row in range(4):
            gates[row] = as_columns(gate_slots[row, 0] + gate_slots[row, 1])

    def units_back():
        def one(t, carry):
            at = span(t, 256)
            wide[:, at] = dot(branch[...].reshape(512, 2048), wd[:, :, :, at].reshape(2048, 256), (1, 0))
            return carry

        lax.fori_loop(0, 4, one, 0)

    def units():
        quarter = (core * 2 + lax.div(z, 2)).astype(F32)
        used_units = tokens[...].reshape(512, 128)[:, 1:2] >= quarter
        gate_all = gates[...].reshape(512, 128)[:, 0:1]

        def one(t, carry):
            at = span(t, 256)
            up = dot(a_two[...].reshape(512, 2048), wu[:, :, :, at].reshape(2048, 256), (1, 0))
            up = jnp.where(used_units, jnp.maximum(up, 0.0), 0.0)
            low = (up * up).astype(BF16)
            act[:, :, :, at] = low.reshape(4, 2, 64, 256)
            act_gated[:, :, :, at] = (low.astype(F32) * gate_all).astype(BF16).reshape(4, 2, 64, 256)
            back = wide[:, at]
            up_low[:, :, :, at] = (back * gate_all * 2.0 * up).astype(BF16).reshape(4, 2, 64, 256)
            pairs = (low.astype(F32) * back).astype(BF16)
            gate_part[...] += dot(jnp.ones((8, 256), BF16), pairs, (1, 1))
            return carry

        lax.fori_loop(0, 4, one, 0)
        pending["gate"] = [links.go(gate_part, gate_near, links.partner)]

    merge_u = Merge(links, up_low, wu, set_b, merged_too)
    merge_f = Merge(links, act, wd, set_a, merged)

    def merge_u_out():
        merge_u.cross()
        wait("gate")
        gate_part[...] = gate_part[...] + gate_near[...]
        moves = [(gate_part.at[:, span(ring(z, k), 128)], gate_far.at[k - 1], links.zs[k]) for k in (1, 2, 3)]
        pending["gate"] = [links.together(moves, gate_far.at[pl.ds(0, 3)])]

    def merge_u_in():
        wait("gate")
        gate_far[3] = gate_part[:, span(z, 128)] + gate_far[0] + gate_far[1] + gate_far[2]
        info[2] = as_columns(gate_far[3])
        merge_u.arrive()

    def outer(left, right, target):
        def one(i, carry):
            part = left[:, :, :, span(i, 256)].reshape(512, 256)
            value = dot(part, right[...].reshape(512, right.shape[-1]), (0, 0)).astype(BF16)
            row, first = lax.div(i, 2), lax.rem(i, 2) * 2
            target[row, first] = value[0:128]
            target[row, first + 1] = value[128:256]
            return carry

        lax.fori_loop(0, 8, one, 0)

    def back_two():
        def step(i, rows):
            at = span(core * 4 + i, 16)
            upstream = upstream_in[rows, :].astype(F32)
            own, tile = tokens[z, at, :], info[1, rows, :]
            bucket, kept = own[:, 1:2], own[:, 2:3]
            inverse, gate = tile[:, 0:1], tile[:, 1:2]
            gate_grad = info[2, at, :][:, 0:1] * kept
            low = a_two[z, core, rows, :].astype(F32)
            grad = merge_u.rows(rows).astype(BF16).astype(F32)
            for b in range(4):
                hot = jnp.where(bucket == b, 1.0, 0.0)
                logit_grad = tile[:, 2 + b : 3 + b] * (hot - gate) * gate_grad
                grad = grad + logit_grad * small[b : b + 1, :]
                small_sum[b] += fold(logit_grad * low)
            scaled = n_two[rows, :]
            small_sum[5] += fold(grad * scaled)
            small_sum[7] += fold(grad)
            back = upstream + norm_back(scaled, inverse, small[5:6, :], grad)
            n_two[rows, :] = back
            hidden_low[z, core, rows, :] = back.astype(BF16)

        in_blocks(4, step)

    def mixed_back():
        d_mixed[...] = dot(hidden_low[...].reshape(512, 2048), wo[...].reshape(2048, 256), (1, 0)).astype(BF16)

    def attend_back():
        def one(index, carry):
            row, rows, (q_at, k_at, v_at), used = spots(index)
            share = probs[index]
            q, k, v = qkv[rows, q_at], qkv[rows, k_at], qkv[rows, v_at]
            grad = (d_mixed[rows, q_at].astype(F32) * used).astype(BF16)
            value_grad = dot(share.astype(BF16), grad, (0, 0))
            share_grad = dot(grad, v, (1, 1))
            inner = jnp.sum(share * share_grad, axis=-1, keepdims=True)
            score_grad = (share * (share_grad - inner)).astype(BF16)

            def rotate_back(value):
                return value * cosines[...] - turn(value * sines[...]) * jnp.where(lane < 64, -1.0, 1.0)

            def put(at, value):
                d_qkv[row, :, :, at] = value.astype(BF16).reshape(2, 64, 128)

            put(q_at, rotate_back(dot(score_grad, k, (1, 0)) * scale))
            put(k_at, rotate_back(dot(score_grad, q, (0, 0))))
            put(v_at, value_grad)
            return carry

        lax.fori_loop(0, 8, one, 0)

    merge_q = Merge(links, d_qkv, wq, set_b, merged_too)
    sums_u = Scatter(links, (wu, pl.ds(0, 512)), (wu, pl.ds(512, 512)), buffers[0:8])
    sums_d = Scatter(links, (grad_d, pl.ds(0, 512)), (grad_d, pl.ds(512, 512)), buffers[8:16])
    sums_q = Scatter(links, (grad_q, pl.ds(0, 384)), (grad_q, pl.ds(384, 384)), buffers[16:24])
    sums_o = Scatter(links, (wo, pl.ds(0, 128)), (wo, pl.ds(128, 128)), buffers[24:32])

    def output_rows():
        merge_f.arrive()

        def step(i, rows):
            kept = tokens[z, span(core * 4 + i, 16), :][:, 2:3]
            produced = merge_f.rows(rows).astype(BF16).astype(F32) * kept
            out_rows[rows, :] = (hidden[rows, :] + info[1, rows, :][:, 1:2] * produced).astype(BF16)

        in_blocks(4, step)
        here = block_out.at[own_64]
        pending["output"] = [keep(out_rows, here), links.go(out_rows, here, links.partner)]

    def back_one():
        merge_q.arrive()

        def step(i, rows):
            grad = merge_q.rows(rows)
            scaled, inverse = n_one[rows, :], info[0, rows, :][:, 0:1]
            small_sum[4] += fold(grad * scaled)
            small_sum[6] += fold(grad)
            n_two[rows, :] = n_two[rows, :] + norm_back(scaled, inverse, small[4:5, :], grad)

        in_blocks(4, step)
        for r in range(8):
            small[r : r + 1, :] = jnp.sum(small_sum[r], axis=0, keepdims=True)
        pending["small"] = [links.go(small, small_near, links.partner)]
        here = input_grad.at[own_64]
        pending["input"] = [keep(n_two, here), links.go(n_two, here, links.partner)]

    def small_to_x():
        wait("small")
        small[...] = small[...] + small_near[...]
        moves = [(small.at[:, span(ring(x, k), 512)], sx_in.at[k], links.xs[k]) for k in (1, 2, 3)]
        pending["small"] = [links.together(moves, sx_in.at[pl.ds(1, 3)])]

    def small_to_y():
        wait("small")
        sx_in[0] = small[:, span(x, 512)] + sx_in[1] + sx_in[2] + sx_in[3]
        moves = [(sx_in.at[0, :, span(ring(y, k), 128)], sy_in.at[k], links.ys[k]) for k in (1, 2, 3)]
        pending["small"] = [links.together(moves, sy_in.at[pl.ds(1, 3)])]

    def small_to_z():
        wait("small")
        sz_in[z] = sx_in[0, :, span(y, 128)] + sy_in[1] + sy_in[2] + sy_in[3]
        pending["small"] = to_all(sz_in.at[z], sz_in.at[pl.ds(0, 3)], links.zs)

    def small_done():
        wait("small")
        small_grad[...] = pltpu.roll(sz_in[0] + sz_in[1] + sz_in[2] + sz_in[3], 128 - 32 * z, 1)
        _, _, update = moment_step(
            router_w[...], small_grad[0:4, 0:32], router_m[...], router_v[...], DECAY_RATE
        )
        squares[8, 0:4, 0:32] = 0.5 * router_w[...] * router_w[...]
        squares[9, 0:4, 0:32] = 0.5 * update * update

    def owners_u():
        pending["own_u"] = to_group(lambda to: [(wu.at[x, y, span(to, 32), :], pack_u.at[:, span(z, 1024)])])

    def owners_d():
        pending["own_d"] = to_group(lambda to: [(grad_d.at[x, y, span(to, 32), :], pack_d.at[:, span(z, 1024)])])

    def owners_o():
        pending["own_o"] = to_group(
            lambda to: [
                (wo.at[x, y, span(to, 32), pl.ds(128 * h, 128)], pack_o.at[2 * z + h]) for h in (0, 1)
            ]
        )

    def owners_q():
        pending["own_q"] = to_group(lambda to: [(grad_q.at[x, y, span(to, 32), :], pack_q.at[z])])

    def moments_wide():
        for number, (name, first, second) in enumerate((("mom_u", up_m, up_v), ("mom_d", down_m, down_v))):
            pending[name] = [
                keep(ref.at[:, pl.ds(1024 * c, 1024)], wide.at[pl.ds(256 * number + 128 * kind + 32 * c, 32)])
                for kind, ref in enumerate((first, second))
                for c in range(4)
            ]

    def squares_wide(number, weights, grads):
        def one(i, carry):
            rows, columns = span(lax.div(i, 4), 16), span(lax.rem(i, 4), 1024)
            weight = weights[rows, columns]
            at = lax.rem(i, 4) * 2 + lax.div(i, 4) + (number - 2) * 16
            _, _, update = moment_step(
                weight, grads[rows, columns].astype(F32), wide[span(at, 16), :], wide[span(at + 8, 16), :], DECAY_RATE
            )
            squares[2 * number] += fold_lanes(weight * weight)
            squares[2 * number + 1] += fold_lanes(update * update)
            return carry

        lax.fori_loop(0, 8, one, 0)

    def squares_u():
        wait("own_u")
        wait("mom_u")
        pending["results"] = [keep(pack_u, up_grad)]
        squares_wide(2, own_u, pack_u)

    def squares_d():
        wait("own_d")
        wait("mom_d")
        pending["results"].append(keep(pack_d, down_grad))
        squares_wide(3, own_d, pack_d)

    def squares_o():
        wait("own_o")
        wait("mom_o")
        pending["results"].append(keep(pack_o, out_grad))

        def one(head, carry):
            weight = own_o[head]
            _, _, update = moment_step(
                weight, pack_o[head].astype(F32), mom_o[0, head], mom_o[1, head], DECAY_RATE
            )
            squares[2] += fold_lanes(weight * weight)
            squares[3] += fold_lanes(update * update)
            return carry

        lax.fori_loop(0, 8, one, 0)

    def squares_q():
        wait("own_q")
        wait("mom_q")
        for c in range(3):
            for head in range(8):
                at = 256 * c + 128 * (head % 2)
                qkv_grad[:, c, head, :] = pack_q[head // 2, :, at : at + 128].astype(F32)

        def one(i, carry):
            rows = pl.ds(i * 4, 4)
            weight = own_q[rows]
            _, _, update = moment_step(weight, qkv_grad[rows], mom_q[0, rows], mom_q[1, rows], DECAY_RATE)
            squares[0] += jnp.sum(jnp.sum(weight * weight, axis=0), axis=0)
            squares[1] += jnp.sum(jnp.sum(update * update, axis=0), axis=0)
            return carry

        lax.fori_loop(0, 8, one, 0)

    def totals():
        here = 4 * core + z
        sets = ((links.zs, links.others, {0: links.partner}), (links.ys,), (links.xs,))
        tile = jnp.sum(squares[...], axis=1)
        for axis, (me, peers) in enumerate(zip((here, y, x), sets)):
            slots[axis, me] = tile
            count = 8 if axis == 0 else 4
            for copy in to_all(slots.at[axis, me], slots.at[axis, pl.ds(0, count - 1)], *peers):
                copy.wait()
            tile = slots[axis, 0]
            for k in range(1, count):
                tile = tile + slots[axis, k]
        norms[...] = tile

    begin()
    slices_q()
    small_x()
    norm_one()
    small_y()
    wait("q")
    ring_q.advance()
    slices_o()
    slices_u()
    small_rows()
    wait("o")
    ring_o.advance()
    rows_one_start()
    token_columns()
    ring_q.advance()
    ring_o.advance()
    rows_branch.start(own=False)
    wait("u")
    ring_u.advance()
    ring_q.advance()
    rows_one.relay()
    ring_o.advance()
    ring_q.advance()
    slices_d()
    rows_one.finish()
    wait("d")
    ring_d.advance()
    rows_branch.relay()
    ring_u.advance()
    ring_o.advance()
    ring_q.advance()
    queries()
    attend(0, 4)
    ring_u.advance()
    ring_o.advance()
    attend(4, 8)
    merge_one.cross()
    merge_one.along()
    ring_d.advance()
    ring_d.advance()
    merge_one.arrive()
    norm_two()
    rows_two_start()
    ring_d.advance()
    rows_branch.finish()
    ring_u.advance()
    rows_two.relay()
    rows_two_finish()
    ring_d.advance()
    units_back()
    ring_u.advance()
    units()
    merge_u_out()
    outer(branch, act_gated, grad_d)
    sums_d.advance()
    merge_u.along()
    outer(a_two, up_low, wu)
    sums_u.advance()
    merge_u_in()
    back_two()
    rows_back.start()
    merge_f.cross()
    sums_d.advance()
    merge_f.along(leave=False)
    rows_back.relay()
    sums_u.advance()
    rows_back.finish()
    merge_f.leave()
    mixed_back()
    attend_back()
    sums_d.advance()
    sums_u.advance()
    outer(a_one, d_qkv, grad_q)
    sums_q.advance()
    merge_q.cross()
    merge_q.along()
    moments_wide()
    sums_u.advance()
    outer(hidden_low, mixed, wo)
    sums_d.advance()
    sums_o.advance()
    sums_u.advance()
    owners_u()
    sums_q.advance()
    output_rows()
    sums_o.advance()
    back_one()
    small_to_x()
    sums_o.advance()
    sums_q.advance()
    squares_u()
    sums_d.advance()
    owners_d()
    small_to_y()
    sums_o.advance()
    sums_q.advance()
    small_to_z()
    sums_o.advance()
    owners_o()
    sums_q.advance()
    owners_q()
    small_done()
    squares_o()
    squares_d()
    squares_q()
    totals()
    wait("output")
    wait("input")
    wait("results")


def layer(*operands):
    def vmem(*shape, kind=BF16):
        return pltpu.VMEM(shape, kind)

    def merge_buffers():
        return [vmem(TILES, 4, 64, TILE), vmem(TILES, 4, 64, TILE), vmem(3, TILES, 64, TILE)]

    def sum_buffers(width):
        return [
            vmem(2, 4, 64, width), vmem(2, 4, 128, width), vmem(2, 64, width), vmem(2, 128, width),
        ] * 2

    rows, rows_low, tokens = vmem(64, 2048, kind=F32), vmem(64, 2048), vmem(4, 2, 64, 2048)
    tile = vmem(4, 8, 128, kind=F32)
    return pl.pallas_call(
        layer_kernel,
        out_shape=(
            jax.ShapeDtypeStruct((128, 2048), BF16),
            jax.ShapeDtypeStruct((128, 2048), F32),
            jax.ShapeDtypeStruct((32, 3, 8, 128), F32),
            jax.ShapeDtypeStruct((8, 32, 128), BF16),
            jax.ShapeDtypeStruct((32, 4096), BF16),
            jax.ShapeDtypeStruct((32, 4096), BF16),
            jax.ShapeDtypeStruct((8, 128), F32),
            jax.ShapeDtypeStruct((16, 128), F32),
        ),
        in_specs=[ANY] * 14 + [VMEM] * 11,
        out_specs=(ANY, ANY, VMEM, ANY, ANY, ANY, VMEM, VMEM),
        scratch_shapes=[
            vmem(32, 3, 8, 128, kind=F32), vmem(8, 32, 128, kind=F32), vmem(32, 4096, kind=F32),
            vmem(32, 4096, kind=F32),
            vmem(4, 32, 768), vmem(8, 32, 128), vmem(32, 4096), vmem(32, 4096),
            vmem(2, 32, 3, 8, 128, kind=F32), vmem(2, 8, 32, 128, kind=F32),
            vmem(4, 4, 128, 768), vmem(4, 4, 128, 256), vmem(4, 4, 128, 1024), vmem(4, 4, 128, 1024),
            vmem(4, 4, 128, 768), vmem(4, 4, 128, 1024),
            tile, vmem(4, 4, 8, 128, kind=F32), vmem(8, 2048, kind=F32), vmem(8, 2048, kind=F32),
            tile, vmem(4, 128, 128, kind=F32), vmem(4, 2, 8, 128, kind=F32), vmem(4, 128, 128, kind=F32),
            vmem(3, 128, 128, kind=F32),
            tokens, tokens, tokens, tokens,
            rows_low, rows_low, rows, rows, rows, rows, rows, rows_low,
            vmem(512, 1024, kind=F32), vmem(512, 768), vmem(8, 128, 128, kind=F32),
            vmem(4, 2, 64, 256), vmem(512, 256), vmem(4, 2, 64, 768), vmem(4, 2, 64, 1024), vmem(4, 2, 64, 1024), vmem(4, 2, 64, 1024),
            *merge_buffers(), *merge_buffers(),
            vmem(8, 512, kind=F32), vmem(8, 512, kind=F32), tile,
            vmem(8, 8, 2048, kind=F32), vmem(4, 8, 512, kind=F32), tile, tile,
            vmem(16, 8, 128, kind=F32), vmem(3, 8, 16, 128, kind=F32),
            *sum_buffers(512), *sum_buffers(512), *sum_buffers(384), *sum_buffers(128),
            DMA((LOCAL_COPIES,)), DMA((LINK_COPIES,)), DMA((LINK_COPIES,)),
        ],
        compiler_params=pltpu.CompilerParams(
            collective_id=0, has_side_effects=True, vmem_limit_bytes=63 * 2**20
        ),
        name="layer",
    )(*operands)


def renew_kernel(norms, small_grad, gains, biases, norm_m, norm_v, *refs):
    ins, outs = refs[:22], refs[22:]
    outs[31][...] = ins[20][...]
    outs[32][...] = ins[21][...]
    sums = jnp.sqrt(jnp.sum(norms[...], axis=1, keepdims=True))
    for index in range(5):
        weight, grad, m, v = (ref[...] for ref in ins[4 * index : 4 * index + 4])
        grad = grad[0:4, 0:32] if index == 4 else grad.astype(F32)
        first, second, update = moment_step(weight, grad, m, v, DECAY_RATE)
        ratio = LEARN_RATE * (sums[2 * index : 2 * index + 1, :] / sums[2 * index + 1 : 2 * index + 2, :])
        ratio = ratio.reshape((1,) * weight.ndim)
        new = weight - ratio * update
        for ref, value in zip(outs[5 * index : 5 * index + 5], (grad, first, second, new, new.astype(BF16))):
            ref[...] = value
    grad = small_grad[4:8, 0:32]
    master = jnp.concatenate([gains[...], biases[...]], axis=0)
    first, second, update = moment_step(master, grad, norm_m[...], norm_v[...], 0.0)
    new = master - NORM_RATE * update
    for ref, value in zip(outs[25:30], (grad, first, second, new, new.astype(BF16))):
        ref[...] = value
    row = lax.broadcasted_iota(jnp.int32, (8, 128), 0)
    lane = lax.broadcasted_iota(jnp.int32, (8, 128), 1)
    tile = jnp.zeros((8, 128), F32)
    for index in range(10):
        here = (row == index % 2) & (lane == index // 2)
        tile = jnp.where(here, sums[index : index + 1, :], tile)
    outs[30][...] = tile[0:2, 0:5]


def renew(norms, small_grad, gains, biases, norm_m, norm_v, *matrices):
    steps = 4

    def whole(shape):
        return pl.BlockSpec(shape, lambda i: (0,) * len(shape))

    blocks = (
        pl.BlockSpec((32 // steps, 3, 8, 128), lambda i: (i, 0, 0, 0)),
        pl.BlockSpec((8 // steps, 32, 128), lambda i: (i, 0, 0)),
        pl.BlockSpec((32, 4096 // steps), lambda i: (0, i)),
        pl.BlockSpec((32, 4096 // steps), lambda i: (0, i)),
        whole((4, 32)),
    )
    shapes = ((32, 3, 8, 128), (8, 32, 128), (32, 4096), (32, 4096), (4, 32), (4, 32))
    in_specs = [whole((16, 128)), whole((8, 128)), whole((2, 32)), whole((2, 32)), whole((4, 32)), whole((4, 32))]
    out_specs, out_shape = [], []
    for index, block in enumerate(blocks):
        in_specs += [block, whole((8, 128)) if index == 4 else block, block, block]
    for block, shape in zip((*blocks, whole((4, 32))), shapes):
        out_specs += [block] * 5
        out_shape += [jax.ShapeDtypeStruct(shape, kind) for kind in (F32, F32, F32, F32, BF16)]
    out_specs.append(whole((2, 5)))
    out_shape.append(jax.ShapeDtypeStruct((2, 5), F32))
    rows = pl.BlockSpec((128 // steps, 2048), lambda i: (i, 0))
    in_specs += [rows, rows]
    out_specs += [rows, rows]
    out_shape += [jax.ShapeDtypeStruct((128, 2048), kind) for kind in (BF16, F32)]
    return pl.pallas_call(
        renew_kernel,
        grid=(steps,),
        in_specs=in_specs,
        out_specs=out_specs,
        out_shape=out_shape,
        compiler_params=pltpu.CompilerParams(vmem_limit_bytes=63 * 2**20),
        name="renew",
    )(norms, small_grad, gains, biases, norm_m, norm_v, *matrices)


def rotary_tables(length, size):
    half_size = size // 2
    frequency = ROPE_BASE ** (-(np.arange(half_size) * 2.0 / size))
    angles = np.arange(length)[:, None] * frequency[None, :]
    cosine_table = np.concatenate([np.cos(angles), np.cos(angles)], axis=-1)
    sine_table = np.concatenate([np.sin(angles), np.sin(angles)], axis=-1)
    return (cosine_table.astype(np.float32), sine_table.astype(np.float32))


def local(
    block_input,
    cotangent,
    head_count,
    width_route,
    forced_width,
    slot_index,
    qkv_weight,
    out_weight,
    up_weight,
    down_weight,
    router_weight,
    norm_gains,
    norm_biases,
    qkv_first,
    qkv_second,
    out_first,
    out_second,
    up_first,
    up_second,
    down_first,
    down_second,
    router_first,
    router_second,
    norm_first,
    norm_second,
):
    def turned(value):
        return value.transpose(0, 2, 1)

    out = turned(out_weight), turned(out_first), turned(out_second)
    down = down_weight.T, down_first.T, down_second.T
    router = router_weight.T, router_first.T, router_second.T
    block_output, input_grad, *grads, small_grad, norms = layer(
        qkv_weight, out[0], up_weight, down[0],
        qkv_first, qkv_second, *out[1:], up_first, up_second, *down[1:],
        block_input, cotangent, *router, norm_gains, norm_biases,
        *(value.reshape(1, -1) for value in (head_count, width_route, forced_width, slot_index)),
        *rotary_tables(128, 128),
    )
    *results, lamb_norms, block_output, input_grad = renew(
        norms, small_grad, norm_gains, norm_biases, norm_first, norm_second,
        qkv_weight, grads[0], qkv_first, qkv_second,
        out[0], grads[1], *out[1:],
        up_weight, grads[2], up_first, up_second,
        down[0], grads[3], *down[1:],
        router[0], small_grad, *router[1:],
        block_output, input_grad,
    )
    kinds = []
    for kind in range(5):
        qkv, out, up, down, router, norm = (results[5 * index + kind] for index in range(6))
        kinds += [qkv, turned(out), up, down.T, router.T, norm]
    return (block_output, input_grad, *kinds, lamb_norms.T)


def solution(mesh):
    qkv, out = P("dp", None, "mp", None), P("mp", None, "dp")
    up, down, router, norms = P("dp", "mp"), P("mp", "dp"), P("dp", None), P(None, "dp")
    rows, tokens = P("dp", None), P("dp")
    matrices = (qkv, out, up, down, router)
    return jax.shard_map(
        local,
        mesh=mesh,
        in_specs=(
            rows, rows, tokens, tokens, tokens, tokens,
            *matrices, norms, norms,
            qkv, qkv, out, out, up, up, down, down, router, router, norms, norms,
        ),
        out_specs=(rows, rows, *((*matrices, norms) * 5), P()),
        check_vma=False,
    )
```

```python
import jax
import jax.numpy as jnp
import numpy as np
from jax import lax
from jax.experimental import pallas as pl
from jax.experimental.pallas import tpu as pltpu
from jax.sharding import PartitionSpec as P

STEP = 5

BETA_ONE = 0.5
BETA_TWO = 0.5
ADAM_EPS = 1e-06
DECAY_RATE = 0.01
LEARN_RATE = 0.5
NORM_RATE = 0.1
NORM_EPS = 1e-05
ROPE_BASE = 10000.0

MESH = pl.DeviceIdType.MESH
BF16 = jnp.bfloat16
F32 = jnp.float32
VMEM = pl.BlockSpec(memory_space=pltpu.VMEM)
ANY = pl.BlockSpec(memory_space=pl.ANY)
DMA = pltpu.SemaphoreType.DMA
ALL = slice(None)
LOW, HIGH = pl.ds(0, 64), pl.ds(64, 64)


def place():
    index = lax.axis_index("dp")
    return lax.div(index, 16), lax.rem(lax.div(index, 4), 4), lax.rem(index, 4), lax.axis_index("mp")


def ring(value, step):
    return lax.rem(value + (step + 4), 4)


def device(x, y, z, core):
    return (x * 16 + y * 4 + z, core)


def greet(peers):
    barrier = pltpu.get_barrier_semaphore()
    for peer in peers:
        pl.semaphore_signal(barrier, inc=1, device_id=peer, device_id_type=MESH)
    return lambda: pl.semaphore_wait(barrier, len(peers))


def send(src, dst, send_sem, recv_sem, peer):
    copy = pltpu.make_async_remote_copy(
        src_ref=src, dst_ref=dst, send_sem=send_sem, recv_sem=recv_sem, device_id=peer, device_id_type=MESH
    )
    copy.start()
    return copy


def span(index, size):
    return pl.ds(pl.multiple_of(index * size, size), size)


def dot(left, right, dims):
    return lax.dot_general(left, right, ((dims[:1], dims[1:]), ((), ())), preferred_element_type=F32)


class Links:
    def __init__(self, send_sems, recv_sems):
        self.x, self.y, self.z, self.core = x, y, z, core = place()
        self.xs = {k: device(ring(x, k), y, z, core) for k in (1, 2, 3)}
        self.ys = {k: device(x, ring(y, k), z, core) for k in (1, 2, 3)}
        self.zs = {k: device(x, y, ring(z, k), core) for k in (1, 2, 3)}
        self.others = {k: device(x, y, ring(z, k), 1 - core) for k in (1, 2, 3)}
        self.across = {(i, j): device(ring(x, i), ring(y, j), z, core) for i in (1, 2, 3) for j in (1, 2, 3)}
        self.partner = device(x, y, z, 1 - core)
        self.send_sems, self.recv_sems, self.used = send_sems, recv_sems, 0

    def go(self, src, dst, peer):
        number = self.used
        self.used += 1
        return send(src, dst, self.send_sems.at[number], self.recv_sems.at[number], peer)

    def bundle(self, whole):
        number = self.used
        self.used += 1
        return Bundle(whole, self.send_sems.at[number], self.recv_sems.at[number])

    def together(self, moves, whole):
        bundle = self.bundle(whole)
        for move in moves:
            bundle.go(*move)
        return bundle


class Bundle:
    def __init__(self, whole, *sems):
        self.whole, self.sems = whole, sems

    def go(self, src, dst, peer):
        send(src, dst, *self.sems, peer)

    def wait(self):
        for sem in self.sems:
            pltpu.make_async_copy(self.whole, self.whole, sem).wait()


class Gather:
    def __init__(self, links, first, second):
        self.links, self.parts, self.number, self.copies = links, (first, second), 0, []

    def advance(self):
        for copy in self.copies:
            copy.wait()
        x, y = self.links.x, self.links.y
        xp, xm, yp, ym = self.links.xs[1], self.links.xs[3], self.links.ys[1], self.links.ys[3]
        xb, xa, yb, ya = ring(x, -1), ring(x, 1), ring(y, -1), ring(y, 1)
        moves = {
            0: (((x, y, ALL), xp), ((x, y, ALL), xm), ((x, y, ALL), yp), ((x, y, ALL), ym)),
            1: (((xb, y, LOW), xp), ((xa, y, HIGH), xm), ((x, yb, LOW), yp), ((x, ya, HIGH), ym)),
            2: (((ALL, y, ALL), yp), ((ALL, y, ALL), ym), ((x, ALL, ALL), xp), ((x, ALL, ALL), xm)),
            3: (((ALL, yb, LOW), yp), ((ALL, ya, HIGH), ym), ((xb, ALL, LOW), xp), ((xa, ALL, HIGH), xm)),
        }.get(self.number, ())
        if moves:
            pairs = [(self.parts[index // 2][0].at[where + (self.parts[index // 2][1],)], peer)
                     for index, (where, peer) in enumerate(moves)]
            ref, columns = self.parts[0]
            whole = (
                ref.at[0, :, :, columns], ref.at[0, pl.ds(0, 2), :, columns],
                ref.at[:, :, :, columns], ref.at[pl.ds(0, 2), :, :, columns],
            )[self.number]
            self.copies = [self.links.together([(block, block, peer) for block, peer in pairs], whole)]
        else:
            self.copies = []
        self.number += 1


def add_into(ref, blocks, columns, sources, row, count):
    steps = count // 16

    def one(index, carry):
        number = lax.div(index, steps)
        step = pl.multiple_of(lax.rem(index, steps) * 16, 16)
        to = blocks[1](number) + (pl.ds(row + step, 16), columns)
        here = ref[to].astype(F32)
        for source, first_row in sources:
            place_in = ((number,) if blocks[0] > 1 else ()) + (pl.ds(first_row + step, 16), ALL)
            here = here + source[place_in].astype(F32)
        ref[to] = here.astype(BF16)
        return carry

    lax.fori_loop(0, blocks[0] * steps, one, 0)


class Scatter:
    def __init__(self, links, first, second, buffers):
        self.links, self.parts = links, (first, second)
        self.buffers = (buffers[:4], buffers[4:])
        self.number, self.halves, self.rest = 0, [], []

    def lanes(self, phase):
        x, y = self.links.x, self.links.y
        found = []
        for part in (0, 1):
            ref, columns = self.parts[part]
            along_y = part == phase
            peers = self.links.ys if along_y else self.links.xs
            if phase == 0 and along_y:
                where, count, each = (lambda k: (ALL, ring(y, k))), 4, (lambda k: lambda i: (i, ring(y, k)))
            elif phase == 0:
                where, count, each = (lambda k: (ring(x, k), ALL)), 4, (lambda k: lambda i: (ring(x, k), i))
            elif along_y:
                where, count, each = (lambda k: (x, ring(y, k))), 1, (lambda k: lambda i: (x, ring(y, k)))
            else:
                where, count, each = (lambda k: (ring(x, k), y)), 1, (lambda k: lambda i: (ring(x, k), y))
            one, two = self.buffers[part][2 * phase : 2 * phase + 2]
            found.append((ref, columns, where, count, each, peers, one, two))
        return found

    def begin(self, phase):
        self.halves, self.rest = [], []
        links = self.links
        for ref, columns, where, count, each, peers, one, two in self.lanes(phase):
            self.halves.append(links.go(ref.at[where(2) + (LOW, columns)], one.at[0], peers[1]))
            self.halves.append(links.go(ref.at[where(2) + (HIGH, columns)], one.at[1], peers[3]))
        moves = []
        for ref, columns, where, count, each, peers, one, two in self.lanes(phase):
            lead = (ALL,) if count > 1 else ()
            moves.append((ref.at[where(1) + (HIGH, columns)], two.at[(0,) + lead + (HIGH,)], peers[1]))
            moves.append((ref.at[where(-1) + (LOW, columns)], two.at[(1,) + lead + (LOW,)], peers[3]))
        self.rest.append(links.together(moves, self.buffers[0][2 * phase + 1]))

    def middle(self, phase):
        lanes, last = self.lanes(phase), self.links.bundle(self.buffers[0][2 * phase + 1])
        self.rest.append(last)
        for side in (0, 1):
            for part in (0, 1):
                ref, columns, where, count, each, peers, one, two = lanes[part]
                lead = (ALL,) if count > 1 else ()
                step, rows, row = ((1, LOW, 0), (-1, HIGH, 64))[side]
                self.halves[2 * part + side].wait()
                add_into(ref, (count, each(step)), columns, [(one.at[side], 0)], row, 64)
                last.go(
                    ref.at[where(step) + (rows, columns)], two.at[(side,) + lead + (rows,)], peers[(1, 3)[side]]
                )

    def end(self, phase):
        for copy in self.rest:
            copy.wait()
        for ref, columns, where, count, each, peers, one, two in self.lanes(phase):
            add_into(ref, (count, each(0)), columns, [(two.at[0], 0), (two.at[1], 0)], 0, 128)

    def advance(self):
        if self.number == 0:
            self.begin(0)
        elif self.number == 1:
            self.middle(0)
        elif self.number == 2:
            self.end(0)
            self.begin(1)
        elif self.number == 3:
            self.middle(1)
        elif self.number == 4:
            self.end(1)
        self.number += 1


class Spread:
    def __init__(self, links, ref):
        self.links, self.ref = links, ref

    def start(self, own=True):
        links = self.links
        here = self.ref.at[links.z, links.core]
        self.passed = links.bundle(self.ref.at[pl.ds(0, 4 if own else 3), 0])
        if own:
            self.passed.go(here, here, links.partner)
        self.flying = [links.go(here, here, links.zs[k]) for k in (1, 3)]

    def relay(self):
        links = self.links
        self.far = links.bundle(self.ref.at[0, 0])
        for side, k, rows in ((0, 1, pl.ds(0, 32)), (1, 3, pl.ds(32, 32))):
            self.flying[side].wait_recv()
            block = self.ref.at[ring(links.z, -k), links.core]
            half = block.at[rows]
            self.far.go(half, half, links.zs[k])
            self.passed.go(block, block, links.partner)

    def finish(self):
        links = self.links
        self.far.wait()
        block = self.ref.at[ring(links.z, 2), links.core]
        self.passed.go(block, block, links.partner)
        for copy in self.flying:
            copy.wait_send()
        self.passed.wait()


TILES, TILE = 4, 512


class Merge:
    def __init__(self, links, left, weights, buffers, out):
        self.links, self.left, self.weights, self.out = links, left, weights, out
        self.near, self.near_in, self.far_in, self.tmp = buffers
        self.crossing, self.flying = [], None

    def tile(self, half, j):
        rows = self.weights[j]
        left = self.left[:, half]
        return dot(left.reshape(256, left.shape[-1]), rows.reshape(TILE, rows.shape[-1]), (1, 1))

    def cross(self):
        for j in range(TILES):
            self.near[j] = self.tile(1 - self.links.core, j).astype(BF16).reshape(4, 64, TILE)
            self.crossing.append(self.links.go(self.near.at[j], self.near_in.at[j], self.links.partner))

    def along(self, leave=True):
        for j in range(TILES):
            value = self.tile(self.links.core, j)
            self.crossing[j].wait()
            value = value + self.near_in[j].astype(F32).reshape(256, TILE)
            self.tmp[0:256, 0:TILE] = value
            self.near[j] = value.astype(BF16).reshape(4, 64, TILE)
            if leave:
                self.leave(j)
            self.out[:, TILE * j : TILE * j + TILE] = self.tmp[span(self.links.z, 64), 0:TILE]

    def leave(self, j=ALL):
        links = self.links
        if self.flying is None:
            self.flying = links.bundle(self.far_in)
        for k in (2, 1, 3):
            self.flying.go(self.near.at[j, ring(links.z, k)], self.far_in.at[k - 1, j], links.zs[k])

    def arrive(self):
        self.flying.wait()

    def rows(self, rows):
        value = self.out[rows, :]
        for k in range(3):
            parts = [self.far_in[k, j, rows, :] for j in range(TILES)]
            value = value + jnp.concatenate(parts, axis=1).astype(F32)
        return value


def norm_parts(value):
    centre = value - jnp.mean(value, axis=-1, keepdims=True)
    inverse = lax.rsqrt(jnp.mean(centre * centre, axis=-1, keepdims=True) + NORM_EPS)
    return centre * inverse, inverse


def norm_back(scaled, inverse, gain_row, upstream):
    dscaled = upstream * gain_row
    inner = (
        dscaled
        - jnp.mean(dscaled, axis=-1, keepdims=True)
        - scaled * jnp.mean(dscaled * scaled, axis=-1, keepdims=True)
    )
    return inner * inverse


def fold(value):
    return value[0:8, :] + value[8:16, :]


def fold_lanes(value):
    total = None
    for row in range(0, value.shape[0], 8):
        for lane in range(0, value.shape[1], 128):
            part = value[row : row + 8, lane : lane + 128]
            total = part if total is None else total + part
    return total


def columns_tile(columns):
    lane = lax.broadcasted_iota(jnp.int32, (16, 128), 1)
    tile = jnp.zeros((16, 128), F32)
    for index, column in enumerate(columns):
        tile = jnp.where(lane == index, column, tile)
    return tile


def as_columns(rows):
    return jnp.concatenate([rows, jnp.zeros((120, 128), F32)], axis=0).T


def turn(value):
    return pltpu.roll(value, 64, 1)


def moment_step(weight, gradient, first_moment, second_moment, decay_rate):
    first_moment = BETA_ONE * first_moment + (1.0 - BETA_ONE) * gradient
    second_moment = BETA_TWO * second_moment + (1.0 - BETA_TWO) * gradient * gradient
    one, two = 1.0 / (1.0 - BETA_ONE**STEP), 1.0 / (1.0 - BETA_TWO**STEP)
    update = (first_moment * one) / (jnp.sqrt(second_moment * two) + ADAM_EPS) + decay_rate * weight
    return (first_moment, second_moment, update)


LINK_COPIES = 123
LOCAL_COPIES = 29


def layer_kernel(
    qkv_w, out_w, up_w, down_w, qkv_m, qkv_v, out_m, out_v, up_m, up_v, down_m, down_v, block_in, cotangent,
    router_w, router_m, router_v, gains, biases, head_count, width_route, forced_width, slot_index, cosines, sines,
    block_out, input_grad, qkv_grad, out_grad, up_grad, down_grad, small_grad, norms,
    own_q, own_o, own_u, own_d, pack_q, pack_o, pack_u, pack_d, mom_q, mom_o,
    wq, wo, wu, wd, grad_q, grad_d, small_slots, small_grid, small, small_near,
    token_rows, tokens, gate_slots, gates, info,
    a_one, a_two, branch, hidden_low,
    rows_in, upstream_in, hidden, n_one, n_two, merged, merged_too, out_rows,
    wide, qkv, probs, mixed, d_mixed, d_qkv, act, act_gated, up_low,
    near_a, near_in_a, far_in_a, near_b, near_in_b, far_in_b,
    gate_part, gate_near, gate_far, small_sum, sx_in, sy_in, sz_in, squares, slots,
    *rest,
):
    buffers, (local_sems, send_sems, recv_sems) = rest[:-3], rest[-3:]
    links = Links(send_sems, recv_sems)
    x, y, z, core = links.x, links.y, links.z, links.core
    own_32, own_64, plane = span(z, 32), span(core, 64), 4 * x + y
    set_a = (near_a, near_in_a, far_in_a, wide)
    set_b = (near_b, near_in_b, far_in_b, wide)
    local_used, pending = [0], {"results": []}

    def keep(src, dst):
        copy = pltpu.make_async_copy(src, dst, local_sems.at[local_used[0]])
        local_used[0] += 1
        copy.start()
        return copy

    def wait(name):
        for copy in pending.pop(name):
            copy.wait()

    def in_blocks(count, step):
        def one(i, carry):
            step(i, span(i, 16))
            return carry

        lax.fori_loop(0, count, one, 0)

    def to_group(whole, moves):
        bundle = links.bundle(whole)
        for k in (2, 1, 3):
            for src, dst in moves(ring(z, k)):
                bundle.go(src, dst, links.zs[k])
        return [bundle, *(keep(src, dst) for src, dst in moves(z))]

    def to_all(here, whole, *sets):
        return [links.together([(here, here, peer) for peers in sets for peer in peers.values()], whole)]

    def begin():
        greeted = greet(
            [peer for peers in (links.xs, links.ys, links.across, links.zs, links.others) for peer in peers.values()]
            + [links.partner]
        )
        loads = [keep(qkv_w, own_q), keep(out_w, own_o), keep(up_w, own_u), keep(down_w, own_d)]
        pending["rows"] = [keep(block_in.at[own_64], rows_in), keep(cotangent.at[own_64], upstream_in)]
        pending["branch"] = [keep(cotangent.at[pl.ds(64 * h, 64)], branch.at[z, h]) for h in (0, 1)]
        pending["mom_q"] = [keep(qkv_m, mom_q.at[0]), keep(qkv_v, mom_q.at[1])]
        pending["mom_o"] = [keep(out_m, mom_o.at[0]), keep(out_v, mom_o.at[1])]
        small_slots[z] = jnp.zeros((8, 128), F32)
        small_slots[z, 0:4, 0:32] = router_w[...].astype(BF16).astype(F32)
        small_slots[z, 4:6, 0:32] = gains[...].astype(BF16).astype(F32)
        small_slots[z, 6:8, 0:32] = biases[...].astype(BF16).astype(F32)
        small_slots[z] = pltpu.roll(small_slots[z], 32 * z, 1)
        bucket_row = jnp.where(forced_width[0] < 4, forced_width[0], width_route[...])
        token_rows[z] = jnp.zeros((8, 128), F32)
        token_rows[z, 0:1, :] = head_count[...].astype(F32)
        token_rows[z, 1:2, :] = bucket_row.astype(F32)
        token_rows[z, 2:3, :] = jnp.where(slot_index[...] >= 0, 1.0, 0.0)
        loads[0].wait()
        for c in range(3):
            for head in range(8):
                at = 256 * c + 128 * (head % 2)
                pack_q[head // 2, :, at : at + 128] = own_q[:, c, head, :].astype(BF16)
        pending["loads"] = loads[1:]
        greeted()

    def pack_rest():
        wait("loads")

        def pack(i, rows):
            pack_u[rows, :] = own_u[rows, :].astype(BF16)
            pack_d[rows, :] = own_d[rows, :].astype(BF16)
            for head in range(8):
                pack_o[head, rows, :] = own_o[head, rows, :].astype(BF16)

        in_blocks(2, pack)
        gates[z] = jnp.zeros((128, 128), F32)
        gate_part[...] = jnp.zeros_like(gate_part)
        small_sum[...] = jnp.zeros_like(small_sum)
        squares[...] = jnp.zeros_like(squares)

    ring_q = Gather(links, (wq, pl.ds(0, 384)), (wq, pl.ds(384, 384)))
    ring_o = Gather(links, (wo, pl.ds(0, 128)), (wo, pl.ds(128, 128)))
    ring_d = Gather(links, (wd, pl.ds(0, 512)), (wd, pl.ds(512, 512)))
    ring_u = Gather(links, (wu, pl.ds(0, 512)), (wu, pl.ds(512, 512)))

    def slices_q():
        pending["q"] = to_group(
            pack_q.at[pl.ds(0, 3)], lambda to: [(pack_q.at[to], wq.at[x, y, own_32, :])])
        pending["small"] = to_all(small_slots.at[z], small_slots.at[pl.ds(0, 3)], links.zs)
        pending["tokens"] = to_all(token_rows.at[z], token_rows.at[pl.ds(0, 3)], links.zs)

    def slices_o():
        pending["o"] = to_group(
            pack_o.at[pl.ds(0, 6)],
            lambda to: [(pack_o.at[2 * to + h], wo.at[x, y, own_32, pl.ds(128 * h, 128)]) for h in (0, 1)]
        )

    def slices_d():
        pending["d"] = to_group(
            pack_d.at[:, pl.ds(0, 3072)], lambda to: [(pack_d.at[:, span(to, 1024)], wd.at[x, y, own_32, :])])

    def slices_u():
        pending["u"] = to_group(
            pack_u.at[:, pl.ds(0, 3072)], lambda to: [(pack_u.at[:, span(to, 1024)], wu.at[x, y, own_32, :])])

    def small_x():
        wait("small")
        small_grid[x, y] = small_slots[0] + small_slots[1] + small_slots[2] + small_slots[3]
        pending["small"] = to_all(small_grid.at[x, y], small_grid.at[0, pl.ds(0, 3)], links.xs)

    def small_y():
        wait("small")
        pending["small"] = to_all(small_grid.at[:, y], small_grid.at[:, pl.ds(0, 3)], links.ys)

    def small_rows():
        wait("small")
        for p in range(16):
            small[:, 128 * p : 128 * p + 128] = small_grid[p // 4, p % 4]

    def token_columns():
        wait("tokens")
        for row in range(4):
            tokens[row] = as_columns(token_rows[row])

    rows_one, rows_branch = Spread(links, a_one), Spread(links, branch)
    rows_two, rows_back = Spread(links, a_two), Spread(links, hidden_low)

    def norm_one():
        wait("rows")

        def step(i, rows):
            scaled, inverse = norm_parts(rows_in[rows, :].astype(F32))
            n_one[rows, :] = scaled
            info[0, rows, :] = columns_tile([inverse])

        in_blocks(4, step)

    def rows_branch_start():
        wait("branch")
        rows_branch.start(own=False)

    def rows_one_start():
        def step(i, rows):
            a_one[z, core, rows, :] = (n_one[rows, :] * small[4:5, :] + small[6:7, :]).astype(BF16)

        in_blocks(4, step)
        rows_one.start()

    lane = lax.broadcasted_iota(jnp.int32, (128, 128), 1)
    causal = lax.broadcasted_iota(jnp.int32, (128, 128), 0) >= lane
    scale = 128 ** (-0.5)

    def queries():
        for c in range(3):
            part = wq[:, :, :, 256 * c : 256 * c + 256].reshape(2048, 256)
            wide[:, 256 * c : 256 * c + 256] = dot(a_one[...].reshape(512, 2048), part, (1, 0))

    def spots(index):
        row, head = lax.div(index, 2), lax.rem(index, 2)
        used = jnp.where((core * 8 + z * 2 + head).astype(F32) < tokens[row][:, 0:1], 1.0, 0.0)
        return row, span(row, 128), [span(2 * c + head, 128) for c in range(3)], used

    def attend(first, last):
        turned_sines = jnp.where(lane < 64, -sines[...], sines[...])

        def one(index, carry):
            row, rows, (q_at, k_at, v_at), used = spots(index)

            def rotate(value):
                return value * cosines[...] + turn(value) * turned_sines

            q = (rotate(wide[rows, q_at]) * scale).astype(BF16)
            k = rotate(wide[rows, k_at]).astype(BF16)
            v = wide[rows, v_at].astype(BF16)
            qkv[rows, q_at], qkv[rows, k_at], qkv[rows, v_at] = q, k, v
            scores = jnp.where(causal, dot(q, k, (1, 1)), -1e30)
            powers = jnp.exp(scores - jnp.max(scores, axis=-1, keepdims=True))
            share = powers / jnp.sum(powers, axis=-1, keepdims=True)
            probs[index] = share
            mixed[row, :, :, q_at] = (dot(share.astype(BF16), v, (1, 0)) * used).astype(BF16).reshape(2, 64, 128)
            return carry

        lax.fori_loop(first, last, one, 0)

    merge_one = Merge(links, mixed, wo, set_a, merged)

    def norm_two():
        def step(i, rows):
            value = rows_in[rows, :].astype(F32) + merge_one.rows(rows)
            hidden[rows, :] = value
            scaled, inverse = norm_parts(value)
            n_two[rows, :] = scaled
            low = (scaled * small[5:6, :] + small[7:8, :]).astype(BF16)
            a_two[z, core, rows, :] = low
            low = low.astype(F32)
            logits = [jnp.sum(low * small[b : b + 1, :], axis=-1, keepdims=True) for b in range(4)]
            top = jnp.maximum(jnp.maximum(logits[0], logits[1]), jnp.maximum(logits[2], logits[3]))
            powers = [jnp.exp(logit - top) for logit in logits]
            whole = powers[0] + powers[1] + powers[2] + powers[3]
            chances = [power / whole for power in powers]
            at = span(core * 4 + i, 16)
            own = tokens[z, at, :]
            bucket, kept = own[:, 1:2], own[:, 2:3]
            gate = jnp.zeros_like(bucket)
            for b in range(4):
                gate = jnp.where(bucket == b, chances[b], gate)
            info[1, rows, :] = columns_tile([inverse, gate, *chances])
            gates[z, at, :] = columns_tile([gate * kept])

        in_blocks(4, step)

    def rows_two_start():
        rows_two.start()
        gate_slots[z, core] = gates[z].T[0:8, :]
        whole = slots.at[0, pl.ds(0, 7), pl.ds(0, 8)]
        pending["gates"] = to_all(gate_slots.at[z, core], whole, links.zs, links.others, {0: links.partner})

    def rows_two_finish():
        rows_two.finish()
        wait("gates")
        for row in range(4):
            gates[row] = as_columns(gate_slots[row, 0] + gate_slots[row, 1])

    def units_back():
        def one(t, carry):
            at = span(t, 256)
            wide[:, at] = dot(branch[...].reshape(512, 2048), wd[:, :, :, at].reshape(2048, 256), (1, 0))
            return carry

        lax.fori_loop(0, 4, one, 0)

    def units():
        quarter = (core * 2 + lax.div(z, 2)).astype(F32)
        used_units = tokens[...].reshape(512, 128)[:, 1:2] >= quarter
        gate_all = gates[...].reshape(512, 128)[:, 0:1]

        def one(t, carry):
            at = span(t, 256)
            up = dot(a_two[...].reshape(512, 2048), wu[:, :, :, at].reshape(2048, 256), (1, 0))
            up = jnp.where(used_units, jnp.maximum(up, 0.0), 0.0)
            low = (up * up).astype(BF16)
            act[:, :, :, at] = low.reshape(4, 2, 64, 256)
            act_gated[:, :, :, at] = (low.astype(F32) * gate_all).astype(BF16).reshape(4, 2, 64, 256)
            back = wide[:, at]
            up_low[:, :, :, at] = (back * gate_all * 2.0 * up).astype(BF16).reshape(4, 2, 64, 256)
            pairs = (low.astype(F32) * back).astype(BF16)
            gate_part[...] += dot(jnp.ones((8, 256), BF16), pairs, (1, 1))
            return carry

        lax.fori_loop(0, 4, one, 0)
        pending["gate"] = [links.go(gate_part, gate_near, links.partner)]

    merge_u = Merge(links, up_low, wu, set_b, merged_too)
    merge_f = Merge(links, act, wd, set_a, merged)

    def merge_u_out():
        merge_u.cross()
        wait("gate")
        gate_part[...] = gate_part[...] + gate_near[...]
        moves = [(gate_part.at[:, span(ring(z, k), 128)], gate_far.at[k - 1], links.zs[k]) for k in (1, 2, 3)]
        pending["gate"] = [links.together(moves, gate_far.at[pl.ds(0, 3)])]

    def merge_u_in():
        wait("gate")
        gate_far[3] = gate_part[:, span(z, 128)] + gate_far[0] + gate_far[1] + gate_far[2]
        info[2] = as_columns(gate_far[3])
        merge_u.arrive()

    def outer(left, right, target):
        def one(i, carry):
            part = left[:, :, :, span(i, 256)].reshape(512, 256)
            value = dot(part, right[...].reshape(512, right.shape[-1]), (0, 0)).astype(BF16)
            row, first = lax.div(i, 2), lax.rem(i, 2) * 2
            target[row, first] = value[0:128]
            target[row, first + 1] = value[128:256]
            return carry

        lax.fori_loop(0, 8, one, 0)

    def back_two():
        def step(i, rows):
            at = span(core * 4 + i, 16)
            upstream = upstream_in[rows, :].astype(F32)
            own, tile = tokens[z, at, :], info[1, rows, :]
            bucket, kept = own[:, 1:2], own[:, 2:3]
            inverse, gate = tile[:, 0:1], tile[:, 1:2]
            gate_grad = info[2, at, :][:, 0:1] * kept
            low = a_two[z, core, rows, :].astype(F32)
            grad = merge_u.rows(rows).astype(BF16).astype(F32)
            for b in range(4):
                hot = jnp.where(bucket == b, 1.0, 0.0)
                logit_grad = tile[:, 2 + b : 3 + b] * (hot - gate) * gate_grad
                grad = grad + logit_grad * small[b : b + 1, :]
                small_sum[b] += fold(logit_grad * low)
            scaled = n_two[rows, :]
            small_sum[5] += fold(grad * scaled)
            small_sum[7] += fold(grad)
            back = upstream + norm_back(scaled, inverse, small[5:6, :], grad)
            n_two[rows, :] = back
            hidden_low[z, core, rows, :] = back.astype(BF16)

        in_blocks(4, step)

    def mixed_back():
        d_mixed[...] = dot(hidden_low[...].reshape(512, 2048), wo[...].reshape(2048, 256), (1, 0)).astype(BF16)

    def attend_back():
        def one(index, carry):
            row, rows, (q_at, k_at, v_at), used = spots(index)
            share = probs[index]
            q, k, v = qkv[rows, q_at], qkv[rows, k_at], qkv[rows, v_at]
            grad = (d_mixed[rows, q_at].astype(F32) * used).astype(BF16)
            value_grad = dot(share.astype(BF16), grad, (0, 0))
            share_grad = dot(grad, v, (1, 1))
            inner = jnp.sum(share * share_grad, axis=-1, keepdims=True)
            score_grad = (share * (share_grad - inner)).astype(BF16)

            def rotate_back(value):
                return value * cosines[...] - turn(value * sines[...]) * jnp.where(lane < 64, -1.0, 1.0)

            def put(at, value):
                d_qkv[row, :, :, at] = value.astype(BF16).reshape(2, 64, 128)

            put(q_at, rotate_back(dot(score_grad, k, (1, 0)) * scale))
            put(k_at, rotate_back(dot(score_grad, q, (0, 0))))
            put(v_at, value_grad)
            return carry

        lax.fori_loop(0, 8, one, 0)

    merge_q = Merge(links, d_qkv, wq, set_b, merged_too)
    sums_u = Scatter(links, (wu, pl.ds(0, 512)), (wu, pl.ds(512, 512)), buffers[0:8])
    sums_d = Scatter(links, (grad_d, pl.ds(0, 512)), (grad_d, pl.ds(512, 512)), buffers[8:16])
    sums_q = Scatter(links, (grad_q, pl.ds(0, 384)), (grad_q, pl.ds(384, 384)), buffers[16:24])
    sums_o = Scatter(links, (wo, pl.ds(0, 128)), (wo, pl.ds(128, 128)), buffers[24:32])

    def output_rows():
        merge_f.arrive()

        def step(i, rows):
            kept = tokens[z, span(core * 4 + i, 16), :][:, 2:3]
            produced = merge_f.rows(rows).astype(BF16).astype(F32) * kept
            out_rows[rows, :] = (hidden[rows, :] + info[1, rows, :][:, 1:2] * produced).astype(BF16)

        in_blocks(4, step)
        here = block_out.at[own_64]
        pending["output"] = [keep(out_rows, here), links.go(out_rows, here, links.partner)]

    def back_one():
        merge_q.arrive()

        def step(i, rows):
            grad = merge_q.rows(rows)
            scaled, inverse = n_one[rows, :], info[0, rows, :][:, 0:1]
            small_sum[4] += fold(grad * scaled)
            small_sum[6] += fold(grad)
            n_two[rows, :] = n_two[rows, :] + norm_back(scaled, inverse, small[4:5, :], grad)

        in_blocks(4, step)
        for r in range(8):
            small[r : r + 1, :] = jnp.sum(small_sum[r], axis=0, keepdims=True)
        pending["small"] = [links.go(small, small_near, links.partner)]
        here = input_grad.at[own_64]
        pending["input"] = [keep(n_two, here), links.go(n_two, here, links.partner)]

    def small_to_x():
        wait("small")
        small[...] = small[...] + small_near[...]
        moves = [(small.at[:, span(ring(x, k), 512)], sx_in.at[k], links.xs[k]) for k in (1, 2, 3)]
        pending["small"] = [links.together(moves, sx_in.at[pl.ds(1, 3)])]

    def small_to_y():
        wait("small")
        sx_in[0] = small[:, span(x, 512)] + sx_in[1] + sx_in[2] + sx_in[3]
        moves = [(sx_in.at[0, :, span(ring(y, k), 128)], sy_in.at[k], links.ys[k]) for k in (1, 2, 3)]
        pending["small"] = [links.together(moves, sy_in.at[pl.ds(1, 3)])]

    def small_to_z():
        wait("small")
        sz_in[z] = sx_in[0, :, span(y, 128)] + sy_in[1] + sy_in[2] + sy_in[3]
        pending["small"] = to_all(sz_in.at[z], sz_in.at[pl.ds(0, 3)], links.zs)

    def small_done():
        wait("small")
        small_grad[...] = pltpu.roll(sz_in[0] + sz_in[1] + sz_in[2] + sz_in[3], 128 - 32 * z, 1)
        _, _, update = moment_step(
            router_w[...], small_grad[0:4, 0:32], router_m[...], router_v[...], DECAY_RATE
        )
        squares[8, 0:4, 0:32] = 0.5 * router_w[...] * router_w[...]
        squares[9, 0:4, 0:32] = 0.5 * update * update

    def owners_u():
        pending["own_u"] = to_group(
            pack_u.at[:, pl.ds(0, 3072)], lambda to: [(wu.at[x, y, span(to, 32), :], pack_u.at[:, span(z, 1024)])])

    def owners_d():
        pending["own_d"] = to_group(
            pack_d.at[:, pl.ds(0, 3072)], lambda to: [(grad_d.at[x, y, span(to, 32), :], pack_d.at[:, span(z, 1024)])])

    def owners_o():
        pending["own_o"] = to_group(
            pack_o.at[pl.ds(0, 6)],
            lambda to: [
                (wo.at[x, y, span(to, 32), pl.ds(128 * h, 128)], pack_o.at[2 * z + h]) for h in (0, 1)
            ]
        )

    def owners_q():
        pending["own_q"] = to_group(
            pack_q.at[pl.ds(0, 3)], lambda to: [(grad_q.at[x, y, span(to, 32), :], pack_q.at[z])])

    def moments_wide():
        for number, (name, first, second) in enumerate((("mom_u", up_m, up_v), ("mom_d", down_m, down_v))):
            sem = local_sems.at[local_used[0]]
            local_used[0] += 1
            for kind, ref in enumerate((first, second)):
                for c in range(4):
                    src = ref.at[:, pl.ds(1024 * c, 1024)]
                    dst = wide.at[pl.ds(256 * number + 128 * kind + 32 * c, 32)]
                    pltpu.make_async_copy(src, dst, sem).start()
            whole = wide.at[pl.ds(256 * number, 256)]
            pending[name] = [pltpu.make_async_copy(whole, whole, sem)]

    def squares_wide(number, weights, grads):
        def one(i, carry):
            rows, columns = span(lax.div(i, 4), 16), span(lax.rem(i, 4), 1024)
            weight = weights[rows, columns]
            at = lax.rem(i, 4) * 2 + lax.div(i, 4) + (number - 2) * 16
            _, _, update = moment_step(
                weight, grads[rows, columns].astype(F32), wide[span(at, 16), :], wide[span(at + 8, 16), :], DECAY_RATE
            )
            squares[2 * number] += fold_lanes(weight * weight)
            squares[2 * number + 1] += fold_lanes(update * update)
            return carry

        lax.fori_loop(0, 8, one, 0)

    def squares_u():
        wait("own_u")
        wait("mom_u")
        pending["results"].append(keep(pack_u, up_grad))
        squares_wide(2, own_u, pack_u)

    def squares_d():
        wait("own_d")
        wait("mom_d")
        pending["results"].append(keep(pack_d, down_grad))
        squares_wide(3, own_d, pack_d)

    def squares_o():
        wait("own_o")
        wait("mom_o")
        pending["results"].append(keep(pack_o, out_grad))

        def one(head, carry):
            weight = own_o[head]
            _, _, update = moment_step(
                weight, pack_o[head].astype(F32), mom_o[0, head], mom_o[1, head], DECAY_RATE
            )
            squares[2] += fold_lanes(weight * weight)
            squares[3] += fold_lanes(update * update)
            return carry

        lax.fori_loop(0, 8, one, 0)

    def squares_q():
        wait("own_q")
        wait("mom_q")
        for c in range(3):
            for head in range(8):
                at = 256 * c + 128 * (head % 2)
                qkv_grad[:, c, head, :] = pack_q[head // 2, :, at : at + 128].astype(F32)

        def one(i, carry):
            rows = pl.ds(i * 4, 4)
            weight = own_q[rows]
            _, _, update = moment_step(weight, qkv_grad[rows], mom_q[0, rows], mom_q[1, rows], DECAY_RATE)
            squares[0] += jnp.sum(jnp.sum(weight * weight, axis=0), axis=0)
            squares[1] += jnp.sum(jnp.sum(update * update, axis=0), axis=0)
            return carry

        lax.fori_loop(0, 8, one, 0)

    def totals():
        here = (4 * core + z, plane)
        sets = ((links.zs, links.others, {0: links.partner}), (links.xs, links.ys, links.across))
        tile = jnp.sum(squares[...], axis=1)
        for axis, count in enumerate((8, 16)):
            slots[axis, here[axis]] = tile
            for copy in to_all(slots.at[axis, here[axis]], slots.at[axis, pl.ds(0, count - 1)], *sets[axis]):
                copy.wait()
            tile = slots[axis, 0]
            for k in range(1, count):
                tile = tile + slots[axis, k]
        norms[...] = tile

    begin()
    slices_q()
    norm_one()
    pack_rest()
    small_x()
    slices_d()
    slices_o()
    wait("q")
    ring_q.advance()
    wait("o")
    ring_o.advance()
    token_columns()
    small_y()
    rows_branch_start()
    ring_q.advance()
    wait("d")
    ring_d.advance()
    small_rows()
    ring_o.advance()
    ring_q.advance()
    ring_d.advance()
    rows_one_start()
    rows_one.relay()
    ring_o.advance()
    ring_q.advance()
    slices_u()
    rows_one.finish()
    ring_o.advance()
    rows_branch.relay()
    wait("u")
    ring_u.advance()
    ring_d.advance()
    ring_q.advance()
    queries()
    attend(0, 4)
    attend(4, 8)
    ring_o.advance()
    merge_one.cross()
    ring_u.advance()
    merge_one.along()
    ring_u.advance()
    rows_branch.finish()
    merge_one.arrive()
    ring_d.advance()
    norm_two()
    rows_two_start()
    ring_u.advance()
    rows_two.relay()
    ring_d.advance()
    units_back()
    rows_two_finish()
    ring_u.advance()
    units()
    outer(branch, act_gated, grad_d)
    sums_d.advance()
    merge_u_out()
    merge_u.along()
    outer(a_two, up_low, wu)
    sums_u.advance()
    merge_f.cross()
    merge_f.along(leave=False)
    sums_d.advance()
    merge_u_in()
    back_two()
    rows_back.start()
    rows_back.relay()
    sums_u.advance()
    sums_d.advance()
    rows_back.finish()
    mixed_back()
    attend_back()
    merge_f.leave()
    sums_d.advance()
    sums_u.advance()
    outer(a_one, d_qkv, grad_q)
    sums_q.advance()
    merge_q.cross()
    merge_q.along()
    sums_d.advance()
    outer(hidden_low, mixed, wo)
    sums_o.advance()
    sums_q.advance()
    sums_o.advance()
    output_rows()
    sums_u.advance()
    sums_o.advance()
    sums_q.advance()
    owners_d()
    back_one()
    sums_u.advance()
    sums_o.advance()
    owners_u()
    sums_q.advance()
    moments_wide()
    small_to_x()
    squares_d()
    sums_o.advance()
    owners_o()
    sums_q.advance()
    owners_q()
    small_to_y()
    squares_u()
    squares_o()
    small_to_z()
    squares_q()
    small_done()
    totals()
    wait("output")
    wait("input")
    wait("results")


def layer(*operands):
    def vmem(*shape, kind=BF16):
        return pltpu.VMEM(shape, kind)

    def merge_buffers():
        return [vmem(TILES, 4, 64, TILE), vmem(TILES, 4, 64, TILE), vmem(3, TILES, 64, TILE)]

    def sum_buffers(width):
        return [
            vmem(2, 4, 64, width), vmem(2, 4, 128, width), vmem(2, 64, width), vmem(2, 128, width),
        ] * 2

    rows, rows_low, tokens = vmem(64, 2048, kind=F32), vmem(64, 2048), vmem(4, 2, 64, 2048)
    tile = vmem(4, 8, 128, kind=F32)
    return pl.pallas_call(
        layer_kernel,
        out_shape=(
            jax.ShapeDtypeStruct((128, 2048), BF16),
            jax.ShapeDtypeStruct((128, 2048), F32),
            jax.ShapeDtypeStruct((32, 3, 8, 128), F32),
            jax.ShapeDtypeStruct((8, 32, 128), BF16),
            jax.ShapeDtypeStruct((32, 4096), BF16),
            jax.ShapeDtypeStruct((32, 4096), BF16),
            jax.ShapeDtypeStruct((8, 128), F32),
            jax.ShapeDtypeStruct((16, 128), F32),
        ),
        in_specs=[ANY] * 14 + [VMEM] * 7 + [pl.BlockSpec(memory_space=pltpu.SMEM)] + [VMEM] * 3,
        out_specs=(ANY, ANY, VMEM, ANY, ANY, ANY, VMEM, VMEM),
        scratch_shapes=[
            vmem(32, 3, 8, 128, kind=F32), vmem(8, 32, 128, kind=F32), vmem(32, 4096, kind=F32),
            vmem(32, 4096, kind=F32),
            vmem(4, 32, 768), vmem(8, 32, 128), vmem(32, 4096), vmem(32, 4096),
            vmem(2, 32, 3, 8, 128, kind=F32), vmem(2, 8, 32, 128, kind=F32),
            vmem(4, 4, 128, 768), vmem(4, 4, 128, 256), vmem(4, 4, 128, 1024), vmem(4, 4, 128, 1024),
            vmem(4, 4, 128, 768), vmem(4, 4, 128, 1024),
            tile, vmem(4, 4, 8, 128, kind=F32), vmem(8, 2048, kind=F32), vmem(8, 2048, kind=F32),
            tile, vmem(4, 128, 128, kind=F32), vmem(4, 2, 8, 128, kind=F32), vmem(4, 128, 128, kind=F32),
            vmem(3, 128, 128, kind=F32),
            tokens, tokens, tokens, tokens,
            rows_low, rows_low, rows, rows, rows, rows, rows, rows_low,
            vmem(512, 1024, kind=F32), vmem(512, 768), vmem(8, 128, 128, kind=F32),
            vmem(4, 2, 64, 256), vmem(512, 256), vmem(4, 2, 64, 768), vmem(4, 2, 64, 1024), vmem(4, 2, 64, 1024), vmem(4, 2, 64, 1024),
            *merge_buffers(), *merge_buffers(),
            vmem(8, 512, kind=F32), vmem(8, 512, kind=F32), tile,
            vmem(8, 8, 2048, kind=F32), vmem(4, 8, 512, kind=F32), tile, tile,
            vmem(16, 8, 128, kind=F32), vmem(2, 16, 16, 128, kind=F32),
            *sum_buffers(512), *sum_buffers(512), *sum_buffers(384), *sum_buffers(128),
            DMA((LOCAL_COPIES,)), DMA((LINK_COPIES,)), DMA((LINK_COPIES,)),
        ],
        compiler_params=pltpu.CompilerParams(
            collective_id=0, has_side_effects=True, vmem_limit_bytes=63 * 2**20
        ),
        name="layer",
    )(*operands)


def renew_kernel(norms, small_grad, gains, biases, norm_m, norm_v, *refs):
    ins, outs = refs[:22], refs[22:]
    outs[31][...] = ins[20][...]
    outs[32][...] = ins[21][...]
    sums = jnp.sqrt(jnp.sum(norms[...], axis=1, keepdims=True))
    for index in range(5):
        weight, grad, m, v = (ref[...] for ref in ins[4 * index : 4 * index + 4])
        grad = grad[0:4, 0:32] if index == 4 else grad.astype(F32)
        first, second, update = moment_step(weight, grad, m, v, DECAY_RATE)
        ratio = LEARN_RATE * (sums[2 * index : 2 * index + 1, :] / sums[2 * index + 1 : 2 * index + 2, :])
        ratio = ratio.reshape((1,) * weight.ndim)
        new = weight - ratio * update
        for ref, value in zip(outs[5 * index : 5 * index + 5], (grad, first, second, new, new.astype(BF16))):
            ref[...] = value
    grad = small_grad[4:8, 0:32]
    master = jnp.concatenate([gains[...], biases[...]], axis=0)
    first, second, update = moment_step(master, grad, norm_m[...], norm_v[...], 0.0)
    new = master - NORM_RATE * update
    for ref, value in zip(outs[25:30], (grad, first, second, new, new.astype(BF16))):
        ref[...] = value
    row = lax.broadcasted_iota(jnp.int32, (8, 128), 0)
    lane = lax.broadcasted_iota(jnp.int32, (8, 128), 1)
    tile = jnp.zeros((8, 128), F32)
    for index in range(10):
        here = (row == index % 2) & (lane == index // 2)
        tile = jnp.where(here, sums[index : index + 1, :], tile)
    outs[30][...] = tile[0:2, 0:5]


def renew(norms, small_grad, gains, biases, norm_m, norm_v, *matrices):
    steps = 2

    def whole(shape):
        return pl.BlockSpec(shape, lambda i: (0,) * len(shape))

    blocks = (
        pl.BlockSpec((32 // steps, 3, 8, 128), lambda i: (i, 0, 0, 0)),
        pl.BlockSpec((8 // steps, 32, 128), lambda i: (i, 0, 0)),
        pl.BlockSpec((32, 4096 // steps), lambda i: (0, i)),
        pl.BlockSpec((32, 4096 // steps), lambda i: (0, i)),
        whole((4, 32)),
    )
    shapes = ((32, 3, 8, 128), (8, 32, 128), (32, 4096), (32, 4096), (4, 32), (4, 32))
    in_specs = [whole((16, 128)), whole((8, 128)), whole((2, 32)), whole((2, 32)), whole((4, 32)), whole((4, 32))]
    out_specs, out_shape = [], []
    for index, block in enumerate(blocks):
        in_specs += [block, whole((8, 128)) if index == 4 else block, block, block]
    for block, shape in zip((*blocks, whole((4, 32))), shapes):
        out_specs += [block] * 5
        out_shape += [jax.ShapeDtypeStruct(shape, kind) for kind in (F32, F32, F32, F32, BF16)]
    out_specs.append(whole((2, 5)))
    out_shape.append(jax.ShapeDtypeStruct((2, 5), F32))
    rows = pl.BlockSpec((128 // steps, 2048), lambda i: (i, 0))
    in_specs += [rows, rows]
    out_specs += [rows, rows]
    out_shape += [jax.ShapeDtypeStruct((128, 2048), kind) for kind in (BF16, F32)]
    return pl.pallas_call(
        renew_kernel,
        grid=(steps,),
        in_specs=in_specs,
        out_specs=out_specs,
        out_shape=out_shape,
        compiler_params=pltpu.CompilerParams(vmem_limit_bytes=63 * 2**20),
        name="renew",
    )(norms, small_grad, gains, biases, norm_m, norm_v, *matrices)


def rotary_tables(length, size):
    half_size = size // 2
    frequency = ROPE_BASE ** (-(np.arange(half_size) * 2.0 / size))
    angles = np.arange(length)[:, None] * frequency[None, :]
    cosine_table = np.concatenate([np.cos(angles), np.cos(angles)], axis=-1)
    sine_table = np.concatenate([np.sin(angles), np.sin(angles)], axis=-1)
    return (cosine_table.astype(np.float32), sine_table.astype(np.float32))


def local(
    block_input,
    cotangent,
    head_count,
    width_route,
    forced_width,
    slot_index,
    qkv_weight,
    out_weight,
    up_weight,
    down_weight,
    router_weight,
    norm_gains,
    norm_biases,
    qkv_first,
    qkv_second,
    out_first,
    out_second,
    up_first,
    up_second,
    down_first,
    down_second,
    router_first,
    router_second,
    norm_first,
    norm_second,
):
    def turned(value):
        return value.transpose(0, 2, 1)

    out = turned(out_weight), turned(out_first), turned(out_second)
    down = down_weight.T, down_first.T, down_second.T
    router = router_weight.T, router_first.T, router_second.T
    block_output, input_grad, *grads, small_grad, norms = layer(
        qkv_weight, out[0], up_weight, down[0],
        qkv_first, qkv_second, *out[1:], up_first, up_second, *down[1:],
        block_input, cotangent, *router, norm_gains, norm_biases,
        head_count.reshape(1, -1), width_route.reshape(1, -1), forced_width, slot_index.reshape(1, -1),
        *rotary_tables(128, 128),
    )
    *results, lamb_norms, block_output, input_grad = renew(
        norms, small_grad, norm_gains, norm_biases, norm_first, norm_second,
        qkv_weight, grads[0], qkv_first, qkv_second,
        out[0], grads[1], *out[1:],
        up_weight, grads[2], up_first, up_second,
        down[0], grads[3], *down[1:],
        router[0], small_grad, *router[1:],
        block_output, input_grad,
    )
    kinds = []
    for kind in range(5):
        qkv, out, up, down, router, norm = (results[5 * index + kind] for index in range(6))
        kinds += [qkv, turned(out), up, down.T, router.T, norm]
    return (block_output, input_grad, *kinds, lamb_norms.T)


def solution(mesh):
    qkv, out = P("dp", None, "mp", None), P("mp", None, "dp")
    up, down, router, norms = P("dp", "mp"), P("mp", "dp"), P("dp", None), P(None, "dp")
    rows, tokens = P("dp", None), P("dp")
    matrices = (qkv, out, up, down, router)
    return jax.shard_map(
        local,
        mesh=mesh,
        in_specs=(
            rows, rows, tokens, tokens, tokens, tokens,
            *matrices, norms, norms,
            qkv, qkv, out, out, up, up, down, down, router, router, norms, norms,
        ),
        out_specs=(rows, rows, *((*matrices, norms) * 5), P()),
        check_vma=False,
    )
```

```python
import jax
import jax.numpy as jnp
import numpy as np
from jax import lax
from jax.experimental import pallas as pl
from jax.experimental.pallas import tpu as pltpu
from jax.sharding import PartitionSpec as P

STEP = 5

BETA_ONE = 0.5
BETA_TWO = 0.5
ADAM_EPS = 1e-06
DECAY_RATE = 0.01
LEARN_RATE = 0.5
NORM_RATE = 0.1
NORM_EPS = 1e-05
ROPE_BASE = 10000.0

MESH = pl.DeviceIdType.MESH
BF16 = jnp.bfloat16
F32 = jnp.float32
VMEM = pl.BlockSpec(memory_space=pltpu.VMEM)
ANY = pl.BlockSpec(memory_space=pl.ANY)
DMA = pltpu.SemaphoreType.DMA
ALL = slice(None)
LOW, HIGH = pl.ds(0, 64), pl.ds(64, 64)


def place():
    index = lax.axis_index("dp")
    return lax.div(index, 16), lax.rem(lax.div(index, 4), 4), lax.rem(index, 4), lax.axis_index("mp")


def ring(value, step):
    return lax.rem(value + (step + 4), 4)


def device(x, y, z, core):
    return (x * 16 + y * 4 + z, core)


def greet(peers):
    barrier = pltpu.get_barrier_semaphore()
    for peer in peers:
        pl.semaphore_signal(barrier, inc=1, device_id=peer, device_id_type=MESH)
    return lambda: pl.semaphore_wait(barrier, len(peers))


def send(src, dst, send_sem, recv_sem, peer):
    copy = pltpu.make_async_remote_copy(
        src_ref=src, dst_ref=dst, send_sem=send_sem, recv_sem=recv_sem, device_id=peer, device_id_type=MESH
    )
    copy.start()
    return copy


def span(index, size):
    return pl.ds(pl.multiple_of(index * size, size), size)


def dot(left, right, dims):
    return lax.dot_general(left, right, ((dims[:1], dims[1:]), ((), ())), preferred_element_type=F32)


class Links:
    def __init__(self, send_sems, recv_sems):
        self.x, self.y, self.z, self.core = x, y, z, core = place()
        self.xs = {k: device(ring(x, k), y, z, core) for k in (1, 2, 3)}
        self.ys = {k: device(x, ring(y, k), z, core) for k in (1, 2, 3)}
        self.zs = {k: device(x, y, ring(z, k), core) for k in (1, 2, 3)}
        self.others = {k: device(x, y, ring(z, k), 1 - core) for k in (1, 2, 3)}
        self.across = {(i, j): device(ring(x, i), ring(y, j), z, core) for i in (1, 2, 3) for j in (1, 2, 3)}
        self.partner = device(x, y, z, 1 - core)
        self.send_sems, self.recv_sems, self.used = send_sems, recv_sems, 0

    def go(self, src, dst, peer):
        number = self.used
        self.used += 1
        return send(src, dst, self.send_sems.at[number], self.recv_sems.at[number], peer)

    def bundle(self, whole):
        number = self.used
        self.used += 1
        return Bundle(whole, self.send_sems.at[number], self.recv_sems.at[number])

    def together(self, moves, whole):
        bundle = self.bundle(whole)
        for move in moves:
            bundle.go(*move)
        return bundle


class Bundle:
    def __init__(self, whole, *sems):
        self.whole, self.sems = whole, sems

    def go(self, src, dst, peer):
        send(src, dst, *self.sems, peer)

    def wait(self):
        for sem in self.sems:
            pltpu.make_async_copy(self.whole, self.whole, sem).wait()


class Gather:
    def __init__(self, links, first, second):
        self.links, self.parts, self.number, self.copies = links, (first, second), 0, []

    def advance(self):
        for copy in self.copies:
            copy.wait()
        x, y = self.links.x, self.links.y
        xp, xm, yp, ym = self.links.xs[1], self.links.xs[3], self.links.ys[1], self.links.ys[3]
        xb, xa, yb, ya = ring(x, -1), ring(x, 1), ring(y, -1), ring(y, 1)
        moves = {
            0: (((x, y, ALL), xp), ((x, y, ALL), xm), ((x, y, ALL), yp), ((x, y, ALL), ym)),
            1: (((xb, y, LOW), xp), ((xa, y, HIGH), xm), ((x, yb, LOW), yp), ((x, ya, HIGH), ym)),
            2: (((ALL, y, ALL), yp), ((ALL, y, ALL), ym), ((x, ALL, ALL), xp), ((x, ALL, ALL), xm)),
            3: (((ALL, yb, LOW), yp), ((ALL, ya, HIGH), ym), ((xb, ALL, LOW), xp), ((xa, ALL, HIGH), xm)),
        }.get(self.number, ())
        if moves:
            pairs = [(self.parts[index // 2][0].at[where + (self.parts[index // 2][1],)], peer)
                     for index, (where, peer) in enumerate(moves)]
            ref, columns = self.parts[0]
            whole = (
                ref.at[0, :, :, columns], ref.at[0, pl.ds(0, 2), :, columns],
                ref.at[:, :, :, columns], ref.at[pl.ds(0, 2), :, :, columns],
            )[self.number]
            self.copies = [self.links.together([(block, block, peer) for block, peer in pairs], whole)]
        else:
            self.copies = []
        self.number += 1


def add_into(ref, blocks, columns, sources, row, count):
    steps = count // 16

    def one(index, carry):
        number = lax.div(index, steps)
        step = pl.multiple_of(lax.rem(index, steps) * 16, 16)
        to = blocks[1](number) + (pl.ds(row + step, 16), columns)
        here = ref[to].astype(F32)
        for source, first_row in sources:
            place_in = ((number,) if blocks[0] > 1 else ()) + (pl.ds(first_row + step, 16), ALL)
            here = here + source[place_in].astype(F32)
        ref[to] = here.astype(BF16)
        return carry

    lax.fori_loop(0, blocks[0] * steps, one, 0)


class Scatter:
    def __init__(self, links, first, second, buffers):
        self.links, self.parts = links, (first, second)
        self.buffers = (buffers[:4], buffers[4:])
        self.number, self.halves, self.rest = 0, [], []

    def lanes(self, phase):
        x, y = self.links.x, self.links.y
        found = []
        for part in (0, 1):
            ref, columns = self.parts[part]
            along_y = part == phase
            peers = self.links.ys if along_y else self.links.xs
            if phase == 0 and along_y:
                where, count, each = (lambda k: (ALL, ring(y, k))), 4, (lambda k: lambda i: (i, ring(y, k)))
            elif phase == 0:
                where, count, each = (lambda k: (ring(x, k), ALL)), 4, (lambda k: lambda i: (ring(x, k), i))
            elif along_y:
                where, count, each = (lambda k: (x, ring(y, k))), 1, (lambda k: lambda i: (x, ring(y, k)))
            else:
                where, count, each = (lambda k: (ring(x, k), y)), 1, (lambda k: lambda i: (ring(x, k), y))
            one, two = self.buffers[part][2 * phase : 2 * phase + 2]
            found.append((ref, columns, where, count, each, peers, one, two))
        return found

    def begin(self, phase):
        self.halves, self.rest = [], []
        links = self.links
        for ref, columns, where, count, each, peers, one, two in self.lanes(phase):
            self.halves.append(links.go(ref.at[where(2) + (LOW, columns)], one.at[0], peers[1]))
            self.halves.append(links.go(ref.at[where(2) + (HIGH, columns)], one.at[1], peers[3]))
        moves = []
        for ref, columns, where, count, each, peers, one, two in self.lanes(phase):
            lead = (ALL,) if count > 1 else ()
            moves.append((ref.at[where(1) + (HIGH, columns)], two.at[(0,) + lead + (HIGH,)], peers[1]))
            moves.append((ref.at[where(-1) + (LOW, columns)], two.at[(1,) + lead + (LOW,)], peers[3]))
        self.rest.append(links.together(moves, self.buffers[0][2 * phase + 1]))

    def middle(self, phase):
        lanes, last = self.lanes(phase), self.links.bundle(self.buffers[0][2 * phase + 1])
        self.rest.append(last)
        for side in (0, 1):
            for part in (0, 1):
                ref, columns, where, count, each, peers, one, two = lanes[part]
                lead = (ALL,) if count > 1 else ()
                step, rows, row = ((1, LOW, 0), (-1, HIGH, 64))[side]
                self.halves[2 * part + side].wait()
                add_into(ref, (count, each(step)), columns, [(one.at[side], 0)], row, 64)
                last.go(
                    ref.at[where(step) + (rows, columns)], two.at[(side,) + lead + (rows,)], peers[(1, 3)[side]]
                )

    def end(self, phase):
        for copy in self.rest:
            copy.wait()
        for ref, columns, where, count, each, peers, one, two in self.lanes(phase):
            add_into(ref, (count, each(0)), columns, [(two.at[0], 0), (two.at[1], 0)], 0, 128)

    def advance(self):
        if self.number == 0:
            self.begin(0)
        elif self.number == 1:
            self.middle(0)
        elif self.number == 2:
            self.end(0)
            self.begin(1)
        elif self.number == 3:
            self.middle(1)
        elif self.number == 4:
            self.end(1)
        self.number += 1


class Spread:
    def __init__(self, links, ref):
        self.links, self.ref = links, ref

    def start(self, own=True):
        links = self.links
        here = self.ref.at[links.z, links.core]
        self.passed = links.bundle(self.ref.at[pl.ds(0, 4 if own else 3), 0])
        if own:
            self.passed.go(here, here, links.partner)
        self.flying = [links.go(here, here, links.zs[k]) for k in (1, 3)]

    def relay(self):
        links = self.links
        self.far = links.bundle(self.ref.at[0, 0])
        for side, k, rows in ((0, 1, pl.ds(0, 32)), (1, 3, pl.ds(32, 32))):
            self.flying[side].wait_recv()
            block = self.ref.at[ring(links.z, -k), links.core]
            half = block.at[rows]
            self.far.go(half, half, links.zs[k])
            self.passed.go(block, block, links.partner)

    def finish(self):
        links = self.links
        self.far.wait()
        block = self.ref.at[ring(links.z, 2), links.core]
        self.passed.go(block, block, links.partner)
        for copy in self.flying:
            copy.wait_send()
        self.passed.wait()


TILES, TILE = 4, 512


class Merge:
    def __init__(self, links, left, weights, buffers, out):
        self.links, self.left, self.weights, self.out = links, left, weights, out
        self.near, self.near_in, self.far_in, self.tmp = buffers
        self.crossing, self.flying = [], None

    def tile(self, half, j):
        rows = self.weights[j]
        left = self.left[:, half]
        return dot(left.reshape(256, left.shape[-1]), rows.reshape(TILE, rows.shape[-1]), (1, 1))

    def cross(self):
        for j in range(TILES):
            self.near[j] = self.tile(1 - self.links.core, j).astype(BF16).reshape(4, 64, TILE)
            self.crossing.append(self.links.go(self.near.at[j], self.near_in.at[j], self.links.partner))

    def along(self, leave=True):
        for j in range(TILES):
            value = self.tile(self.links.core, j)
            self.crossing[j].wait()
            value = value + self.near_in[j].astype(F32).reshape(256, TILE)
            self.tmp[0:256, 0:TILE] = value
            self.near[j] = value.astype(BF16).reshape(4, 64, TILE)
            if leave:
                self.leave(j)
            self.out[:, TILE * j : TILE * j + TILE] = self.tmp[span(self.links.z, 64), 0:TILE]

    def leave(self, j=ALL):
        links = self.links
        if self.flying is None:
            self.flying = links.bundle(self.far_in)
        for k in (2, 1, 3):
            self.flying.go(self.near.at[j, ring(links.z, k)], self.far_in.at[k - 1, j], links.zs[k])

    def arrive(self):
        self.flying.wait()

    def rows(self, rows):
        value = self.out[rows, :]
        for k in range(3):
            parts = [self.far_in[k, j, rows, :] for j in range(TILES)]
            value = value + jnp.concatenate(parts, axis=1).astype(F32)
        return value


def norm_parts(value):
    centre = value - jnp.mean(value, axis=-1, keepdims=True)
    inverse = lax.rsqrt(jnp.mean(centre * centre, axis=-1, keepdims=True) + NORM_EPS)
    return centre * inverse, inverse


def norm_back(scaled, inverse, gain_row, upstream):
    dscaled = upstream * gain_row
    inner = (
        dscaled
        - jnp.mean(dscaled, axis=-1, keepdims=True)
        - scaled * jnp.mean(dscaled * scaled, axis=-1, keepdims=True)
    )
    return inner * inverse


def fold(value):
    return value[0:8, :] + value[8:16, :]


def fold_lanes(value):
    total = None
    for row in range(0, value.shape[0], 8):
        for lane in range(0, value.shape[1], 128):
            part = value[row : row + 8, lane : lane + 128]
            total = part if total is None else total + part
    return total


def columns_tile(columns):
    lane = lax.broadcasted_iota(jnp.int32, (16, 128), 1)
    tile = jnp.zeros((16, 128), F32)
    for index, column in enumerate(columns):
        tile = jnp.where(lane == index, column, tile)
    return tile


def as_columns(rows):
    return jnp.concatenate([rows, jnp.zeros((120, 128), F32)], axis=0).T


def turn(value):
    return pltpu.roll(value, 64, 1)


def moment_step(weight, gradient, first_moment, second_moment, decay_rate):
    first_moment = BETA_ONE * first_moment + (1.0 - BETA_ONE) * gradient
    second_moment = BETA_TWO * second_moment + (1.0 - BETA_TWO) * gradient * gradient
    one, two = 1.0 / (1.0 - BETA_ONE**STEP), 1.0 / (1.0 - BETA_TWO**STEP)
    update = (first_moment * one) / (jnp.sqrt(second_moment * two) + ADAM_EPS) + decay_rate * weight
    return (first_moment, second_moment, update)


LINK_COPIES = 123
LOCAL_COPIES = 29


def layer_kernel(
    qkv_w, out_w, up_w, down_w, qkv_m, qkv_v, out_m, out_v, up_m, up_v, down_m, down_v, block_in, cotangent,
    router_w, router_m, router_v, gains, biases, head_count, width_route, forced_width, slot_index, cosines, sines,
    block_out, input_grad, qkv_grad, out_grad, up_grad, down_grad, small_grad, norms,
    own_q, own_o, own_u, own_d, pack_q, pack_o, pack_u, pack_d, mom_q, mom_o,
    wq, wo, wu, wd, grad_q, grad_d, small_slots, small_grid, small, small_near,
    token_rows, tokens, gate_slots, gates, info,
    a_one, a_two, branch, hidden_low,
    rows_in, upstream_in, hidden, n_one, n_two, merged, merged_too, out_rows,
    wide, qkv, probs, mixed, d_mixed, d_qkv, act, act_gated, up_low,
    near_a, near_in_a, far_in_a, near_b, near_in_b, far_in_b,
    gate_part, gate_near, gate_far, small_sum, sx_in, sy_in, sz_in, squares, slots,
    *rest,
):
    buffers, (local_sems, send_sems, recv_sems) = rest[:-3], rest[-3:]
    links = Links(send_sems, recv_sems)
    x, y, z, core = links.x, links.y, links.z, links.core
    own_32, own_64, plane = span(z, 32), span(core, 64), 4 * x + y
    set_a = (near_a, near_in_a, far_in_a, wide)
    set_b = (near_b, near_in_b, far_in_b, wide)
    local_used, pending = [0], {"results": []}

    def keep(src, dst):
        copy = pltpu.make_async_copy(src, dst, local_sems.at[local_used[0]])
        local_used[0] += 1
        copy.start()
        return copy

    def wait(name):
        for copy in pending.pop(name):
            copy.wait()

    def in_blocks(count, step):
        def one(i, carry):
            step(i, span(i, 16))
            return carry

        lax.fori_loop(0, count, one, 0, unroll=2)

    def to_group(whole, moves):
        bundle = links.bundle(whole)
        for k in (2, 1, 3):
            for src, dst in moves(ring(z, k)):
                bundle.go(src, dst, links.zs[k])
        return [bundle, *(keep(src, dst) for src, dst in moves(z))]

    def to_all(here, whole, *sets):
        return [links.together([(here, here, peer) for peers in sets for peer in peers.values()], whole)]

    def begin():
        greeted = greet(
            [peer for peers in (links.xs, links.ys, links.across, links.zs, links.others) for peer in peers.values()]
            + [links.partner]
        )
        loads = [keep(qkv_w, own_q), keep(out_w, own_o), keep(up_w, own_u), keep(down_w, own_d)]
        pending["rows"] = [keep(block_in.at[own_64], rows_in), keep(cotangent.at[own_64], upstream_in)]
        pending["branch"] = [keep(cotangent.at[pl.ds(64 * h, 64)], branch.at[z, h]) for h in (0, 1)]
        pending["mom_q"] = [keep(qkv_m, mom_q.at[0]), keep(qkv_v, mom_q.at[1])]
        pending["mom_o"] = [keep(out_m, mom_o.at[0]), keep(out_v, mom_o.at[1])]
        small_slots[z] = jnp.zeros((8, 128), F32)
        small_slots[z, 0:4, 0:32] = router_w[...].astype(BF16).astype(F32)
        small_slots[z, 4:6, 0:32] = gains[...].astype(BF16).astype(F32)
        small_slots[z, 6:8, 0:32] = biases[...].astype(BF16).astype(F32)
        small_slots[z] = pltpu.roll(small_slots[z], 32 * z, 1)
        bucket_row = jnp.where(forced_width[0] < 4, forced_width[0], width_route[...])
        token_rows[z] = jnp.zeros((8, 128), F32)
        token_rows[z, 0:1, :] = head_count[...].astype(F32)
        token_rows[z, 1:2, :] = bucket_row.astype(F32)
        token_rows[z, 2:3, :] = jnp.where(slot_index[...] >= 0, 1.0, 0.0)
        loads[0].wait()
        for c in range(3):
            for head in range(8):
                at = 256 * c + 128 * (head % 2)
                pack_q[head // 2, :, at : at + 128] = own_q[:, c, head, :].astype(BF16)
        pending["loads"] = loads[1:]
        greeted()

    def pack_rest():
        wait("loads")

        def pack(i, rows):
            pack_u[rows, :] = own_u[rows, :].astype(BF16)
            pack_d[rows, :] = own_d[rows, :].astype(BF16)
            for head in range(8):
                pack_o[head, rows, :] = own_o[head, rows, :].astype(BF16)

        in_blocks(2, pack)
        gates[z] = jnp.zeros((128, 128), F32)
        gate_part[...] = jnp.zeros_like(gate_part)
        small_sum[...] = jnp.zeros_like(small_sum)
        squares[...] = jnp.zeros_like(squares)

    ring_q = Gather(links, (wq, pl.ds(0, 384)), (wq, pl.ds(384, 384)))
    ring_o = Gather(links, (wo, pl.ds(0, 128)), (wo, pl.ds(128, 128)))
    ring_d = Gather(links, (wd, pl.ds(0, 512)), (wd, pl.ds(512, 512)))
    ring_u = Gather(links, (wu, pl.ds(0, 512)), (wu, pl.ds(512, 512)))

    def slices_q():
        pending["q"] = to_group(
            pack_q.at[pl.ds(0, 3)], lambda to: [(pack_q.at[to], wq.at[x, y, own_32, :])])
        pending["small"] = to_all(small_slots.at[z], small_slots.at[pl.ds(0, 3)], links.zs)
        pending["tokens"] = to_all(token_rows.at[z], token_rows.at[pl.ds(0, 3)], links.zs)

    def slices_o():
        pending["o"] = to_group(
            pack_o.at[pl.ds(0, 6)],
            lambda to: [(pack_o.at[2 * to + h], wo.at[x, y, own_32, pl.ds(128 * h, 128)]) for h in (0, 1)]
        )

    def slices_d():
        pending["d"] = to_group(
            pack_d.at[:, pl.ds(0, 3072)], lambda to: [(pack_d.at[:, span(to, 1024)], wd.at[x, y, own_32, :])])

    def slices_u():
        pending["u"] = to_group(
            pack_u.at[:, pl.ds(0, 3072)], lambda to: [(pack_u.at[:, span(to, 1024)], wu.at[x, y, own_32, :])])

    def small_x():
        wait("small")
        small_grid[x, y] = small_slots[0] + small_slots[1] + small_slots[2] + small_slots[3]
        pending["small"] = to_all(small_grid.at[x, y], small_grid.at[0, pl.ds(0, 3)], links.xs)

    def small_y():
        wait("small")
        pending["small"] = to_all(small_grid.at[:, y], small_grid.at[:, pl.ds(0, 3)], links.ys)

    def small_rows():
        wait("small")
        for p in range(16):
            small[:, 128 * p : 128 * p + 128] = small_grid[p // 4, p % 4]

    def token_columns():
        wait("tokens")
        for row in range(4):
            tokens[row] = as_columns(token_rows[row])

    rows_one, rows_branch = Spread(links, a_one), Spread(links, branch)
    rows_two, rows_back = Spread(links, a_two), Spread(links, hidden_low)

    def norm_one():
        wait("rows")

        def step(i, rows):
            scaled, inverse = norm_parts(rows_in[rows, :].astype(F32))
            n_one[rows, :] = scaled
            info[0, rows, :] = columns_tile([inverse])

        in_blocks(4, step)

    def rows_branch_start():
        wait("branch")
        rows_branch.start(own=False)

    def rows_one_start():
        def step(i, rows):
            a_one[z, core, rows, :] = (n_one[rows, :] * small[4:5, :] + small[6:7, :]).astype(BF16)

        in_blocks(4, step)
        rows_one.start()

    lane = lax.broadcasted_iota(jnp.int32, (128, 128), 1)
    causal = lax.broadcasted_iota(jnp.int32, (128, 128), 0) >= lane
    scale = 128 ** (-0.5)

    def queries():
        for c in range(3):
            part = wq[:, :, :, 256 * c : 256 * c + 256].reshape(2048, 256)
            wide[:, 256 * c : 256 * c + 256] = dot(a_one[...].reshape(512, 2048), part, (1, 0))

    def spots(row, head):
        used = jnp.where((core * 8 + z * 2 + head).astype(F32) < tokens[row][:, 0:1], 1.0, 0.0)
        return span(row, 128), [pl.ds(128 * (2 * c + head), 128) for c in range(3)], used

    def attend(first):
        turned_sines = jnp.where(lane < 64, -sines[...], sines[...])

        def rotate(value):
            return value * cosines[...] + turn(value) * turned_sines

        found = []
        for row, head in [(first + r, h) for r in (0, 1) for h in (0, 1)]:
            rows, spots_at, used = spots(row, head)
            q_at, k_at, v_at = spots_at
            q = (rotate(wide[rows, q_at]) * scale).astype(BF16)
            k = rotate(wide[rows, k_at]).astype(BF16)
            v = wide[rows, v_at].astype(BF16)
            scores = jnp.where(causal, dot(q, k, (1, 1)), -1e30)
            powers = jnp.exp(scores - jnp.max(scores, axis=-1, keepdims=True))
            share = powers / jnp.sum(powers, axis=-1, keepdims=True)
            heads = (dot(share.astype(BF16), v, (1, 0)) * used).astype(BF16)
            found.append((row, head, rows, spots_at, (q, k, v), share, heads))
        for row, head, rows, spots_at, values, share, heads in found:
            for at, value in zip(spots_at, values):
                qkv[rows, at] = value
            probs[2 * row + head] = share
            mixed[row, :, :, spots_at[0]] = heads.reshape(2, 64, 128)

    merge_one = Merge(links, mixed, wo, set_a, merged)

    def norm_two():
        def step(i, rows):
            value = rows_in[rows, :].astype(F32) + merge_one.rows(rows)
            hidden[rows, :] = value
            scaled, inverse = norm_parts(value)
            n_two[rows, :] = scaled
            low = (scaled * small[5:6, :] + small[7:8, :]).astype(BF16)
            a_two[z, core, rows, :] = low
            low = low.astype(F32)
            logits = [jnp.sum(low * small[b : b + 1, :], axis=-1, keepdims=True) for b in range(4)]
            top = jnp.maximum(jnp.maximum(logits[0], logits[1]), jnp.maximum(logits[2], logits[3]))
            powers = [jnp.exp(logit - top) for logit in logits]
            whole = powers[0] + powers[1] + powers[2] + powers[3]
            chances = [power / whole for power in powers]
            at = span(core * 4 + i, 16)
            own = tokens[z, at, :]
            bucket, kept = own[:, 1:2], own[:, 2:3]
            gate = jnp.zeros_like(bucket)
            for b in range(4):
                gate = jnp.where(bucket == b, chances[b], gate)
            info[1, rows, :] = columns_tile([inverse, gate, *chances])
            gates[z, at, :] = columns_tile([gate * kept])

        in_blocks(4, step)

    def rows_two_start():
        rows_two.start()
        gate_slots[z, core] = gates[z].T[0:8, :]
        whole = slots.at[0, pl.ds(0, 7), pl.ds(0, 8)]
        pending["gates"] = to_all(gate_slots.at[z, core], whole, links.zs, links.others, {0: links.partner})

    def rows_two_finish():
        rows_two.finish()
        wait("gates")
        for row in range(4):
            gates[row] = as_columns(gate_slots[row, 0] + gate_slots[row, 1])

    def units_back():
        def one(t, carry):
            at = span(t, 256)
            wide[:, at] = dot(branch[...].reshape(512, 2048), wd[:, :, :, at].reshape(2048, 256), (1, 0))
            return carry

        lax.fori_loop(0, 4, one, 0)

    def units():
        quarter = (core * 2 + lax.div(z, 2)).astype(F32)
        used_units = tokens[...].reshape(512, 128)[:, 1:2] >= quarter
        gate_all = gates[...].reshape(512, 128)[:, 0:1]

        def one(t, carry):
            at = span(t, 256)
            up = dot(a_two[...].reshape(512, 2048), wu[:, :, :, at].reshape(2048, 256), (1, 0))
            up = jnp.where(used_units, jnp.maximum(up, 0.0), 0.0)
            low = (up * up).astype(BF16)
            act[:, :, :, at] = low.reshape(4, 2, 64, 256)
            act_gated[:, :, :, at] = (low.astype(F32) * gate_all).astype(BF16).reshape(4, 2, 64, 256)
            back = wide[:, at]
            up_low[:, :, :, at] = (back * gate_all * 2.0 * up).astype(BF16).reshape(4, 2, 64, 256)
            pairs = (low.astype(F32) * back).astype(BF16)
            gate_part[...] += dot(jnp.ones((8, 256), BF16), pairs, (1, 1))
            return carry

        lax.fori_loop(0, 4, one, 0)
        pending["gate"] = [links.go(gate_part, gate_near, links.partner)]

    merge_u = Merge(links, up_low, wu, set_b, merged_too)
    merge_f = Merge(links, act, wd, set_a, merged)

    def merge_u_out():
        merge_u.cross()
        wait("gate")
        gate_part[...] = gate_part[...] + gate_near[...]
        moves = [(gate_part.at[:, span(ring(z, k), 128)], gate_far.at[k - 1], links.zs[k]) for k in (1, 2, 3)]
        pending["gate"] = [links.together(moves, gate_far.at[pl.ds(0, 3)])]

    def merge_u_in():
        wait("gate")
        gate_far[3] = gate_part[:, span(z, 128)] + gate_far[0] + gate_far[1] + gate_far[2]
        info[2] = as_columns(gate_far[3])
        merge_u.arrive()

    def outer(left, right, target):
        def one(i, carry):
            part = left[:, :, :, span(i, 512)].reshape(512, 512)
            value = dot(part, right[...].reshape(512, right.shape[-1]), (0, 0)).astype(BF16)
            target[i] = value.reshape(4, 128, right.shape[-1])
            return carry

        lax.fori_loop(0, 4, one, 0)

    def back_two():
        def step(i, rows):
            at = span(core * 4 + i, 16)
            upstream = upstream_in[rows, :].astype(F32)
            own, tile = tokens[z, at, :], info[1, rows, :]
            bucket, kept = own[:, 1:2], own[:, 2:3]
            inverse, gate = tile[:, 0:1], tile[:, 1:2]
            gate_grad = info[2, at, :][:, 0:1] * kept
            low = a_two[z, core, rows, :].astype(F32)
            grad = merge_u.rows(rows).astype(BF16).astype(F32)
            for b in range(4):
                hot = jnp.where(bucket == b, 1.0, 0.0)
                logit_grad = tile[:, 2 + b : 3 + b] * (hot - gate) * gate_grad
                grad = grad + logit_grad * small[b : b + 1, :]
                small_sum[b] += fold(logit_grad * low)
            scaled = n_two[rows, :]
            small_sum[5] += fold(grad * scaled)
            small_sum[7] += fold(grad)
            back = upstream + norm_back(scaled, inverse, small[5:6, :], grad)
            n_two[rows, :] = back
            hidden_low[z, core, rows, :] = back.astype(BF16)

        in_blocks(4, step)

    def mixed_back():
        d_mixed[...] = dot(hidden_low[...].reshape(512, 2048), wo[...].reshape(2048, 256), (1, 0)).astype(BF16)

    def attend_back():
        def rotate_back(value):
            return value * cosines[...] - turn(value * sines[...]) * jnp.where(lane < 64, -1.0, 1.0)

        def one(pair, carry):
            found = []
            for row, head in [(2 * pair + r, h) for r in (0, 1) for h in (0, 1)]:
                rows, (q_at, k_at, v_at), used = spots(row, head)
                share = probs[2 * row + head]
                q, k, v = qkv[rows, q_at], qkv[rows, k_at], qkv[rows, v_at]
                grad = (d_mixed[rows, q_at].astype(F32) * used).astype(BF16)
                value_grad = dot(share.astype(BF16), grad, (0, 0))
                share_grad = dot(grad, v, (1, 1))
                inner = jnp.sum(share * share_grad, axis=-1, keepdims=True)
                score_grad = (share * (share_grad - inner)).astype(BF16)
                found.append((row, q_at, rotate_back(dot(score_grad, k, (1, 0)) * scale)))
                found.append((row, k_at, rotate_back(dot(score_grad, q, (0, 0)))))
                found.append((row, v_at, value_grad))
            for row, at, value in found:
                d_qkv[row, :, :, at] = value.astype(BF16).reshape(2, 64, 128)
            return carry

        lax.fori_loop(0, 2, one, 0)

    merge_q = Merge(links, d_qkv, wq, set_b, merged_too)
    sums_u = Scatter(links, (wu, pl.ds(0, 512)), (wu, pl.ds(512, 512)), buffers[0:8])
    sums_d = Scatter(links, (grad_d, pl.ds(0, 512)), (grad_d, pl.ds(512, 512)), buffers[8:16])
    sums_q = Scatter(links, (grad_q, pl.ds(0, 384)), (grad_q, pl.ds(384, 384)), buffers[16:24])
    sums_o = Scatter(links, (wo, pl.ds(0, 128)), (wo, pl.ds(128, 128)), buffers[24:32])

    def output_rows():
        merge_f.arrive()

        def step(i, rows):
            kept = tokens[z, span(core * 4 + i, 16), :][:, 2:3]
            produced = merge_f.rows(rows).astype(BF16).astype(F32) * kept
            out_rows[rows, :] = (hidden[rows, :] + info[1, rows, :][:, 1:2] * produced).astype(BF16)

        in_blocks(4, step)
        here = block_out.at[own_64]
        pending["output"] = [keep(out_rows, here), links.go(out_rows, here, links.partner)]

    def back_one():
        merge_q.arrive()

        def step(i, rows):
            grad = merge_q.rows(rows)
            scaled, inverse = n_one[rows, :], info[0, rows, :][:, 0:1]
            small_sum[4] += fold(grad * scaled)
            small_sum[6] += fold(grad)
            n_two[rows, :] = n_two[rows, :] + norm_back(scaled, inverse, small[4:5, :], grad)

        in_blocks(4, step)
        for r in range(8):
            small[r : r + 1, :] = jnp.sum(small_sum[r], axis=0, keepdims=True)
        pending["small"] = [links.go(small, small_near, links.partner)]
        here = input_grad.at[own_64]
        pending["input"] = [keep(n_two, here), links.go(n_two, here, links.partner)]

    def small_to_x():
        wait("small")
        small[...] = small[...] + small_near[...]
        moves = [(small.at[:, span(ring(x, k), 512)], sx_in.at[k], links.xs[k]) for k in (1, 2, 3)]
        pending["small"] = [links.together(moves, sx_in.at[pl.ds(1, 3)])]

    def small_to_y():
        wait("small")
        sx_in[0] = small[:, span(x, 512)] + sx_in[1] + sx_in[2] + sx_in[3]
        moves = [(sx_in.at[0, :, span(ring(y, k), 128)], sy_in.at[k], links.ys[k]) for k in (1, 2, 3)]
        pending["small"] = [links.together(moves, sy_in.at[pl.ds(1, 3)])]

    def small_to_z():
        wait("small")
        sz_in[z] = sx_in[0, :, span(y, 128)] + sy_in[1] + sy_in[2] + sy_in[3]
        pending["small"] = to_all(sz_in.at[z], sz_in.at[pl.ds(0, 3)], links.zs)

    def small_done():
        wait("small")
        small_grad[...] = pltpu.roll(sz_in[0] + sz_in[1] + sz_in[2] + sz_in[3], 128 - 32 * z, 1)
        _, _, update = moment_step(
            router_w[...], small_grad[0:4, 0:32], router_m[...], router_v[...], DECAY_RATE
        )
        squares[8, 0:4, 0:32] = 0.5 * router_w[...] * router_w[...]
        squares[9, 0:4, 0:32] = 0.5 * update * update

    def owners_u():
        pending["own_u"] = to_group(
            pack_u.at[:, pl.ds(0, 3072)], lambda to: [(wu.at[x, y, span(to, 32), :], pack_u.at[:, span(z, 1024)])])

    def owners_d():
        pending["own_d"] = to_group(
            pack_d.at[:, pl.ds(0, 3072)], lambda to: [(grad_d.at[x, y, span(to, 32), :], pack_d.at[:, span(z, 1024)])])

    def owners_o():
        pending["own_o"] = to_group(
            pack_o.at[pl.ds(0, 6)],
            lambda to: [
                (wo.at[x, y, span(to, 32), pl.ds(128 * h, 128)], pack_o.at[2 * z + h]) for h in (0, 1)
            ]
        )

    def owners_q():
        pending["own_q"] = to_group(
            pack_q.at[pl.ds(0, 3)], lambda to: [(grad_q.at[x, y, span(to, 32), :], pack_q.at[z])])

    def moments_wide():
        for number, (name, first, second) in enumerate((("mom_u", up_m, up_v), ("mom_d", down_m, down_v))):
            sem = local_sems.at[local_used[0]]
            local_used[0] += 1
            for kind, ref in enumerate((first, second)):
                for c in range(4):
                    src = ref.at[:, pl.ds(1024 * c, 1024)]
                    dst = wide.at[pl.ds(256 * number + 128 * kind + 32 * c, 32)]
                    pltpu.make_async_copy(src, dst, sem).start()
            whole = wide.at[pl.ds(256 * number, 256)]
            pending[name] = [pltpu.make_async_copy(whole, whole, sem)]

    def squares_wide(number, weights, grads):
        def one(i, carry):
            rows, columns = span(lax.div(i, 4), 16), span(lax.rem(i, 4), 1024)
            weight = weights[rows, columns]
            at = lax.rem(i, 4) * 2 + lax.div(i, 4) + (number - 2) * 16
            _, _, update = moment_step(
                weight, grads[rows, columns].astype(F32), wide[span(at, 16), :], wide[span(at + 8, 16), :], DECAY_RATE
            )
            squares[2 * number] += fold_lanes(weight * weight)
            squares[2 * number + 1] += fold_lanes(update * update)
            return carry

        lax.fori_loop(0, 8, one, 0)

    def squares_u():
        wait("own_u")
        wait("mom_u")
        pending["results"].append(keep(pack_u, up_grad))
        squares_wide(2, own_u, pack_u)

    def squares_d():
        wait("own_d")
        wait("mom_d")
        pending["results"].append(keep(pack_d, down_grad))
        squares_wide(3, own_d, pack_d)

    def squares_o():
        wait("own_o")
        wait("mom_o")
        pending["results"].append(keep(pack_o, out_grad))

        def one(head, carry):
            weight = own_o[head]
            _, _, update = moment_step(
                weight, pack_o[head].astype(F32), mom_o[0, head], mom_o[1, head], DECAY_RATE
            )
            squares[2] += fold_lanes(weight * weight)
            squares[3] += fold_lanes(update * update)
            return carry

        lax.fori_loop(0, 8, one, 0)

    def squares_q():
        wait("own_q")
        wait("mom_q")
        for c in range(3):
            for head in range(8):
                at = 256 * c + 128 * (head % 2)
                qkv_grad[:, c, head, :] = pack_q[head // 2, :, at : at + 128].astype(F32)

        def one(i, carry):
            rows = pl.ds(i * 4, 4)
            weight = own_q[rows]
            _, _, update = moment_step(weight, qkv_grad[rows], mom_q[0, rows], mom_q[1, rows], DECAY_RATE)
            squares[0] += jnp.sum(jnp.sum(weight * weight, axis=0), axis=0)
            squares[1] += jnp.sum(jnp.sum(update * update, axis=0), axis=0)
            return carry

        lax.fori_loop(0, 8, one, 0)

    def totals():
        here = (4 * core + z, plane)
        sets = ((links.zs, links.others, {0: links.partner}), (links.xs, links.ys, links.across))
        tile = jnp.sum(squares[...], axis=1)
        for axis, count in enumerate((8, 16)):
            slots[axis, here[axis]] = tile
            for copy in to_all(slots.at[axis, here[axis]], slots.at[axis, pl.ds(0, count - 1)], *sets[axis]):
                copy.wait()
            tile = slots[axis, 0]
            for k in range(1, count):
                tile = tile + slots[axis, k]
        norms[...] = tile

    begin()
    slices_q()
    norm_one()
    pack_rest()
    slices_o()
    wait("q")
    ring_q.advance()
    small_x()
    slices_d()
    small_y()
    wait("o")
    ring_o.advance()
    rows_branch_start()
    ring_q.advance()
    wait("d")
    ring_d.advance()
    ring_o.advance()
    small_rows()
    rows_one_start()
    token_columns()
    ring_q.advance()
    rows_one.relay()
    slices_u()
    ring_o.advance()
    ring_q.advance()
    ring_d.advance()
    rows_one.finish()
    ring_o.advance()
    rows_branch.relay()
    wait("u")
    ring_u.advance()
    ring_d.advance()
    ring_q.advance()
    queries()
    attend(0)
    attend(2)
    ring_o.advance()
    merge_one.cross()
    ring_u.advance()
    merge_one.along()
    rows_branch.finish()
    ring_u.advance()
    merge_one.arrive()
    norm_two()
    rows_two_start()
    ring_d.advance()
    rows_two.relay()
    ring_u.advance()
    ring_d.advance()
    units_back()
    rows_two_finish()
    ring_u.advance()
    units()
    outer(branch, act_gated, grad_d)
    sums_d.advance()
    merge_u_out()
    merge_u.along()
    merge_f.cross()
    outer(a_two, up_low, wu)
    sums_u.advance()
    sums_d.advance()
    merge_f.along(leave=False)
    merge_u_in()
    back_two()
    rows_back.start()
    rows_back.relay()
    sums_u.advance()
    sums_d.advance()
    rows_back.finish()
    merge_f.leave()
    mixed_back()
    attend_back()
    sums_d.advance()
    outer(a_one, d_qkv, grad_q)
    sums_q.advance()
    merge_q.cross()
    merge_q.along()
    moments_wide()
    sums_u.advance()
    sums_d.advance()
    outer(hidden_low, mixed, wo)
    sums_o.advance()
    sums_q.advance()
    sums_u.advance()
    back_one()
    sums_o.advance()
    output_rows()
    small_to_x()
    sums_q.advance()
    sums_u.advance()
    owners_d()
    small_to_y()
    sums_o.advance()
    owners_u()
    sums_q.advance()
    small_to_z()
    sums_o.advance()
    sums_q.advance()
    owners_q()
    squares_u()
    small_done()
    sums_o.advance()
    owners_o()
    squares_d()
    squares_q()
    squares_o()
    totals()
    wait("output")
    wait("input")
    wait("results")


def layer(*operands):
    def vmem(*shape, kind=BF16):
        return pltpu.VMEM(shape, kind)

    def merge_buffers():
        return [vmem(TILES, 4, 64, TILE), vmem(TILES, 4, 64, TILE), vmem(3, TILES, 64, TILE)]

    def sum_buffers(width):
        return [
            vmem(2, 4, 64, width), vmem(2, 4, 128, width), vmem(2, 64, width), vmem(2, 128, width),
        ] * 2

    rows, rows_low, tokens = vmem(64, 2048, kind=F32), vmem(64, 2048), vmem(4, 2, 64, 2048)
    tile = vmem(4, 8, 128, kind=F32)
    return pl.pallas_call(
        layer_kernel,
        out_shape=(
            jax.ShapeDtypeStruct((128, 2048), BF16),
            jax.ShapeDtypeStruct((128, 2048), F32),
            jax.ShapeDtypeStruct((32, 3, 8, 128), F32),
            jax.ShapeDtypeStruct((8, 32, 128), BF16),
            jax.ShapeDtypeStruct((32, 4096), BF16),
            jax.ShapeDtypeStruct((32, 4096), BF16),
            jax.ShapeDtypeStruct((8, 128), F32),
            jax.ShapeDtypeStruct((16, 128), F32),
        ),
        in_specs=[ANY] * 14 + [VMEM] * 7 + [pl.BlockSpec(memory_space=pltpu.SMEM)] + [VMEM] * 3,
        out_specs=(ANY, ANY, VMEM, ANY, ANY, ANY, VMEM, VMEM),
        scratch_shapes=[
            vmem(32, 3, 8, 128, kind=F32), vmem(8, 32, 128, kind=F32), vmem(32, 4096, kind=F32),
            vmem(32, 4096, kind=F32),
            vmem(4, 32, 768), vmem(8, 32, 128), vmem(32, 4096), vmem(32, 4096),
            vmem(2, 32, 3, 8, 128, kind=F32), vmem(2, 8, 32, 128, kind=F32),
            vmem(4, 4, 128, 768), vmem(4, 4, 128, 256), vmem(4, 4, 128, 1024), vmem(4, 4, 128, 1024),
            vmem(4, 4, 128, 768), vmem(4, 4, 128, 1024),
            tile, vmem(4, 4, 8, 128, kind=F32), vmem(8, 2048, kind=F32), vmem(8, 2048, kind=F32),
            tile, vmem(4, 128, 128, kind=F32), vmem(4, 2, 8, 128, kind=F32), vmem(4, 128, 128, kind=F32),
            vmem(3, 128, 128, kind=F32),
            tokens, tokens, tokens, tokens,
            rows_low, rows_low, rows, rows, rows, rows, rows, rows_low,
            vmem(512, 1024, kind=F32), vmem(512, 768), vmem(8, 128, 128, kind=F32),
            vmem(4, 2, 64, 256), vmem(512, 256), vmem(4, 2, 64, 768), vmem(4, 2, 64, 1024), vmem(4, 2, 64, 1024), vmem(4, 2, 64, 1024),
            *merge_buffers(), *merge_buffers(),
            vmem(8, 512, kind=F32), vmem(8, 512, kind=F32), tile,
            vmem(8, 8, 2048, kind=F32), vmem(4, 8, 512, kind=F32), tile, tile,
            vmem(16, 8, 128, kind=F32), vmem(2, 16, 16, 128, kind=F32),
            *sum_buffers(512), *sum_buffers(512), *sum_buffers(384), *sum_buffers(128),
            DMA((LOCAL_COPIES,)), DMA((LINK_COPIES,)), DMA((LINK_COPIES,)),
        ],
        compiler_params=pltpu.CompilerParams(
            collective_id=0, has_side_effects=True, vmem_limit_bytes=63 * 2**20
        ),
        name="layer",
    )(*operands)


def renew_kernel(norms, small_grad, gains, biases, norm_m, norm_v, *refs):
    ins, outs = refs[:22], refs[22:]
    outs[31][...] = ins[20][...]
    outs[32][...] = ins[21][...]
    sums = jnp.sqrt(jnp.sum(norms[...], axis=1, keepdims=True))
    for index in range(5):
        weight, grad, m, v = (ref[...] for ref in ins[4 * index : 4 * index + 4])
        grad = grad[0:4, 0:32] if index == 4 else grad.astype(F32)
        first, second, update = moment_step(weight, grad, m, v, DECAY_RATE)
        ratio = LEARN_RATE * (sums[2 * index : 2 * index + 1, :] / sums[2 * index + 1 : 2 * index + 2, :])
        ratio = ratio.reshape((1,) * weight.ndim)
        new = weight - ratio * update
        for ref, value in zip(outs[5 * index : 5 * index + 5], (grad, first, second, new, new.astype(BF16))):
            ref[...] = value
    grad = small_grad[4:8, 0:32]
    master = jnp.concatenate([gains[...], biases[...]], axis=0)
    first, second, update = moment_step(master, grad, norm_m[...], norm_v[...], 0.0)
    new = master - NORM_RATE * update
    for ref, value in zip(outs[25:30], (grad, first, second, new, new.astype(BF16))):
        ref[...] = value
    row = lax.broadcasted_iota(jnp.int32, (8, 128), 0)
    lane = lax.broadcasted_iota(jnp.int32, (8, 128), 1)
    tile = jnp.zeros((8, 128), F32)
    for index in range(10):
        here = (row == index % 2) & (lane == index // 2)
        tile = jnp.where(here, sums[index : index + 1, :], tile)
    outs[30][...] = tile[0:2, 0:5]


def renew(norms, small_grad, gains, biases, norm_m, norm_v, *matrices):
    steps = 2

    def whole(shape):
        return pl.BlockSpec(shape, lambda i: (0,) * len(shape))

    blocks = (
        pl.BlockSpec((32 // steps, 3, 8, 128), lambda i: (i, 0, 0, 0)),
        pl.BlockSpec((8 // steps, 32, 128), lambda i: (i, 0, 0)),
        pl.BlockSpec((32, 4096 // steps), lambda i: (0, i)),
        pl.BlockSpec((32, 4096 // steps), lambda i: (0, i)),
        whole((4, 32)),
    )
    shapes = ((32, 3, 8, 128), (8, 32, 128), (32, 4096), (32, 4096), (4, 32), (4, 32))
    in_specs = [whole((16, 128)), whole((8, 128)), whole((2, 32)), whole((2, 32)), whole((4, 32)), whole((4, 32))]
    out_specs, out_shape = [], []
    for index, block in enumerate(blocks):
        in_specs += [block, whole((8, 128)) if index == 4 else block, block, block]
    for block, shape in zip((*blocks, whole((4, 32))), shapes):
        out_specs += [block] * 5
        out_shape += [jax.ShapeDtypeStruct(shape, kind) for kind in (F32, F32, F32, F32, BF16)]
    out_specs.append(whole((2, 5)))
    out_shape.append(jax.ShapeDtypeStruct((2, 5), F32))
    rows = pl.BlockSpec((128 // steps, 2048), lambda i: (i, 0))
    in_specs += [rows, rows]
    out_specs += [rows, rows]
    out_shape += [jax.ShapeDtypeStruct((128, 2048), kind) for kind in (BF16, F32)]
    return pl.pallas_call(
        renew_kernel,
        grid=(steps,),
        in_specs=in_specs,
        out_specs=out_specs,
        out_shape=out_shape,
        compiler_params=pltpu.CompilerParams(vmem_limit_bytes=63 * 2**20),
        name="renew",
    )(norms, small_grad, gains, biases, norm_m, norm_v, *matrices)


def rotary_tables(length, size):
    half_size = size // 2
    frequency = ROPE_BASE ** (-(np.arange(half_size) * 2.0 / size))
    angles = np.arange(length)[:, None] * frequency[None, :]
    cosine_table = np.concatenate([np.cos(angles), np.cos(angles)], axis=-1)
    sine_table = np.concatenate([np.sin(angles), np.sin(angles)], axis=-1)
    return (cosine_table.astype(np.float32), sine_table.astype(np.float32))


def local(
    block_input,
    cotangent,
    head_count,
    width_route,
    forced_width,
    slot_index,
    qkv_weight,
    out_weight,
    up_weight,
    down_weight,
    router_weight,
    norm_gains,
    norm_biases,
    qkv_first,
    qkv_second,
    out_first,
    out_second,
    up_first,
    up_second,
    down_first,
    down_second,
    router_first,
    router_second,
    norm_first,
    norm_second,
):
    def turned(value):
        return value.transpose(0, 2, 1)

    out = turned(out_weight), turned(out_first), turned(out_second)
    down = down_weight.T, down_first.T, down_second.T
    router = router_weight.T, router_first.T, router_second.T
    block_output, input_grad, *grads, small_grad, norms = layer(
        qkv_weight, out[0], up_weight, down[0],
        qkv_first, qkv_second, *out[1:], up_first, up_second, *down[1:],
        block_input, cotangent, *router, norm_gains, norm_biases,
        head_count.reshape(1, -1), width_route.reshape(1, -1), forced_width, slot_index.reshape(1, -1),
        *rotary_tables(128, 128),
    )
    *results, lamb_norms, block_output, input_grad = renew(
        norms, small_grad, norm_gains, norm_biases, norm_first, norm_second,
        qkv_weight, grads[0], qkv_first, qkv_second,
        out[0], grads[1], *out[1:],
        up_weight, grads[2], up_first, up_second,
        down[0], grads[3], *down[1:],
        router[0], small_grad, *router[1:],
        block_output, input_grad,
    )
    kinds = []
    for kind in range(5):
        qkv, out, up, down, router, norm = (results[5 * index + kind] for index in range(6))
        kinds += [qkv, turned(out), up, down.T, router.T, norm]
    return (block_output, input_grad, *kinds, lamb_norms.T)


def solution(mesh):
    qkv, out = P("dp", None, "mp", None), P("mp", None, "dp")
    up, down, router, norms = P("dp", "mp"), P("mp", "dp"), P("dp", None), P(None, "dp")
    rows, tokens = P("dp", None), P("dp")
    matrices = (qkv, out, up, down, router)
    return jax.shard_map(
        local,
        mesh=mesh,
        in_specs=(
            rows, rows, tokens, tokens, tokens, tokens,
            *matrices, norms, norms,
            qkv, qkv, out, out, up, up, down, down, router, router, norms, norms,
        ),
        out_specs=(rows, rows, *((*matrices, norms) * 5), P()),
        check_vma=False,
    )
```
